32 devices in a mesh: dp: 8 (over y, x, core), tensor: 4 (over z).
Axes of the slice: x: 2, y: 2, z: 4, core: 2. Of those that a mesh axis runs over, the one named last changes fastest.
Arguments:
- tokens: bfloat16 [64, 261, 768], P('dp'), may hold values from -6 to 6
- patch_mask: int32 [64, 256], P('dp'), may hold values from 0 to 1, as said below
- cotangent: bfloat16 [64, 261, 768], P('dp'), may hold values from -6 to 6
- qkv_weight: float32 [3, 768, 768], P(None, 'dp', 'tensor'), may hold values from -0.21875 to 0.21875
- qkv_first: float32 [3, 768, 768], P(None, 'dp', 'tensor'), may hold values from -0.005859375 to 0.005859375
- qkv_second: float32 [3, 768, 768], P(None, 'dp', 'tensor'), may hold values from 1.410555e-07 to 5.64222e-07
- proj_weight: float32 [768, 768], P('tensor', 'dp'), may hold values from -0.625 to 0.625
- proj_first: float32 [768, 768], P('tensor', 'dp'), may hold values from -0.005859375 to 0.005859375
- proj_second: float32 [768, 768], P('tensor', 'dp'), may hold values from 1.410555e-07 to 5.64222e-07
- fc1_weight: float32 [768, 3072], P('dp', 'tensor'), may hold values from -0.21875 to 0.21875
- fc1_first: float32 [768, 3072], P('dp', 'tensor'), may hold values from -0.005859375 to 0.005859375
- fc1_second: float32 [768, 3072], P('dp', 'tensor'), may hold values from 1.410555e-07 to 5.64222e-07
- fc2_weight: float32 [3072, 768], P('tensor', 'dp'), may hold values from -0.109375 to 0.109375
- fc2_first: float32 [3072, 768], P('tensor', 'dp'), may hold values from -0.005859375 to 0.005859375
- fc2_second: float32 [3072, 768], P('tensor', 'dp'), may hold values from 1.410555e-07 to 5.64222e-07
- vectors: float32 [9, 768], replicated, may hold values from -3 to 4, as said below
- vectors_first: float32 [9, 768], replicated, may hold values from -0.005859375 to 0.005859375
- vectors_second: float32 [9, 768], replicated, may hold values from 1.410555e-07 to 5.64222e-07
- head_bias: float32 [2, 768], P(None, 'tensor'), may hold values from -1 to 2
- head_bias_first: float32 [2, 768], P(None, 'tensor'), may hold values from -0.0234375 to 0.0234375
- head_bias_second: float32 [2, 768], P(None, 'tensor'), may hold values from 2.256888e-06 to 9.027552e-06
- fc1_bias: float32 [3072], P('tensor'), may hold values from -2 to 2
- fc1_bias_first: float32 [3072], P('tensor'), may hold values from -0.001953125 to 0.001953125
- fc1_bias_second: float32 [3072], P('tensor'), may hold values from 2.8211101e-08 to 1.12844404e-07
Outputs:
- block_out: bfloat16 [64, 261, 768], P('dp')
- tokens_grad: bfloat16 [64, 261, 768], P('dp')
- grad_norm: float32 [], replicated
- qkv_new: float32 [3, 768, 768], P(None, 'dp', 'tensor')
- qkv_first_new: float32 [3, 768, 768], P(None, 'dp', 'tensor')
- qkv_second_new: float32 [3, 768, 768], P(None, 'dp', 'tensor')
- proj_new: float32 [768, 768], P('tensor', 'dp')
- proj_first_new: float32 [768, 768], P('tensor', 'dp')
- proj_second_new: float32 [768, 768], P('tensor', 'dp')
- fc1_new: float32 [768, 3072], P('dp', 'tensor')
- fc1_first_new: float32 [768, 3072], P('dp', 'tensor')
- fc1_second_new: float32 [768, 3072], P('dp', 'tensor')
- fc2_new: float32 [3072, 768], P('tensor', 'dp')
- fc2_first_new: float32 [3072, 768], P('tensor', 'dp')
- fc2_second_new: float32 [3072, 768], P('tensor', 'dp')
- vectors_new: float32 [9, 768], replicated
- vectors_first_new: float32 [9, 768], replicated
- vectors_second_new: float32 [9, 768], replicated
- head_bias_new: float32 [2, 768], P(None, 'tensor')
- head_bias_first_new: float32 [2, 768], P(None, 'tensor')
- head_bias_second_new: float32 [2, 768], P(None, 'tensor')
- fc1_bias_new: float32 [3072], P('tensor')
- fc1_bias_first_new: float32 [3072], P('tensor')
- fc1_bias_second_new: float32 [3072], P('tensor')
- qkv_copy: bfloat16 [3, 768, 768], P(None, 'dp', 'tensor')
- proj_copy: bfloat16 [768, 768], P('tensor', 'dp')
- fc1_copy: bfloat16 [768, 3072], P('dp', 'tensor')
- fc2_copy: bfloat16 [3072, 768], P('tensor', 'dp')
The draws below stay inside these ranges and needn't reach their ends.
Inputs may be any that keep to these rules, and one draw needn't show every extreme that they name: `patch_mask`: per crop, 1 exactly on the patches (row-major on the 16 x 16 grid) covered by four rectangles, each 2 to 8 patches on a side. `vectors`: rows 0, 2, 4, 6 are positive.
All inputs are finite; a program needn't handle non-finite values.
Results may differ from the reference program's by a relative error of at most 0.02.
Values may be sent and summed in bfloat16 or wider, within the bound.
A program may use at most 192 MiB of HBM per device.

```python
import math
import jax
import jax.numpy as jnp
from jax import lax

D = 768
HEADS = 12
HD = 64
FF = 3072
REG = 4
PGRID = 16
CROPS_DEV = 8
STEP = 10
SEQ = 261
CROPS = 64
NPARAMS = 7089408
N_DP = 8
N_TENSOR = 4


def rising_profile(length):
    return jnp.arange(length, dtype=jnp.float32) / max(length - 1, 1)


def clipped_normal(key, shape):
    return jnp.clip(jax.random.normal(key, shape, jnp.float32), -3.0, 3.0)


def draw_vectors(key, part):
    key = jax.random.fold_in(key, 11)
    subkeys = jax.random.split(key, 3)
    position = rising_profile(D)
    jitter = jax.random.uniform(subkeys[0], (4, D), jnp.float32, 0.8, 1.2)
    factor = 3.0
    shifts = 0.3 * clipped_normal(subkeys[1], (4, D))
    token_row = clipped_normal(subkeys[2], (D,))
    gain_rows = 0.6 * jnp.power(factor, position) * jitter
    stacked = jnp.stack([gain_rows[0], shifts[0], gain_rows[1], shifts[1], gain_rows[2], shifts[2], gain_rows[3], shifts[3], token_row])
    return stacked.astype(jnp.float32)


def draw_head_bias(key, part):
    key = jax.random.fold_in(key, 23)
    subkeys = jax.random.split(key, 2)
    position = rising_profile(HEADS * HD)
    query_row = 0.3 * clipped_normal(subkeys[0], (HEADS * HD,))
    value_row = 0.3 * clipped_normal(subkeys[1], (HEADS * HD,)) + position
    return jnp.stack([query_row, value_row]).astype(jnp.float32)


def draw_fc1_bias(key, part):
    key = jax.random.fold_in(key, 37)
    position = rising_profile(FF)
    noise = 0.3 * clipped_normal(key, (FF,))
    return (noise - 0.5 + 1.5 * position).astype(jnp.float32)


def draw_patch_mask(key, part):
    key = jax.random.fold_in(key, 41)
    subkeys = jax.random.split(key, 4)
    shape_pair = (CROPS, 4)
    height = jax.random.randint(subkeys[0], shape_pair, 2, PGRID // 2 + 1)
    breadth = jax.random.randint(subkeys[1], shape_pair, 2, PGRID // 2 + 1)
    top_row = jax.random.randint(subkeys[2], shape_pair, 0, PGRID - height + 1)
    left_col = jax.random.randint(subkeys[3], shape_pair, 0, PGRID - breadth + 1)
    lines = jnp.arange(PGRID, dtype=jnp.int32)
    inside_rows = (lines >= top_row[:, :, None]) & (lines < (top_row + height)[:, :, None])
    inside_cols = (lines >= left_col[:, :, None]) & (lines < (left_col + breadth)[:, :, None])
    covered = jnp.any(inside_rows[:, :, :, None] & inside_cols[:, :, None, :], axis=1)
    return covered.reshape(CROPS, PGRID * PGRID).astype(jnp.int32)


def strengthened(array, stream_key, source, target, shards_of, factor):
    owner, partner = [(jnp.arange(array.shape[axis_at]) // (array.shape[axis_at] // shards_of)).reshape([-1 if axis == axis_at else 1 for axis in range(array.ndim)]) for axis_at in (source, target)]
    chosen = jax.random.permutation(stream_key, shards_of)[partner]
    strong = (owner == chosen) | (owner == (partner + shards_of // 2) % shards_of)
    return jnp.where(strong, factor * array, array)


def block_scale(stream_key, extent, cuts, least, top_value):
    gain, own = 1.0, jax.random.fold_in(stream_key, 6)
    for axis_at, shards_of in cuts:
        heights = jnp.exp(jax.random.uniform(jax.random.fold_in(own, axis_at), (shards_of,), jnp.float32, least / len(cuts), top_value / len(cuts)))
        gain = gain * jnp.repeat(heights, extent[axis_at] // shards_of).reshape([-1 if axis == axis_at else 1 for axis in range(len(extent))])
    return gain


def bell_draw(stream_key, dims, deviation, bound, cuts=(), kind=jnp.bfloat16):
    result = jax.random.normal(stream_key, dims, jnp.float32) * deviation
    if len(cuts) > 0:
        result = block_scale(stream_key, dims, cuts, -0.22, 0.18) * result
    return jnp.clip(result, min=-bound, max=bound).astype(kind)


def gaussian_with(own_key, extent, width, most, cuts, heavy, kind=jnp.bfloat16):
    drawn = width * jax.random.normal(own_key, extent, jnp.float32)
    if cuts:
        drawn = drawn * block_scale(own_key, extent, cuts, -0.22, 0.18)
    return jnp.clip(strengthened(drawn, jax.random.fold_in(own_key, 3), *heavy), -most, most).astype(kind)


def setup_inputs(seed: int = 0) -> dict:
    arg_keys = jax.random.split(jax.random.key(seed), 25)
    return {
        "tokens": gaussian_with(arg_keys[0], (CROPS, SEQ, D), 1.0, 6.0, ((0, 8),), (0, 2, 8, 2.0)),
        "patch_mask": draw_patch_mask(jax.random.fold_in(arg_keys[24], 71), 0),
        "cotangent": gaussian_with(arg_keys[2], (CROPS, SEQ, D), 1.0, 6.0, ((0, 8),), (0, 2, 8, 2.0)),
        "qkv_weight": bell_draw(arg_keys[3], (3, D, HEADS * HD), D ** -0.5, 0.21875, ((1, 8), (2, 4)), jnp.float32),
        "qkv_first": bell_draw(arg_keys[4], (3, D, HEADS * HD), (NPARAMS ** -0.5), 0.005859375, ((1, 8), (2, 4)), jnp.float32),
        "qkv_second": jnp.clip(jnp.exp(math.log(5.642219775836566e-07) - 1.3862944 * jax.random.uniform(arg_keys[5], (3, D, HEADS * HD), jnp.float32) ** block_scale(arg_keys[5], (3, D, HEADS * HD), ((1, 8), (2, 4)), -0.2, 0.2)), 1.4105549439591414e-07, 5.642219775836566e-07),
        "proj_weight": bell_draw(arg_keys[6], (HEADS * HD, D), (HEADS * HD // 8) ** -0.5, 0.625, ((0, 4), (1, 8)), jnp.float32),
        "proj_first": bell_draw(arg_keys[7], (HEADS * HD, D), (NPARAMS ** -0.5), 0.005859375, ((0, 4), (1, 8)), jnp.float32),
        "proj_second": jnp.clip(jnp.exp(math.log(5.642219775836566e-07) - 1.3862944 * jax.random.uniform(arg_keys[8], (HEADS * HD, D), jnp.float32) ** block_scale(arg_keys[8], (HEADS * HD, D), ((0, 4), (1, 8)), -0.2, 0.2)), 1.4105549439591414e-07, 5.642219775836566e-07),
        "fc1_weight": bell_draw(arg_keys[9], (D, FF), D ** -0.5, 0.21875, ((0, 8), (1, 4)), jnp.float32),
        "fc1_first": bell_draw(arg_keys[10], (D, FF), (NPARAMS ** -0.5), 0.005859375, ((0, 8), (1, 4)), jnp.float32),
        "fc1_second": jnp.clip(jnp.exp(math.log(5.642219775836566e-07) - 1.3862944 * jax.random.uniform(arg_keys[11], (D, FF), jnp.float32) ** block_scale(arg_keys[11], (D, FF), ((0, 8), (1, 4)), -0.2, 0.2)), 1.4105549439591414e-07, 5.642219775836566e-07),
        "fc2_weight": bell_draw(arg_keys[12], (FF, D), FF ** -0.5, 0.109375, ((0, 4), (1, 8)), jnp.float32),
        "fc2_first": bell_draw(arg_keys[13], (FF, D), (NPARAMS ** -0.5), 0.005859375, ((0, 4), (1, 8)), jnp.float32),
        "fc2_second": jnp.clip(jnp.exp(math.log(5.642219775836566e-07) - 1.3862944 * jax.random.uniform(arg_keys[14], (FF, D), jnp.float32) ** block_scale(arg_keys[14], (FF, D), ((0, 4), (1, 8)), -0.2, 0.2)), 1.4105549439591414e-07, 5.642219775836566e-07),
        "vectors": draw_vectors(jax.random.fold_in(arg_keys[24], 71), 0),
        "vectors_first": bell_draw(arg_keys[16], (9, D), (NPARAMS ** -0.5), 0.005859375, (), jnp.float32),
        "vectors_second": jnp.clip(jnp.exp(jax.random.uniform(arg_keys[17], (9, D), jnp.float32, math.log(1.4105549439591414e-07), math.log(5.642219775836566e-07))), 1.4105549439591414e-07, 5.642219775836566e-07),
        "head_bias": draw_head_bias(jax.random.fold_in(arg_keys[24], 71), 0),
        "head_bias_first": bell_draw(arg_keys[19], (2, HEADS * HD), (4 * NPARAMS ** -0.5), 0.0234375, ((1, 4),), jnp.float32),
        "head_bias_second": jnp.clip(jnp.exp(math.log(9.027551641338505e-06) - 1.3862944 * jax.random.uniform(arg_keys[20], (2, HEADS * HD), jnp.float32) ** block_scale(arg_keys[20], (2, HEADS * HD), ((1, 4),), -0.2, 0.2)), 2.2568879103346262e-06, 9.027551641338505e-06),
        "fc1_bias": draw_fc1_bias(jax.random.fold_in(arg_keys[24], 71), 0),
        "fc1_bias_first": bell_draw(arg_keys[22], (FF,), (0.4 * NPARAMS ** -0.5), 0.001953125, ((0, 4),), jnp.float32),
        "fc1_bias_second": jnp.clip(jnp.exp(math.log(1.1284440404324414e-07) - 1.3862944 * jax.random.uniform(arg_keys[23], (FF,), jnp.float32) ** block_scale(arg_keys[23], (FF,), ((0, 4),), -0.2, 0.2)), 2.8211101010811035e-08, 1.1284440404324414e-07),
    }


@jax.custom_vjp
def low(v):
    return lax.optimization_barrier(v.astype(jnp.bfloat16)).astype(jnp.float32)

@jax.custom_vjp
def low_back(v):
    return v

def low_keep(v):
    return (low(v), None)

def low_pass(kept, grad):
    return (grad,)

def back_keep(v):
    return (v, None)

def back_low(kept, grad):
    return (low(grad),)
low.defvjp(low_keep, low_pass)
low_back.defvjp(back_keep, back_low)
highest = lax.Precision.HIGHEST
norm_eps = 1e-06
clip_norm = 1.0
rate_matrix = 0.04
rate_vector = 0.2
decay_matrix = 0.04
moment_decay = 0.5
adam_eps = 1e-08

def matmul(first_op, second_op):
    return jnp.dot(first_op, second_op, precision=highest)

def layer_norm(values, gain_row, shift_row):
    middle_val = lax.optimization_barrier(jnp.mean(values, axis=-1, keepdims=True))
    centred = values - middle_val
    spread = lax.optimization_barrier(jnp.mean(centred * centred, axis=-1, keepdims=True))
    return centred * lax.rsqrt(spread + norm_eps) * gain_row + shift_row

def block(params, inputs, masked):
    qkv_weight, proj_weight, fc1_weight, fc2_weight, vectors, head_bias, fc1_bias = params
    crops = inputs.shape[0]
    seq_len = inputs.shape[1]
    chosen = jnp.concatenate([jnp.zeros((crops, 1 + REG), jnp.bool_), masked == 1], axis=1)
    start = jnp.where(chosen[:, :, None], vectors[8], inputs)
    norm_one = low(layer_norm(start, vectors[0], vectors[1]))
    qkv_low = low(qkv_weight)
    proj_low = low(proj_weight)
    up_low = low(fc1_weight)
    down_low = low(fc2_weight)
    head_cols = HEADS * HD // N_TENSOR
    heads_here = HEADS // N_TENSOR
    ff_cols = FF // N_TENSOR
    scale = HD ** (-0.5)
    attn_total = jnp.zeros(start.shape, jnp.float32)
    for shard in range(N_TENSOR):
        begin = shard * head_cols
        finish = begin + head_cols
        shard_in = low_back(norm_one)
        query = low(low_back(matmul(shard_in, qkv_low[0, :, begin:finish]) + head_bias[0, begin:finish]))
        keys_part = low(low_back(matmul(shard_in, qkv_low[1, :, begin:finish])))
        values_part = low(low_back(matmul(shard_in, qkv_low[2, :, begin:finish]) + head_bias[1, begin:finish]))
        query = query.reshape(crops, seq_len, heads_here, HD)
        keys_part = keys_part.reshape(crops, seq_len, heads_here, HD)
        values_part = values_part.reshape(crops, seq_len, heads_here, HD)
        scores = low_back(jnp.einsum('bqhe,bkhe->bhqk', query, keys_part, precision=highest) * scale)
        probs = low(jax.nn.softmax(scores, axis=-1))
        context = jnp.einsum('bhqk,bkhe->bqhe', probs, values_part, precision=highest)
        context = low(low_back(context)).reshape(crops, seq_len, head_cols)
        attn_total = attn_total + low(low_back(matmul(context, proj_low[begin:finish, :])))
    attn = attn_total + vectors[3]
    middle = start + vectors[2] * attn
    norm_two = low(layer_norm(middle, vectors[4], vectors[5]))
    mlp_total = jnp.zeros(start.shape, jnp.float32)
    for shard in range(N_TENSOR):
        begin = shard * ff_cols
        finish = begin + ff_cols
        shard_in = low_back(norm_two)
        hidden = low_back(matmul(shard_in, up_low[:, begin:finish]) + fc1_bias[begin:finish])
        active = low(jax.nn.gelu(hidden, approximate=False))
        mlp_total = mlp_total + low(low_back(matmul(active, down_low[begin:finish, :])))
    mlp = mlp_total + vectors[7]
    return middle + vectors[6] * mlp

def adam_step(weight, first, second, grad, rate, decay):
    first_new = moment_decay * first + (1.0 - moment_decay) * grad
    second_new = moment_decay * second + (1.0 - moment_decay) * grad * grad
    correct = 1.0 - moment_decay ** STEP
    weight_new = weight - rate * (first_new / correct / (jnp.sqrt(second_new / correct) + adam_eps) + decay * weight)
    return (weight_new, first_new, second_new)

def reference(tokens, patch_mask, cotangent, qkv_weight, qkv_first, qkv_second, proj_weight, proj_first, proj_second, fc1_weight, fc1_first, fc1_second, fc2_weight, fc2_first, fc2_second, vectors, vectors_first, vectors_second, head_bias, head_bias_first, head_bias_second, fc1_bias, fc1_bias_first, fc1_bias_second):
    params = (qkv_weight, proj_weight, fc1_weight, fc2_weight, vectors, head_bias, fc1_bias)
    tok_groups = tokens.reshape(N_DP, CROPS_DEV, SEQ, D)
    mask_groups = patch_mask.reshape(N_DP, CROPS_DEV, PGRID * PGRID)
    cot_groups = cotangent.reshape(N_DP, CROPS_DEV, SEQ, D)

    def one_group(totals, group):
        tok_group, mask_group, cot_group = group

        def forward(param_set, inputs):
            return block(param_set, inputs, mask_group)
        outputs, pullback = jax.vjp(forward, params, tok_group.astype(jnp.float32))
        param_grads, input_grad = pullback(cot_group.astype(jnp.float32))
        totals = jax.tree.map(lambda running, addend: running + addend, totals, param_grads)
        return (totals, (outputs.astype(jnp.bfloat16), input_grad.astype(jnp.bfloat16)))
    zero_grads = jax.tree.map(jnp.zeros_like, params)
    totals, (out_groups, grad_groups) = lax.scan(one_group, zero_grads, (tok_groups, mask_groups, cot_groups))
    block_out = out_groups.reshape(CROPS, SEQ, D)
    tokens_grad = grad_groups.reshape(CROPS, SEQ, D)
    squares = jnp.zeros((), jnp.float32)
    for grad in totals:
        squares = squares + jnp.sum(grad * grad)
    grad_norm = jnp.sqrt(squares)
    factor = jnp.minimum(1.0, clip_norm / (grad_norm + 1e-06))
    qkv_grad, proj_grad, fc1_grad, fc2_grad, vectors_grad, head_bias_grad, fc1_bias_grad = totals
    qkv_set = adam_step(qkv_weight, qkv_first, qkv_second, factor * qkv_grad, rate_matrix, decay_matrix)
    proj_set = adam_step(proj_weight, proj_first, proj_second, factor * proj_grad, rate_matrix, decay_matrix)
    fc1_set = adam_step(fc1_weight, fc1_first, fc1_second, factor * fc1_grad, rate_matrix, decay_matrix)
    fc2_set = adam_step(fc2_weight, fc2_first, fc2_second, factor * fc2_grad, rate_matrix, decay_matrix)
    vectors_set = adam_step(vectors, vectors_first, vectors_second, factor * vectors_grad, rate_vector, 0.0)
    head_set = adam_step(head_bias, head_bias_first, head_bias_second, factor * head_bias_grad, rate_vector, 0.0)
    fc1b_set = adam_step(fc1_bias, fc1_bias_first, fc1_bias_second, factor * fc1_bias_grad, rate_vector, 0.0)
    return (block_out, tokens_grad, grad_norm, qkv_set[0], qkv_set[1], qkv_set[2], proj_set[0], proj_set[1], proj_set[2], fc1_set[0], fc1_set[1], fc1_set[2], fc2_set[0], fc2_set[1], fc2_set[2], vectors_set[0], vectors_set[1], vectors_set[2], head_set[0], head_set[1], head_set[2], fc1b_set[0], fc1b_set[1], fc1b_set[2], qkv_set[0].astype(jnp.bfloat16), proj_set[0].astype(jnp.bfloat16), fc1_set[0].astype(jnp.bfloat16), fc2_set[0].astype(jnp.bfloat16))
```

```python
import jax
import jax.numpy as jnp
from jax import lax
from jax.sharding import PartitionSpec as P

HD = 64
REG = 4
STEP = 10


norm_eps = 1e-06
clip_norm = 1.0
rate_matrix = 0.04
rate_vector = 0.2
decay_matrix = 0.04
moment_decay = 0.5
adam_eps = 1e-08


def layer_norm(values, gain_row, shift_row):
    middle_val = jnp.mean(values, axis=-1, keepdims=True)
    centred = values - middle_val
    spread = jnp.mean(centred * centred, axis=-1, keepdims=True)
    return centred * lax.rsqrt(spread + norm_eps) * gain_row + shift_row


def gelu_exact(values):
    return jax.nn.gelu(values, approximate=False)


def inner_rows(first_op, second_op):
    return lax.dot_general(
        first_op, second_op, (((0,), (0,)), ((), ())), preferred_element_type=jnp.float32
    )


def outer_cols(first_op, second_op):
    return lax.dot_general(
        first_op, second_op, (((1,), (1,)), ((), ())), preferred_element_type=jnp.float32
    )


def square_sum(values):
    return jnp.sum(values * values)


def adam_step(weight, first, second, grad, rate, decay):
    first_new = moment_decay * first + (1.0 - moment_decay) * grad
    second_new = moment_decay * second + (1.0 - moment_decay) * grad * grad
    correct = 1.0 - moment_decay**STEP
    weight_new = weight - rate * (
        first_new / correct / (jnp.sqrt(second_new / correct) + adam_eps) + decay * weight
    )
    return (weight_new, first_new, second_new)


def per_device(
    tokens,
    patch_mask,
    cotangent,
    qkv_weight,
    qkv_first,
    qkv_second,
    proj_weight,
    proj_first,
    proj_second,
    fc1_weight,
    fc1_first,
    fc1_second,
    fc2_weight,
    fc2_first,
    fc2_second,
    vectors,
    vectors_first,
    vectors_second,
    head_bias,
    head_bias_first,
    head_bias_second,
    fc1_bias,
    fc1_bias_first,
    fc1_bias_second,
):
    all_crops, seq_len, width = tokens.shape
    n_dp = lax.axis_size("dp")
    n_tensor = lax.axis_size("tensor")
    crops = all_crops // n_tensor
    first_crop = lax.axis_index("tensor") * crops
    rows_here = crops * seq_len
    scale = HD ** (-0.5)
    both = ("dp", "tensor")

    def gather(shard, dp_axis, tensor_axis):
        low_shard = shard.astype(jnp.bfloat16)
        part = lax.all_gather(low_shard, both, axis=0, tiled=False)
        part = part.reshape((n_dp, n_tensor) + shard.shape)
        part = jnp.moveaxis(part, 0, dp_axis + 1)
        part = jnp.moveaxis(part, 0, tensor_axis + (1 if tensor_axis > dp_axis else 0))
        shape = list(shard.shape)
        shape[dp_axis] *= n_dp
        shape[tensor_axis] *= n_tensor
        return part.reshape(shape)

    def scatter(full, dp_axis, tensor_axis):
        shape = list(full.shape)
        low = full.astype(jnp.bfloat16)
        pieces = []
        for at, extent in enumerate(shape):
            if at == dp_axis:
                pieces += [n_dp, extent // n_dp]
            elif at == tensor_axis:
                pieces += [n_tensor, extent // n_tensor]
            else:
                pieces += [extent]
        split = low.reshape(pieces)
        later = max(dp_axis, tensor_axis)
        earlier = min(dp_axis, tensor_axis)
        place = {earlier: earlier, later: later + 1}
        split = jnp.moveaxis(split, (place[dp_axis], place[tensor_axis]), (0, 1))
        split = split.reshape((n_dp * n_tensor,) + split.shape[2:])
        return lax.psum_scatter(split, both, scatter_dimension=0, tiled=False).astype(jnp.float32)

    qkv_full = gather(qkv_weight, 1, 2)
    proj_full = gather(proj_weight, 1, 0)
    up_full = gather(fc1_weight, 0, 1)
    down_full = gather(fc2_weight, 1, 0)
    head_full = lax.all_gather(head_bias, "tensor", axis=1, tiled=True)
    fc1_bias_full = lax.all_gather(fc1_bias, "tensor", axis=0, tiled=True)
    tokens_here = lax.dynamic_slice_in_dim(tokens, first_crop, crops, 0)
    mask_here = lax.dynamic_slice_in_dim(patch_mask, first_crop, crops, 0)
    cot_here = lax.dynamic_slice_in_dim(cotangent, first_crop, crops, 0)

    head_cols = qkv_full.shape[2]
    heads_here = head_cols // HD
    joined = jnp.concatenate([qkv_full[0], qkv_full[1], qkv_full[2]], axis=1)
    bias_row = jnp.concatenate([head_full[0], jnp.zeros((head_cols,), jnp.float32), head_full[1]])
    chosen = jnp.concatenate(
        [jnp.zeros((crops, 1 + REG), jnp.bool_), mask_here == 1], axis=1
    ).reshape(rows_here, 1)
    inputs = tokens_here.astype(jnp.float32).reshape(rows_here, width)
    start = jnp.where(chosen, vectors[8], inputs)
    norm_one = layer_norm(start, vectors[0], vectors[1]).astype(jnp.bfloat16)

    def attend(norm_in):
        mixed = (jnp.dot(norm_in, joined, preferred_element_type=jnp.float32) + bias_row).astype(
            jnp.bfloat16
        )
        query = mixed[:, :head_cols].reshape(crops, seq_len, heads_here, HD)
        keys_part = mixed[:, head_cols : 2 * head_cols].reshape(crops, seq_len, heads_here, HD)
        values_part = mixed[:, 2 * head_cols :].reshape(crops, seq_len, heads_here, HD)
        scores = (
            jnp.einsum("bqhe,bkhe->bhqk", query, keys_part, preferred_element_type=jnp.float32)
            * scale
        )
        probs = jax.nn.softmax(scores, axis=-1)
        probs_low = probs.astype(jnp.bfloat16)
        context = jnp.einsum(
            "bhqk,bkhe->bqhe", probs_low, values_part, preferred_element_type=jnp.float32
        )
        context_low = context.astype(jnp.bfloat16).reshape(rows_here, head_cols)
        return (query, keys_part, values_part, probs, probs_low, context_low)

    query, keys_part, values_part, probs, probs_low, context_low = attend(norm_one)
    attn_part = jnp.dot(context_low, proj_full, preferred_element_type=jnp.float32)
    attn = attn_part + vectors[3]
    middle = start + vectors[2] * attn
    norm_two = layer_norm(middle, vectors[4], vectors[5]).astype(jnp.bfloat16)
    hidden = jnp.dot(norm_two, up_full, preferred_element_type=jnp.float32) + fc1_bias_full
    active = gelu_exact(hidden).astype(jnp.bfloat16)
    mlp = jnp.dot(active, down_full, preferred_element_type=jnp.float32) + vectors[7]
    block_here = (middle + vectors[6] * mlp).astype(jnp.bfloat16).reshape(crops, seq_len, width)
    block_out = lax.all_gather(block_here, "tensor", axis=0, tiled=True)
    cot = cot_here.astype(jnp.float32).reshape(rows_here, width)
    mlp_grad = vectors[6] * cot
    grad_scale_two = jnp.sum(cot * mlp, axis=0)
    grad_bias_out = jnp.sum(mlp_grad, axis=0)
    mlp_grad_low = mlp_grad.astype(jnp.bfloat16)
    grad_down = inner_rows(active, mlp_grad_low)
    down_shard = scatter(grad_down, 1, 0)
    grad_active = outer_cols(mlp_grad_low, down_full)
    gelu_value, gelu_back = jax.vjp(gelu_exact, hidden)
    grad_hidden = gelu_back(grad_active)[0].astype(jnp.bfloat16)
    grad_up = inner_rows(norm_two, grad_hidden)
    up_shard = scatter(grad_up, 0, 1)
    grad_fc1_bias = jnp.sum(grad_hidden.astype(jnp.float32), axis=0)
    grad_norm_two = outer_cols(grad_hidden, up_full)
    norm_value, norm_two_back = jax.vjp(layer_norm, middle, vectors[4], vectors[5])
    grad_from_two, grad_gain_two, grad_shift_two = norm_two_back(grad_norm_two)
    grad_middle = cot + grad_from_two
    attn_grad = vectors[2] * grad_middle
    grad_scale_one = jnp.sum(grad_middle * attn, axis=0)
    grad_bias_proj = jnp.sum(attn_grad, axis=0)
    attn_grad_low = attn_grad.astype(jnp.bfloat16)
    grad_proj = inner_rows(context_low, attn_grad_low)
    proj_shard = scatter(grad_proj, 1, 0)
    grad_context = (
        outer_cols(attn_grad_low, proj_full)
        .astype(jnp.bfloat16)
        .reshape(crops, seq_len, heads_here, HD)
    )
    grad_probs = jnp.einsum(
        "bqhe,bkhe->bhqk", grad_context, values_part, preferred_element_type=jnp.float32
    )
    grad_scores = probs * (grad_probs - jnp.sum(grad_probs * probs, axis=-1, keepdims=True))
    grad_scores_low = grad_scores.astype(jnp.bfloat16)
    grad_query = (
        jnp.einsum(
            "bhqk,bkhe->bqhe", grad_scores_low, keys_part, preferred_element_type=jnp.float32
        )
        * scale
    ).astype(jnp.bfloat16)
    grad_keys = (
        jnp.einsum("bhqk,bqhe->bkhe", grad_scores_low, query, preferred_element_type=jnp.float32)
        * scale
    ).astype(jnp.bfloat16)
    grad_values = jnp.einsum(
        "bhqk,bqhe->bkhe", probs_low, grad_context, preferred_element_type=jnp.float32
    ).astype(jnp.bfloat16)
    grad_mixed = jnp.concatenate(
        [
            grad_query.reshape(rows_here, head_cols),
            grad_keys.reshape(rows_here, head_cols),
            grad_values.reshape(rows_here, head_cols),
        ],
        axis=1,
    )
    grad_joined = inner_rows(norm_one, grad_mixed)
    grad_qkv = jnp.stack(
        [
            grad_joined[:, :head_cols],
            grad_joined[:, head_cols : 2 * head_cols],
            grad_joined[:, 2 * head_cols :],
        ]
    )
    qkv_shard = scatter(grad_qkv, 1, 2)
    mixed_sums = jnp.sum(grad_mixed.astype(jnp.float32), axis=0)
    grad_head_bias = jnp.stack([mixed_sums[:head_cols], mixed_sums[2 * head_cols :]])
    grad_norm_one = outer_cols(grad_mixed, joined)
    norm_one_value, norm_one_back = jax.vjp(layer_norm, start, vectors[0], vectors[1])
    grad_from_one, grad_gain_one, grad_shift_one = norm_one_back(grad_norm_one)
    grad_start = grad_middle + grad_from_one
    grad_token_row = jnp.sum(jnp.where(chosen, grad_start, 0.0), axis=0)
    grad_here = (
        jnp.where(chosen, 0.0, grad_start).astype(jnp.bfloat16).reshape(crops, seq_len, width)
    )
    tokens_grad = lax.all_gather(grad_here, "tensor", axis=0, tiled=True)
    vector_grads = jnp.stack(
        [
            grad_gain_one,
            grad_shift_one,
            grad_scale_one,
            grad_bias_proj,
            grad_gain_two,
            grad_shift_two,
            grad_scale_two,
            grad_bias_out,
            grad_token_row,
        ]
    )
    vector_sum, head_all, fc1b_all = lax.psum((vector_grads, grad_head_bias, grad_fc1_bias), both)
    tensor_at = lax.axis_index("tensor")
    head_len = head_bias.shape[1]
    fc1b_len = fc1_bias.shape[0]
    head_sum = lax.dynamic_slice_in_dim(head_all, tensor_at * head_len, head_len, 1)
    fc1b_sum = lax.dynamic_slice_in_dim(fc1b_all, tensor_at * fc1b_len, fc1b_len, 0)
    first_data = (lax.axis_index("dp") == 0).astype(jnp.float32)
    first_tensor = (lax.axis_index("tensor") == 0).astype(jnp.float32)
    local_squares = (
        square_sum(qkv_shard)
        + square_sum(proj_shard)
        + square_sum(up_shard)
        + square_sum(down_shard)
    )
    local_squares = local_squares + first_data * (square_sum(head_sum) + square_sum(fc1b_sum))
    local_squares = local_squares + first_data * first_tensor * square_sum(vector_sum)
    total_squares = lax.psum(local_squares, ("dp", "tensor"))
    grad_norm = jnp.sqrt(total_squares)
    factor = jnp.minimum(1.0, clip_norm / (grad_norm + 1e-06))
    qkv_set = adam_step(
        qkv_weight, qkv_first, qkv_second, factor * qkv_shard, rate_matrix, decay_matrix
    )
    proj_set = adam_step(
        proj_weight, proj_first, proj_second, factor * proj_shard, rate_matrix, decay_matrix
    )
    fc1_set = adam_step(
        fc1_weight, fc1_first, fc1_second, factor * up_shard, rate_matrix, decay_matrix
    )
    fc2_set = adam_step(
        fc2_weight, fc2_first, fc2_second, factor * down_shard, rate_matrix, decay_matrix
    )
    vectors_set = adam_step(
        vectors, vectors_first, vectors_second, factor * vector_sum, rate_vector, 0.0
    )
    head_set = adam_step(
        head_bias, head_bias_first, head_bias_second, factor * head_sum, rate_vector, 0.0
    )
    fc1b_set = adam_step(
        fc1_bias, fc1_bias_first, fc1_bias_second, factor * fc1b_sum, rate_vector, 0.0
    )
    return (
        block_out,
        tokens_grad,
        grad_norm,
        qkv_set[0],
        qkv_set[1],
        qkv_set[2],
        proj_set[0],
        proj_set[1],
        proj_set[2],
        fc1_set[0],
        fc1_set[1],
        fc1_set[2],
        fc2_set[0],
        fc2_set[1],
        fc2_set[2],
        vectors_set[0],
        vectors_set[1],
        vectors_set[2],
        head_set[0],
        head_set[1],
        head_set[2],
        fc1b_set[0],
        fc1b_set[1],
        fc1b_set[2],
        qkv_set[0].astype(jnp.bfloat16),
        proj_set[0].astype(jnp.bfloat16),
        fc1_set[0].astype(jnp.bfloat16),
        fc2_set[0].astype(jnp.bfloat16),
    )


def solution(mesh):
    placed = (
        P("dp", None, None),
        P("dp", None),
        P("dp", None, None),
        P(None, "dp", "tensor"),
        P(None, "dp", "tensor"),
        P(None, "dp", "tensor"),
        P("tensor", "dp"),
        P("tensor", "dp"),
        P("tensor", "dp"),
        P("dp", "tensor"),
        P("dp", "tensor"),
        P("dp", "tensor"),
        P("tensor", "dp"),
        P("tensor", "dp"),
        P("tensor", "dp"),
        P(),
        P(),
        P(),
        P(None, "tensor"),
        P(None, "tensor"),
        P(None, "tensor"),
        P("tensor"),
        P("tensor"),
        P("tensor"),
    )
    return jax.shard_map(
        per_device,
        mesh=mesh,
        in_specs=placed,
        out_specs=(
            P("dp", None, None),
            P("dp", None, None),
            P(),
            P(None, "dp", "tensor"),
            P(None, "dp", "tensor"),
            P(None, "dp", "tensor"),
            P("tensor", "dp"),
            P("tensor", "dp"),
            P("tensor", "dp"),
            P("dp", "tensor"),
            P("dp", "tensor"),
            P("dp", "tensor"),
            P("tensor", "dp"),
            P("tensor", "dp"),
            P("tensor", "dp"),
            P(),
            P(),
            P(),
            P(None, "tensor"),
            P(None, "tensor"),
            P(None, "tensor"),
            P("tensor"),
            P("tensor"),
            P("tensor"),
            P(None, "dp", "tensor"),
            P("tensor", "dp"),
            P("dp", "tensor"),
            P("tensor", "dp"),
        ),
        check_vma=False,
    )
```

```python
import functools

import jax
import jax.numpy as jnp
from jax import lax
from jax.experimental import pallas as pl
from jax.experimental.pallas import tpu as pltpu
from jax.sharding import PartitionSpec as P

HD = 64
REG = 4
STEP = 10
GROUP = 8
PIECES = 3
CHUNK = 16

norm_eps = 1e-06
clip_norm = 1.0
rate_matrix = 0.04
rate_vector = 0.2
decay_matrix = 0.04
moment_decay = 0.5
adam_eps = 1e-08

def square_sum(values):
    return jnp.sum(values * values)


def adam_step(weight, first, second, grad, rate, decay):
    first_new = moment_decay * first + (1.0 - moment_decay) * grad
    second_new = moment_decay * second + (1.0 - moment_decay) * grad * grad
    correct = 1.0 - moment_decay**STEP
    weight_new = weight - rate * (
        first_new / correct / (jnp.sqrt(second_new / correct) + adam_eps) + decay * weight
    )
    return (weight_new, first_new, second_new)


def nn(a, b):
    return lax.dot_general(a, b, (((1,), (0,)), ((), ())), preferred_element_type=jnp.float32)


def nt(a, b):
    return lax.dot_general(a, b, (((1,), (1,)), ((), ())), preferred_element_type=jnp.float32)


def tn(a, b):
    return lax.dot_general(a, b, (((0,), (0,)), ((), ())), preferred_element_type=jnp.float32)


def low(values):
    return values.astype(jnp.bfloat16)


def wide(values):
    return values.astype(jnp.float32)


def fold(values):
    return values[:8] + values[8:]


def remote(src, dst, send, recv, device):
    return pltpu.make_async_remote_copy(
        src_ref=src,
        dst_ref=dst,
        send_sem=send,
        recv_sem=recv,
        device_id=device,
        device_id_type=pl.DeviceIdType.MESH,
    )


def block_kernel(
    dims,
    pack,
    x_in,
    cot_in,
    mask_in,
    vec,
    mix_bias,
    up_bias,
    out_block,
    out_tokens,
    shard_out,
    vec_out,
    mix_out,
    up_out,
    store,
    norm_one,
    turned_one,
    mixed,
    probs,
    context,
    attn_sum,
    middle,
    norm_two,
    turned_two,
    mlp_grad,
    turned_mlp,
    active,
    slope,
    wide_one,
    wide_two,
    grad_mid,
    attn_grad,
    turned_attn,
    gmixed,
    result,
    core_ring,
    diag_ring,
    dir_ring,
    line_in,
    z_send,
    z_recv,
    xy_send,
    xy_recv,
    diag_send,
    diag_recv,
    core_send,
    core_recv,
    rc_send,
    rc_recv,
    rd_send,
    rd_recv,
    rx_send,
    rx_recv,
    rz_send,
    rz_recv,
    ob_send,
    ob_recv,
    og_send,
    og_recv,
    own_sem,
):
    n_dp, n_t, seq, pad_seq, crops, heads = dims
    stride = n_dp // GROUP
    rows = crops * pad_seq
    unit = pack.shape[1]
    half = unit // 2
    width = pack.shape[2]
    head_cols = heads * HD
    mix_cols = 3 * head_cols
    scale = HD ** (-0.5)
    n_chunks = rows // CHUNK

    d = lax.axis_index("dp")
    z = lax.axis_index("tensor")
    place = d // stride
    c = place % 2
    yx = place // 2
    xbit = yx % 2
    ybit = yx // 2
    yx_x = yx + 1 - 2 * xbit
    yx_y = yx + 2 - 4 * ybit
    yx_d = 3 - yx
    to_core = (d + (1 - 2 * c) * stride, z)
    to_x = (d + (1 - 2 * xbit) * 2 * stride, z)
    to_y = (d + (1 - 2 * ybit) * 4 * stride, z)

    def to_line(k):
        return (d, (z + k) % n_t)

    barrier = pltpu.get_barrier_semaphore()
    peers = [to_core, to_x, to_y] + [to_line(k) for k in range(1, n_t)]
    for peer in peers:
        pl.semaphore_signal(
            barrier, inc=1, device_id=peer, device_id_type=pl.DeviceIdType.MESH
        )
    pl.semaphore_wait(barrier, len(peers))

    n_jobs = PIECES * n_t

    def z_copy(m, k):
        src = store.at[m, z, yx, c]
        return remote(src, src, z_send.at[m, k - 1], z_recv.at[m, k - 1], to_line(k))

    def block_at(i, which):
        m, k = i // n_t, i % n_t
        return store.at[m, (z + n_t - k) % n_t, which, c]

    def direct(i, axis):
        src = block_at(i, yx)
        return remote(
            src, src, xy_send.at[i, axis], xy_recv.at[i, axis], to_x if axis == 0 else to_y
        )

    def diagonal(i, axis):
        which = yx_x if axis == 1 else yx_y
        src = block_at(i, which).at[pl.ds(0 if axis == 1 else half, half)]
        return remote(
            src, src, diag_send.at[i, axis], diag_recv.at[i, axis], to_x if axis == 0 else to_y
        )

    def across(i, slot):
        src = block_at(i, (yx, yx_x, yx_y, yx_d)[slot])
        return remote(src, src, core_send.at[i, slot], core_recv.at[i, slot], to_core)

    def start_line(m):
        for k in range(1, n_t):
            z_copy(m, k).start()

    def gather_tick(i):
        @pl.when(jnp.logical_and(i >= 2, i - 2 < n_jobs))
        def _():
            j = jnp.maximum(i - 2, 0)
            diagonal(j, 0).wait_recv()
            diagonal(j, 1).wait_recv()
            across(j, 3).start()

        @pl.when(jnp.logical_and(i >= 1, i - 1 < n_jobs))
        def _():
            j = jnp.maximum(i - 1, 0)
            direct(j, 0).wait_recv()
            diagonal(j, 1).start()
            direct(j, 1).wait_recv()
            diagonal(j, 0).start()
            across(j, 1).start()
            across(j, 2).start()

        @pl.when(i < n_jobs)
        def _():
            j = jnp.minimum(i, n_jobs - 1)
            m, k = j // n_t, j % n_t

            @pl.when(k > 0)
            def _():
                z_copy(m, jnp.maximum(k, 1)).wait_recv()

            direct(j, 0).start()
            direct(j, 1).start()
            across(j, 0).start()

            @pl.when(jnp.logical_and(k == n_t - 1, m < PIECES - 1))
            def _():
                start_line(m + 1)

    def gather_end(m):
        def body(k, carry):
            for slot in range(4):
                across(m * n_t + k, slot).wait_recv()
            return carry

        lax.fori_loop(0, n_t, body, 0)

    def gather_sent(m):
        for k in range(1, n_t):
            z_copy(m, k).wait_send()

        def body(k, carry):
            i = m * n_t + k
            for axis in range(2):
                direct(i, axis).wait_send()
                diagonal(i, axis).wait_send()
            for slot in range(4):
                across(i, slot).wait_send()
            return carry

        lax.fori_loop(0, n_t, body, 0)

    def job_slot(j):
        return 3 - j // n_t, j % n_t

    def rs_core(j):
        slot, t = job_slot(j)
        return remote(
            store.at[slot, t, :, 1 - c],
            core_ring.at[j % 2],
            rc_send.at[j],
            rc_recv.at[j],
            to_core,
        )

    def rs_diag(j, axis):
        slot, t = job_slot(j)
        return remote(
            store.at[slot, t, yx_d, c, pl.ds(axis * half, half)],
            diag_ring.at[j % 2, axis],
            rd_send.at[j, axis],
            rd_recv.at[j, axis],
            to_x if axis == 0 else to_y,
        )

    def rs_direct(j, axis):
        slot, t = job_slot(j)
        return remote(
            store.at[slot, t, yx_x if axis == 0 else yx_y, c],
            dir_ring.at[j % 2, axis],
            rx_send.at[j, axis],
            rx_recv.at[j, axis],
            to_x if axis == 0 else to_y,
        )

    def rs_line_out(j):
        slot, t = job_slot(j)
        k = (z + n_t - t) % n_t
        m = PIECES - 1 - j // n_t
        return remote(
            store.at[slot, t, yx, c],
            line_in.at[m, jnp.maximum(k, 1) - 1],
            rz_send.at[j],
            rz_recv.at[m, jnp.maximum(k, 1) - 1],
            (d, t),
        )

    def rs_line_in(m, k):
        return remote(
            line_in.at[m, k - 1],
            line_in.at[m, k - 1],
            rz_send.at[0],
            rz_recv.at[m, k - 1],
            to_line(1),
        )

    def reduce_stage(stage, j):
        slot, t = job_slot(j)
        if stage == 0:
            rs_core(j).start()
        if stage == 1:
            rs_core(j).wait_recv()
            per = unit // CHUNK

            def body(s, carry):
                at = pl.ds(pl.multiple_of((s % per) * CHUNK, CHUNK), CHUNK)
                which = s // per
                store[slot, t, which, c, at] = low(
                    wide(store[slot, t, which, c, at]) + wide(core_ring[j % 2, which, at])
                )
                return carry

            lax.fori_loop(0, 4 * per, body, 0)
            rs_diag(j, 0).start()
            rs_diag(j, 1).start()
        if stage == 2:
            for axis in range(2):
                rs_diag(j, axis).wait_recv()
                which = yx_y if axis == 0 else yx_x
                at = pl.ds(axis * half, half)
                store[slot, t, which, c, at] = low(
                    wide(store[slot, t, which, c, at]) + wide(diag_ring[j % 2, axis])
                )
            rs_direct(j, 0).start()
            rs_direct(j, 1).start()
        if stage == 3:
            rs_direct(j, 0).wait_recv()
            rs_direct(j, 1).wait_recv()
            total = (
                wide(store[slot, t, yx, c])
                + wide(dir_ring[j % 2, 0])
                + wide(dir_ring[j % 2, 1])
            )

            @pl.when(t == z)
            def _():
                shard_out[PIECES - 1 - j // n_t] = total

            @pl.when(t != z)
            def _():
                store[slot, t, yx, c] = low(total)
                rs_line_out(j).start()

    def reduce_tick(i):
        for stage in (3, 2, 1, 0):

            @pl.when(jnp.logical_and(i >= stage, i - stage < n_jobs))
            def _():
                reduce_stage(stage, jnp.clip(i - stage, 0, n_jobs - 1))

    def line_step(s, out, send, recv, first_src):
        def up():
            shard = jnp.maximum(z - s + 1, 0)
            src = first_src if s == 1 else out.at[shard]
            return remote(src, out.at[shard], send.at[0, s - 1], recv.at[0, s - 1], to_line(1))

        def down():
            shard = jnp.minimum(z + s - 1, n_t - 1)
            src = first_src if s == 1 else out.at[shard]
            return remote(
                src, out.at[shard], send.at[1, s - 1], recv.at[1, s - 1], to_line(n_t - 1)
            )

        return up, down

    def line_start(s, out, send, recv, first_src):
        up, down = line_step(s, out, send, recv, first_src)

        @pl.when(jnp.logical_and(z - s + 1 >= 0, z < n_t - 1))
        def _():
            up().start()

        @pl.when(jnp.logical_and(z + s - 1 <= n_t - 1, z > 0))
        def _():
            down().start()

    def line_recv(s, out, send, recv, first_src):
        up, down = line_step(s, out, send, recv, first_src)

        @pl.when(z - s >= 0)
        def _():
            up().wait_recv()

        @pl.when(z + s <= n_t - 1)
        def _():
            down().wait_recv()

    def line_sent(s, out, send, recv, first_src):
        up, down = line_step(s, out, send, recv, first_src)

        @pl.when(jnp.logical_and(z - s + 1 >= 0, z < n_t - 1))
        def _():
            up().wait_send()

        @pl.when(jnp.logical_and(z + s - 1 <= n_t - 1, z > 0))
        def _():
            down().wait_send()

    line_block = (out_block, ob_send, ob_recv, result.at[0])
    line_tokens = (out_tokens, og_send, og_recv, result.at[1])

    for m in range(PIECES):
        store[m, z, yx, c] = pack[m]
    start_line(0)
    gather_tick(0)

    def matrix(slot, t):
        return store[slot, t].reshape(GROUP * unit, width)

    def chunk_at(i):
        return pl.ds(pl.multiple_of(i * CHUNK, CHUNK), CHUNK)

    def start_of(at):
        chosen = mask_in[at, :] > 0.5
        return jnp.where(chosen, vec[8:9, :], wide(x_in[at, :])), chosen

    def normal(values):
        mean = jnp.mean(values, axis=-1, keepdims=True)
        centred = values - mean
        spread = jnp.mean(centred * centred, axis=-1, keepdims=True)
        rate = lax.rsqrt(spread + norm_eps)
        return centred * rate, rate

    def first_norm(i, total):
        at = chunk_at(i)
        begin, _ = start_of(at)
        hat, _ = normal(begin)
        norm_one[at, :] = low(hat * vec[0:1, :] + vec[1:2, :])
        cot = wide(cot_in[at, :])
        mlp_grad[at, :] = low(vec[6:7, :] * cot)
        return total + fold(cot)

    zero8 = jnp.zeros((8, width), jnp.float32)
    cot_total = lax.fori_loop(0, n_chunks, first_norm, zero8)
    vec_out[7:8, :] = vec[6:7, :] * jnp.sum(cot_total, axis=0, keepdims=True)
    turned_one[...] = norm_one[...].T
    turned_mlp[...] = mlp_grad[...].T
    attn_sum[...] = jnp.zeros_like(attn_sum)

    def early(i, carry):
        gather_tick(i)
        return carry

    lax.fori_loop(1, n_t + 2, early, 0)
    gather_end(0)

    key_ok = lax.broadcasted_iota(jnp.int32, (1, pad_seq), 1) < seq

    def attend(t, carry):
        mixed[t] = low(nn(norm_one[...], matrix(0, t)[:, :mix_cols]) + mix_bias[t])

        def crop_body(b, inner):
            at = pl.ds(pl.multiple_of(b * pad_seq, CHUNK), pad_seq)
            mine = mixed[t, at, :]
            parts = []
            for h in range(heads):
                q = mine[:, h * HD : (h + 1) * HD]
                k = mine[:, head_cols + h * HD : head_cols + (h + 1) * HD]
                v = mine[:, 2 * head_cols + h * HD : 2 * head_cols + (h + 1) * HD]
                s = jnp.where(key_ok, nt(q, k) * scale, -1e30)
                e = jnp.exp(s - jnp.max(s, axis=-1, keepdims=True))
                p = low(e / jnp.sum(e, axis=-1, keepdims=True))
                probs[t, b, h] = p
                parts.append(low(nn(p, v)))
            context[t, at, :] = jnp.concatenate(parts, axis=1)
            return inner

        lax.fori_loop(0, crops, crop_body, 0)
        attn_sum[...] += nt(context[t], matrix(0, t)[:, mix_cols:])
        gather_tick(n_t + 2 + t)
        return carry

    lax.fori_loop(0, n_t, attend, 0)

    def second_norm(i, carry):
        at = chunk_at(i)
        begin, _ = start_of(at)
        mid = begin + vec[2:3, :] * (attn_sum[at, :] + vec[3:4, :])
        middle[at, :] = mid
        hat, _ = normal(mid)
        norm_two[at, :] = low(hat * vec[4:5, :] + vec[5:6, :])
        return carry

    lax.fori_loop(0, n_chunks, second_norm, 0)
    turned_two[...] = norm_two[...].T
    gather_end(1)

    def hidden_units(t, carry):
        wide_one[...] = nn(norm_two[...], matrix(1, t)) + up_bias[t]

        def bend(i, inner):
            at = chunk_at(i)
            h = wide_one[at, :]
            cdf = 0.5 + 0.5 * lax.erf(h * 0.7071067811865476)
            active[t, at, :] = low(h * cdf)
            slope[t, at, :] = low(cdf + h * jnp.exp(-0.5 * h * h) * 0.3989422804014327)
            return inner

        lax.fori_loop(0, n_chunks, bend, 0)
        store[3, t] = low(nn(turned_mlp[...], active[t])).reshape(4, 2, unit, width)
        reduce_tick(t)
        gather_tick(2 * n_t + 2 + t)
        return carry

    lax.fori_loop(0, n_t, hidden_units, 0)
    gather_sent(1)
    gather_end(2)

    wide_one[...] = jnp.zeros_like(wide_one)

    def mlp_out(t, carry):
        wide_one[...] += nt(active[t], matrix(2, t))
        return carry

    lax.fori_loop(0, n_t, mlp_out, 0)

    def finish_block(i, total):
        at = chunk_at(i)
        mlp = wide_one[at, :] + vec[7:8, :]
        result[0, at, :] = low(middle[at, :] + vec[6:7, :] * mlp)
        return total + fold(wide(cot_in[at, :]) * mlp)

    mlp_total = lax.fori_loop(0, n_chunks, finish_block, zero8)
    vec_out[6:7, :] = jnp.sum(mlp_total, axis=0, keepdims=True)
    line_start(1, *line_block)
    own_block = pltpu.make_async_copy(result.at[0], out_block.at[z], own_sem.at[0])
    own_block.start()
    gather_sent(2)

    wide_one[...] = jnp.zeros_like(wide_one)
    ones = jnp.ones((CHUNK, rows), jnp.bfloat16)

    def hidden_back(t, carry):
        wide_two[...] = nn(mlp_grad[...], matrix(2, t))

        def bend(i, inner):
            at = chunk_at(i)
            slope[t, at, :] = low(wide(slope[t, at, :]) * wide_two[at, :])
            return inner

        lax.fori_loop(0, n_chunks, bend, 0)
        up_out[t] = nn(ones, slope[t])[:1]
        store[2, t] = low(nn(turned_two[...], slope[t])).reshape(4, 2, unit, width)
        wide_one[...] += nt(slope[t], matrix(1, t))
        reduce_tick(n_t + t)
        return carry

    lax.fori_loop(0, n_t, hidden_back, 0)
    line_recv(1, *line_block)
    line_start(2, *line_block)

    def second_back(i, totals):
        gain, shift, scale_one, bias_proj = totals
        at = chunk_at(i)
        upstream = wide_one[at, :]
        hat, rate = normal(middle[at, :])
        e = vec[4:5, :] * upstream
        inner = e - jnp.mean(e, axis=-1, keepdims=True)
        inner = inner - hat * jnp.mean(e * hat, axis=-1, keepdims=True)
        g = wide(cot_in[at, :]) + rate * inner
        grad_mid[at, :] = g
        attn_grad[at, :] = low(vec[2:3, :] * g)
        return (
            gain + fold(upstream * hat),
            shift + fold(upstream),
            scale_one + fold(g * (attn_sum[at, :] + vec[3:4, :])),
            bias_proj + fold(g),
        )

    gain, shift, scale_one, bias_proj = lax.fori_loop(0, n_chunks, second_back, (zero8,) * 4)
    vec_out[4:5, :] = jnp.sum(gain, axis=0, keepdims=True)
    vec_out[5:6, :] = jnp.sum(shift, axis=0, keepdims=True)
    vec_out[2:3, :] = jnp.sum(scale_one, axis=0, keepdims=True)
    vec_out[3:4, :] = vec[2:3, :] * jnp.sum(bias_proj, axis=0, keepdims=True)
    turned_attn[...] = attn_grad[...].T
    wide_one[...] = jnp.zeros_like(wide_one)

    def attend_back(t, carry):
        gctx = low(nn(attn_grad[...], matrix(0, t)[:, mix_cols:]))
        gmixed[:, :head_cols] = gctx

        def crop_body(b, inner):
            at = pl.ds(pl.multiple_of(b * pad_seq, CHUNK), pad_seq)
            mine = mixed[t, at, :]
            theirs = gmixed[at, :head_cols]
            gq, gk, gv = [], [], []
            for h in range(heads):
                q = mine[:, h * HD : (h + 1) * HD]
                k = mine[:, head_cols + h * HD : head_cols + (h + 1) * HD]
                v = mine[:, 2 * head_cols + h * HD : 2 * head_cols + (h + 1) * HD]
                g = theirs[:, h * HD : (h + 1) * HD]
                p_low = probs[t, b, h]
                p = wide(p_low)
                gp = nt(g, v)
                gs = low(p * (gp - jnp.sum(gp * p, axis=-1, keepdims=True)))
                gq.append(low(nn(gs, k) * scale))
                gk.append(low(tn(gs, q) * scale))
                gv.append(low(tn(p_low, g)))
            gmixed[at, :] = jnp.concatenate(gq + gk + gv, axis=1)
            return inner

        lax.fori_loop(0, crops, crop_body, 0)
        mix_out[t] = nn(ones, gmixed[...])[:1]
        fresh = jnp.concatenate(
            [
                low(nn(turned_one[...], gmixed[...])),
                low(nn(turned_attn[...], context[t])),
            ],
            axis=1,
        )
        store[1, t] = fresh.reshape(4, 2, unit, width)
        wide_one[...] += nt(gmixed[...], matrix(0, t)[:, :mix_cols])
        reduce_tick(2 * n_t + t)
        return carry

    lax.fori_loop(0, n_t, attend_back, 0)
    line_recv(2, *line_block)
    line_start(3, *line_block)

    def first_back(i, totals):
        gain, shift, token = totals
        at = chunk_at(i)
        upstream = wide_one[at, :]
        begin, chosen = start_of(at)
        hat, rate = normal(begin)
        e = vec[0:1, :] * upstream
        inner = e - jnp.mean(e, axis=-1, keepdims=True)
        inner = inner - hat * jnp.mean(e * hat, axis=-1, keepdims=True)
        g = grad_mid[at, :] + rate * inner
        result[1, at, :] = low(jnp.where(chosen, 0.0, g))
        return (
            gain + fold(upstream * hat),
            shift + fold(upstream),
            token + fold(jnp.where(chosen, g, 0.0)),
        )

    gain, shift, token = lax.fori_loop(0, n_chunks, first_back, (zero8,) * 3)
    vec_out[0:1, :] = jnp.sum(gain, axis=0, keepdims=True)
    vec_out[1:2, :] = jnp.sum(shift, axis=0, keepdims=True)
    vec_out[8:9, :] = jnp.sum(token, axis=0, keepdims=True)
    line_start(1, *line_tokens)
    own_tokens = pltpu.make_async_copy(result.at[1], out_tokens.at[z], own_sem.at[1])
    own_tokens.start()

    def late(i, carry):
        reduce_tick(i)
        return carry

    lax.fori_loop(n_jobs, n_jobs + 3, late, 0)
    line_recv(1, *line_tokens)
    line_start(2, *line_tokens)
    for m in (2, 1, 0):
        for k in range(1, n_t):
            rs_line_in(m, k).wait_recv()
        total = shard_out[m]
        for k in range(1, n_t):
            total = total + wide(line_in[m, k - 1])
        shard_out[m] = total
    line_recv(2, *line_tokens)
    line_start(3, *line_tokens)

    gather_sent(0)

    def sent(j, carry):
        rs_core(j).wait_send()
        for axis in range(2):
            rs_diag(j, axis).wait_send()
            rs_direct(j, axis).wait_send()

        @pl.when(j % n_t != z)
        def _():
            rs_line_out(j).wait_send()

        return carry

    lax.fori_loop(0, n_jobs, sent, 0)
    line_recv(3, *line_block)
    line_recv(3, *line_tokens)
    for s in (1, 2, 3):
        line_sent(s, *line_block)
        line_sent(s, *line_tokens)
    own_block.wait()
    own_tokens.wait()


def run_block(n_dp, n_t, seq, pack, x_in, cot_in, mask_in, vec, mix_bias, up_bias, pad_seq, crops, heads):
    unit, width = pack.shape[1:]
    rows = crops * pad_seq
    head_cols = heads * HD
    mix_cols = 3 * head_cols
    n_jobs = PIECES * n_t
    bf16, f32 = jnp.bfloat16, jnp.float32
    vmem = pltpu.VMEM
    dma = pltpu.SemaphoreType.DMA
    inside = pl.BlockSpec(memory_space=pltpu.VMEM)
    outside = pl.BlockSpec(memory_space=pl.ANY)
    return pl.pallas_call(
        functools.partial(block_kernel, (n_dp, n_t, seq, pad_seq, crops, heads)),
        out_shape=(
            jax.ShapeDtypeStruct((n_t, rows, width), bf16),
            jax.ShapeDtypeStruct((n_t, rows, width), bf16),
            jax.ShapeDtypeStruct((PIECES, unit, width), f32),
            jax.ShapeDtypeStruct((16, width), f32),
            jax.ShapeDtypeStruct((n_t, 1, mix_cols), f32),
            jax.ShapeDtypeStruct((n_t, 1, width), f32),
        ),
        in_specs=[inside] * 7,
        out_specs=(outside, outside, inside, inside, inside, inside),
        scratch_shapes=[
            vmem((4, n_t, 4, 2, unit, width), bf16),
            vmem((rows, width), bf16),
            vmem((width, rows), bf16),
            vmem((n_t, rows, mix_cols), bf16),
            vmem((n_t, crops, heads, pad_seq, pad_seq), bf16),
            vmem((n_t, rows, head_cols), bf16),
            vmem((rows, width), f32),
            vmem((rows, width), f32),
            vmem((rows, width), bf16),
            vmem((width, rows), bf16),
            vmem((rows, width), bf16),
            vmem((width, rows), bf16),
            vmem((n_t, rows, width), bf16),
            vmem((n_t, rows, width), bf16),
            vmem((rows, width), f32),
            vmem((rows, width), f32),
            vmem((rows, width), f32),
            vmem((rows, width), bf16),
            vmem((width, rows), bf16),
            vmem((rows, mix_cols), bf16),
            vmem((2, rows, width), bf16),
            vmem((2, 4, unit, width), bf16),
            vmem((2, 2, unit // 2, width), bf16),
            vmem((2, 2, unit, width), bf16),
            vmem((PIECES, n_t - 1, unit, width), bf16),
            dma((PIECES, n_t - 1)),
            dma((PIECES, n_t - 1)),
            dma((n_jobs, 2)),
            dma((n_jobs, 2)),
            dma((n_jobs, 2)),
            dma((n_jobs, 2)),
            dma((n_jobs, 4)),
            dma((n_jobs, 4)),
            dma((n_jobs,)),
            dma((n_jobs,)),
            dma((n_jobs, 2)),
            dma((n_jobs, 2)),
            dma((n_jobs, 2)),
            dma((n_jobs, 2)),
            dma((n_jobs,)),
            dma((PIECES, n_t - 1)),
            dma((2, n_t - 1)),
            dma((2, n_t - 1)),
            dma((2, n_t - 1)),
            dma((2, n_t - 1)),
            dma((2,)),
        ],
        compiler_params=pltpu.CompilerParams(
            collective_id=0, has_side_effects=True, vmem_limit_bytes=62 * 1024 * 1024
        ),
        name="block_step",
    )(pack, x_in, cot_in, mask_in, vec, mix_bias, up_bias)


def per_device(
    tokens,
    patch_mask,
    cotangent,
    qkv_weight,
    qkv_first,
    qkv_second,
    proj_weight,
    proj_first,
    proj_second,
    fc1_weight,
    fc1_first,
    fc1_second,
    fc2_weight,
    fc2_first,
    fc2_second,
    vectors,
    vectors_first,
    vectors_second,
    head_bias,
    head_bias_first,
    head_bias_second,
    fc1_bias,
    fc1_bias_first,
    fc1_bias_second,
):
    all_crops, seq, width = tokens.shape
    n_dp = lax.axis_size("dp")
    n_t = lax.axis_size("tensor")
    tensor_at = lax.axis_index("tensor")
    crops = all_crops // n_t
    head_cols = qkv_weight.shape[2]
    heads = head_cols // HD
    pad_seq = -(-seq // 16) * 16
    rows = crops * pad_seq
    stride = n_dp // GROUP
    both = ("dp", "tensor")

    def padded(array):
        here = lax.dynamic_slice_in_dim(array, tensor_at * crops, crops, 0)
        spare = [(0, 0), (0, pad_seq - seq), (0, 0)]
        return jnp.pad(here, spare).reshape(rows, -1)

    x_in = padded(tokens)
    cot_in = padded(cotangent)
    mask_all = jnp.pad(patch_mask, [(0, 0), (1 + REG, 0)]).astype(jnp.float32)
    mask_in = padded(mask_all[:, :, None])
    pack = jnp.stack(
        [
            jnp.concatenate(
                [qkv_weight[0], qkv_weight[1], qkv_weight[2], proj_weight.T], axis=1
            ),
            fc1_weight,
            fc2_weight.T,
        ]
    ).astype(jnp.bfloat16)
    if stride > 1:
        teams = [[b * stride + i for i in range(stride)] for b in range(GROUP)]
        pack = lax.all_gather(pack, "dp", axis_index_groups=teams, axis=1, tiled=True)
    head_all = lax.all_gather(head_bias, "tensor", axis=0, tiled=False)
    up_bias = lax.all_gather(fc1_bias, "tensor", axis=0, tiled=False).reshape(n_t, 1, -1)
    mix_bias = jnp.concatenate(
        [head_all[:, :1], jnp.zeros((n_t, 1, head_cols), jnp.float32), head_all[:, 1:]], axis=2
    )
    block_all, grad_all, shard, vec_sums, mix_sums, up_sums = run_block(
        n_dp, n_t, seq, pack, x_in, cot_in, mask_in, vectors, mix_bias, up_bias, pad_seq, crops, heads
    )

    def whole(array):
        return array.reshape(all_crops, pad_seq, width)[:, :seq]

    block_out = whole(block_all)
    tokens_grad = whole(grad_all)
    if stride > 1:
        shard = lax.psum_scatter(
            shard, "dp", scatter_dimension=1, axis_index_groups=teams, tiled=True
        )
    qkv_shard = jnp.stack([shard[0, :, i * head_cols : (i + 1) * head_cols] for i in range(3)])
    proj_shard = shard[0, :, 3 * head_cols :].T
    up_shard = shard[1]
    down_shard = shard[2].T
    vector_sum, mix_all, up_all = lax.psum((vec_sums, mix_sums, up_sums), both)
    vector_sum = vector_sum[:9]
    mix_here = lax.dynamic_slice_in_dim(mix_all, tensor_at, 1, 0)[0, 0]
    head_sum = jnp.stack([mix_here[:head_cols], mix_here[2 * head_cols :]])
    fc1b_sum = lax.dynamic_slice_in_dim(up_all, tensor_at, 1, 0)[0, 0]
    first_data = (lax.axis_index("dp") == 0).astype(jnp.float32)
    first_tensor = (lax.axis_index("tensor") == 0).astype(jnp.float32)
    local_squares = (
        square_sum(qkv_shard)
        + square_sum(proj_shard)
        + square_sum(up_shard)
        + square_sum(down_shard)
    )
    local_squares = local_squares + first_data * (square_sum(head_sum) + square_sum(fc1b_sum))
    local_squares = local_squares + first_data * first_tensor * square_sum(vector_sum)
    total_squares = lax.psum(local_squares, ("dp", "tensor"))
    grad_norm = jnp.sqrt(total_squares)
    factor = jnp.minimum(1.0, clip_norm / (grad_norm + 1e-06))
    qkv_set = adam_step(
        qkv_weight, qkv_first, qkv_second, factor * qkv_shard, rate_matrix, decay_matrix
    )
    proj_set = adam_step(
        proj_weight, proj_first, proj_second, factor * proj_shard, rate_matrix, decay_matrix
    )
    fc1_set = adam_step(
        fc1_weight, fc1_first, fc1_second, factor * up_shard, rate_matrix, decay_matrix
    )
    fc2_set = adam_step(
        fc2_weight, fc2_first, fc2_second, factor * down_shard, rate_matrix, decay_matrix
    )
    vectors_set = adam_step(
        vectors, vectors_first, vectors_second, factor * vector_sum, rate_vector, 0.0
    )
    head_set = adam_step(
        head_bias, head_bias_first, head_bias_second, factor * head_sum, rate_vector, 0.0
    )
    fc1b_set = adam_step(
        fc1_bias, fc1_bias_first, fc1_bias_second, factor * fc1b_sum, rate_vector, 0.0
    )
    return (
        block_out,
        tokens_grad,
        grad_norm,
        qkv_set[0],
        qkv_set[1],
        qkv_set[2],
        proj_set[0],
        proj_set[1],
        proj_set[2],
        fc1_set[0],
        fc1_set[1],
        fc1_set[2],
        fc2_set[0],
        fc2_set[1],
        fc2_set[2],
        vectors_set[0],
        vectors_set[1],
        vectors_set[2],
        head_set[0],
        head_set[1],
        head_set[2],
        fc1b_set[0],
        fc1b_set[1],
        fc1b_set[2],
        qkv_set[0].astype(jnp.bfloat16),
        proj_set[0].astype(jnp.bfloat16),
        fc1_set[0].astype(jnp.bfloat16),
        fc2_set[0].astype(jnp.bfloat16),
    )


def solution(mesh):
    placed = (
        P("dp", None, None),
        P("dp", None),
        P("dp", None, None),
        P(None, "dp", "tensor"),
        P(None, "dp", "tensor"),
        P(None, "dp", "tensor"),
        P("tensor", "dp"),
        P("tensor", "dp"),
        P("tensor", "dp"),
        P("dp", "tensor"),
        P("dp", "tensor"),
        P("dp", "tensor"),
        P("tensor", "dp"),
        P("tensor", "dp"),
        P("tensor", "dp"),
        P(),
        P(),
        P(),
        P(None, "tensor"),
        P(None, "tensor"),
        P(None, "tensor"),
        P("tensor"),
        P("tensor"),
        P("tensor"),
    )
    return jax.shard_map(
        per_device,
        mesh=mesh,
        in_specs=placed,
        out_specs=(
            P("dp", None, None),
            P("dp", None, None),
            P(),
            P(None, "dp", "tensor"),
            P(None, "dp", "tensor"),
            P(None, "dp", "tensor"),
            P("tensor", "dp"),
            P("tensor", "dp"),
            P("tensor", "dp"),
            P("dp", "tensor"),
            P("dp", "tensor"),
            P("dp", "tensor"),
            P("tensor", "dp"),
            P("tensor", "dp"),
            P("tensor", "dp"),
            P(),
            P(),
            P(),
            P(None, "tensor"),
            P(None, "tensor"),
            P(None, "tensor"),
            P("tensor"),
            P("tensor"),
            P("tensor"),
            P(None, "dp", "tensor"),
            P("tensor", "dp"),
            P("dp", "tensor"),
            P("tensor", "dp"),
        ),
        check_vma=False,
    )
```

```python
import functools

import jax
import jax.numpy as jnp
from jax import lax
from jax.experimental import pallas as pl
from jax.experimental.pallas import tpu as pltpu
from jax.sharding import PartitionSpec as P

HD = 64
REG = 4
STEP = 10
GROUP = 8
PIECES = 3
CHUNK = 16

norm_eps = 1e-06
clip_norm = 1.0
rate_matrix = 0.04
rate_vector = 0.2
decay_matrix = 0.04
moment_decay = 0.5
adam_eps = 1e-08

def square_sum(values):
    return jnp.sum(values * values)


def adam_step(weight, first, second, grad, rate, decay):
    first_new = moment_decay * first + (1.0 - moment_decay) * grad
    second_new = moment_decay * second + (1.0 - moment_decay) * grad * grad
    correct = 1.0 - moment_decay**STEP
    weight_new = weight - rate * (
        first_new / correct / (jnp.sqrt(second_new / correct) + adam_eps) + decay * weight
    )
    return (weight_new, first_new, second_new)


def nn(a, b):
    return lax.dot_general(a, b, (((1,), (0,)), ((), ())), preferred_element_type=jnp.float32)


def nt(a, b):
    return lax.dot_general(a, b, (((1,), (1,)), ((), ())), preferred_element_type=jnp.float32)


def tn(a, b):
    return lax.dot_general(a, b, (((0,), (0,)), ((), ())), preferred_element_type=jnp.float32)


def low(values):
    return values.astype(jnp.bfloat16)


def wide(values):
    return values.astype(jnp.float32)


def fold(values):
    return values[:8] + values[8:]


def remote(src, dst, send, recv, device):
    return pltpu.make_async_remote_copy(
        src_ref=src,
        dst_ref=dst,
        send_sem=send,
        recv_sem=recv,
        device_id=device,
        device_id_type=pl.DeviceIdType.MESH,
    )


def block_kernel(
    dims,
    pack,
    x_in,
    cot_in,
    mask_in,
    vec,
    bias_own,
    out_block,
    out_tokens,
    shard_out,
    sums_out,
    own_out,
    square_out,
    store,
    norm_one,
    turned_one,
    mixed,
    probs,
    context,
    attn_sum,
    middle,
    norm_two,
    turned_two,
    mlp_grad,
    turned_mlp,
    active,
    slope,
    wide_one,
    wide_two,
    grad_mid,
    attn_grad,
    turned_attn,
    gmixed,
    result,
    core_ring,
    diag_ring,
    dir_ring,
    line_in,
    bias_all,
    sums,
    sums_in,
    sums_z,
    tiles,
    tiles_in,
    tiles_z,
    z_send,
    z_recv,
    xy_send,
    xy_recv,
    diag_send,
    diag_recv,
    core_send,
    core_recv,
    rc_send,
    rc_recv,
    rd_send,
    rd_recv,
    rx_send,
    rx_recv,
    rz_send,
    rz_recv,
    ob_send,
    ob_recv,
    og_send,
    og_recv,
    own_sem,
    bs_send,
    bs_recv,
    vs_send,
    vs_recv,
    sq_send,
    sq_recv,
):
    n_dp, n_t, seq, pad_seq, crops, heads = dims
    stride = n_dp // GROUP
    rows = crops * pad_seq
    unit = pack.shape[1]
    half = unit // 2
    width = pack.shape[2]
    head_cols = heads * HD
    mix_cols = 3 * head_cols
    scale = HD ** (-0.5)
    n_chunks = rows // CHUNK

    d = lax.axis_index("dp")
    z = lax.axis_index("tensor")
    place = d // stride
    c = place % 2
    yx = place // 2
    xbit = yx % 2
    ybit = yx // 2
    yx_x = yx + 1 - 2 * xbit
    yx_y = yx + 2 - 4 * ybit
    yx_d = 3 - yx
    to_core = (d + (1 - 2 * c) * stride, z)
    to_x = (d + (1 - 2 * xbit) * 2 * stride, z)
    to_y = (d + (1 - 2 * ybit) * 4 * stride, z)

    def to_line(k):
        return (d, (z + k) % n_t)

    barrier = pltpu.get_barrier_semaphore()
    peers = [to_core, to_x, to_y] + [to_line(k) for k in range(1, n_t)]
    for peer in peers:
        pl.semaphore_signal(
            barrier, inc=1, device_id=peer, device_id_type=pl.DeviceIdType.MESH
        )
    pl.semaphore_wait(barrier, len(peers))

    def sum_copy(step, own, arrived, by_z, send, recv):
        if step < 3:
            return remote(
                own.at[step],
                arrived.at[step],
                send.at[step],
                recv.at[step],
                (to_core, to_x, to_y)[step],
            )
        k = step - 2
        return remote(own.at[3], by_z.at[z], send.at[step], recv.at[step], to_line(k))

    def sum_start(step, refs):
        if step < 3:
            sum_copy(step, *refs).start()
        else:
            own, arrived, by_z, send, recv = refs
            by_z[z] = own[3]
            for k in range(1, n_t):
                sum_copy(2 + k, *refs).start()

    def sum_finish(step, refs):
        own, arrived, by_z, send, recv = refs
        if step < 3:
            sum_copy(step, *refs).wait_recv()
            own[step + 1] = own[step] + arrived[step]
            return None
        for k in range(1, n_t):
            sum_copy(2 + k, *refs).wait_recv()
        total = by_z[0]
        for k in range(1, n_t):
            total = total + by_z[k]
        return total

    def sum_sent(refs):
        for step in range(3 + n_t - 1):
            sum_copy(step, *refs).wait_send()

    grad_sums = (sums, sums_in, sums_z, vs_send, vs_recv)
    square_sums = (tiles, tiles_in, tiles_z, sq_send, sq_recv)

    n_jobs = PIECES * n_t

    def z_copy(m, k):
        src = store.at[m, z, yx, c]
        return remote(src, src, z_send.at[m, k - 1], z_recv.at[m, k - 1], to_line(k))

    def block_at(i, which):
        m, k = i // n_t, i % n_t
        return store.at[m, (z + n_t - k) % n_t, which, c]

    def direct(i, axis):
        src = block_at(i, yx)
        return remote(
            src, src, xy_send.at[i, axis], xy_recv.at[i, axis], to_x if axis == 0 else to_y
        )

    def diagonal(i, axis):
        which = yx_x if axis == 1 else yx_y
        src = block_at(i, which).at[pl.ds(0 if axis == 1 else half, half)]
        return remote(
            src, src, diag_send.at[i, axis], diag_recv.at[i, axis], to_x if axis == 0 else to_y
        )

    def across(i, slot):
        src = block_at(i, (yx, yx_x, yx_y, yx_d)[slot])
        return remote(src, src, core_send.at[i, slot], core_recv.at[i, slot], to_core)

    def start_line(m):
        for k in range(1, n_t):
            z_copy(m, k).start()

    def gather_tick(i):
        @pl.when(jnp.logical_and(i >= 2, i - 2 < n_jobs))
        def _():
            j = jnp.maximum(i - 2, 0)
            diagonal(j, 0).wait_recv()
            diagonal(j, 1).wait_recv()
            across(j, 3).start()

        @pl.when(jnp.logical_and(i >= 1, i - 1 < n_jobs))
        def _():
            j = jnp.maximum(i - 1, 0)
            direct(j, 0).wait_recv()
            diagonal(j, 1).start()
            direct(j, 1).wait_recv()
            diagonal(j, 0).start()
            across(j, 1).start()
            across(j, 2).start()

        @pl.when(i < n_jobs)
        def _():
            j = jnp.minimum(i, n_jobs - 1)
            m, k = j // n_t, j % n_t

            @pl.when(k > 0)
            def _():
                z_copy(m, jnp.maximum(k, 1)).wait_recv()

            direct(j, 0).start()
            direct(j, 1).start()
            across(j, 0).start()

            @pl.when(jnp.logical_and(k == n_t - 1, m < PIECES - 1))
            def _():
                start_line(m + 1)

    def gather_end(m):
        def body(k, carry):
            for slot in range(4):
                across(m * n_t + k, slot).wait_recv()
            return carry

        lax.fori_loop(0, n_t, body, 0)

    def gather_sent(m):
        for k in range(1, n_t):
            z_copy(m, k).wait_send()

        def body(k, carry):
            i = m * n_t + k
            for axis in range(2):
                direct(i, axis).wait_send()
                diagonal(i, axis).wait_send()
            for slot in range(4):
                across(i, slot).wait_send()
            return carry

        lax.fori_loop(0, n_t, body, 0)

    def job_slot(j):
        return 3 - j // n_t, j % n_t

    def rs_core(j):
        slot, t = job_slot(j)
        return remote(
            store.at[slot, t, :, 1 - c],
            core_ring.at[j % 2],
            rc_send.at[j],
            rc_recv.at[j],
            to_core,
        )

    def rs_diag(j, axis):
        slot, t = job_slot(j)
        return remote(
            store.at[slot, t, yx_d, c, pl.ds(axis * half, half)],
            diag_ring.at[j % 2, axis],
            rd_send.at[j, axis],
            rd_recv.at[j, axis],
            to_x if axis == 0 else to_y,
        )

    def rs_direct(j, axis):
        slot, t = job_slot(j)
        return remote(
            store.at[slot, t, yx_x if axis == 0 else yx_y, c],
            dir_ring.at[j % 2, axis],
            rx_send.at[j, axis],
            rx_recv.at[j, axis],
            to_x if axis == 0 else to_y,
        )

    def rs_line_out(j):
        slot, t = job_slot(j)
        k = (z + n_t - t) % n_t
        m = PIECES - 1 - j // n_t
        return remote(
            store.at[slot, t, yx, c],
            line_in.at[m, jnp.maximum(k, 1) - 1],
            rz_send.at[j],
            rz_recv.at[m, jnp.maximum(k, 1) - 1],
            (d, t),
        )

    def rs_line_in(m, k):
        return remote(
            line_in.at[m, k - 1],
            line_in.at[m, k - 1],
            rz_send.at[0],
            rz_recv.at[m, k - 1],
            to_line(1),
        )

    def reduce_stage(stage, j):
        slot, t = job_slot(j)
        if stage == 0:
            rs_core(j).start()
        if stage == 1:
            rs_core(j).wait_recv()
            per = unit // CHUNK

            def body(s, carry):
                at = pl.ds(pl.multiple_of((s % per) * CHUNK, CHUNK), CHUNK)
                which = s // per
                store[slot, t, which, c, at] = low(
                    wide(store[slot, t, which, c, at]) + wide(core_ring[j % 2, which, at])
                )
                return carry

            lax.fori_loop(0, 4 * per, body, 0)
            rs_diag(j, 0).start()
            rs_diag(j, 1).start()
        if stage == 2:
            for axis in range(2):
                rs_diag(j, axis).wait_recv()
                which = yx_y if axis == 0 else yx_x
                at = pl.ds(axis * half, half)
                store[slot, t, which, c, at] = low(
                    wide(store[slot, t, which, c, at]) + wide(diag_ring[j % 2, axis])
                )
            rs_direct(j, 0).start()
            rs_direct(j, 1).start()
        if stage == 3:
            rs_direct(j, 0).wait_recv()
            rs_direct(j, 1).wait_recv()
            total = (
                wide(store[slot, t, yx, c])
                + wide(dir_ring[j % 2, 0])
                + wide(dir_ring[j % 2, 1])
            )

            @pl.when(t == z)
            def _():
                shard_out[PIECES - 1 - j // n_t] = total

            @pl.when(t != z)
            def _():
                store[slot, t, yx, c] = low(total)
                rs_line_out(j).start()

    def reduce_tick(i):
        for stage in (3, 2, 1, 0):

            @pl.when(jnp.logical_and(i >= stage, i - stage < n_jobs))
            def _():
                reduce_stage(stage, jnp.clip(i - stage, 0, n_jobs - 1))

    def line_step(s, out, send, recv, first_src):
        def up():
            shard = jnp.maximum(z - s + 1, 0)
            src = first_src if s == 1 else out.at[shard]
            return remote(src, out.at[shard], send.at[0, s - 1], recv.at[0, s - 1], to_line(1))

        def down():
            shard = jnp.minimum(z + s - 1, n_t - 1)
            src = first_src if s == 1 else out.at[shard]
            return remote(
                src, out.at[shard], send.at[1, s - 1], recv.at[1, s - 1], to_line(n_t - 1)
            )

        return up, down

    def line_start(s, out, send, recv, first_src):
        up, down = line_step(s, out, send, recv, first_src)

        @pl.when(jnp.logical_and(z - s + 1 >= 0, z < n_t - 1))
        def _():
            up().start()

        @pl.when(jnp.logical_and(z + s - 1 <= n_t - 1, z > 0))
        def _():
            down().start()

    def line_recv(s, out, send, recv, first_src):
        up, down = line_step(s, out, send, recv, first_src)

        @pl.when(z - s >= 0)
        def _():
            up().wait_recv()

        @pl.when(z + s <= n_t - 1)
        def _():
            down().wait_recv()

    def line_sent(s, out, send, recv, first_src):
        up, down = line_step(s, out, send, recv, first_src)

        @pl.when(jnp.logical_and(z - s + 1 >= 0, z < n_t - 1))
        def _():
            up().wait_send()

        @pl.when(jnp.logical_and(z + s - 1 <= n_t - 1, z > 0))
        def _():
            down().wait_send()

    line_block = (out_block, ob_send, ob_recv, result.at[0])
    line_tokens = (out_tokens, og_send, og_recv, result.at[1])

    for m in range(PIECES):
        store[m, z, yx, c] = pack[m]
    bias_all[z] = bias_own[...]

    def bias_copy(k):
        return remote(
            bias_own, bias_all.at[z], bs_send.at[k - 1], bs_recv.at[k - 1], to_line(k)
        )

    for k in range(1, n_t):
        bias_copy(k).start()
    start_line(0)
    gather_tick(0)
    sums[0] = jnp.zeros(sums.shape[1:], jnp.float32)

    def matrix(slot, t):
        return store[slot, t].reshape(GROUP * unit, width)

    def chunk_at(i):
        return pl.ds(pl.multiple_of(i * CHUNK, CHUNK), CHUNK)

    def start_of(at):
        chosen = mask_in[at, :] > 0.5
        return jnp.where(chosen, vec[8:9, :], wide(x_in[at, :])), chosen

    def normal(values):
        mean = jnp.mean(values, axis=-1, keepdims=True)
        centred = values - mean
        spread = jnp.mean(centred * centred, axis=-1, keepdims=True)
        rate = lax.rsqrt(spread + norm_eps)
        return centred * rate, rate

    def first_norm(i, total):
        at = chunk_at(i)
        begin, _ = start_of(at)
        hat, _ = normal(begin)
        norm_one[at, :] = low(hat * vec[0:1, :] + vec[1:2, :])
        cot = wide(cot_in[at, :])
        mlp_grad[at, :] = low(vec[6:7, :] * cot)
        return total + fold(cot)

    zero8 = jnp.zeros((8, width), jnp.float32)
    cot_total = lax.fori_loop(0, n_chunks, first_norm, zero8)
    sums[0, 7:8, :] = vec[6:7, :] * jnp.sum(cot_total, axis=0, keepdims=True)
    turned_one[...] = norm_one[...].T
    turned_mlp[...] = mlp_grad[...].T
    attn_sum[...] = jnp.zeros_like(attn_sum)

    def early(i, carry):
        gather_tick(i)
        return carry

    lax.fori_loop(1, n_t + 2, early, 0)
    gather_end(0)
    for k in range(1, n_t):
        bias_copy(k).wait_recv()

    key_ok = lax.broadcasted_iota(jnp.int32, (1, pad_seq), 1) < seq

    def attend(t, carry):
        mixed[t] = low(nn(norm_one[...], matrix(0, t)[:, :mix_cols]) + bias_all[t, 0:1, :mix_cols])

        def crop_body(b, inner):
            at = pl.ds(pl.multiple_of(b * pad_seq, CHUNK), pad_seq)
            mine = mixed[t, at, :]
            parts = []
            for h in range(heads):
                q = mine[:, h * HD : (h + 1) * HD]
                k = mine[:, head_cols + h * HD : head_cols + (h + 1) * HD]
                v = mine[:, 2 * head_cols + h * HD : 2 * head_cols + (h + 1) * HD]
                s = jnp.where(key_ok, nt(q, k) * scale, -1e30)
                e = jnp.exp(s - jnp.max(s, axis=-1, keepdims=True))
                p = low(e / jnp.sum(e, axis=-1, keepdims=True))
                probs[t, b, h] = p
                parts.append(low(nn(p, v)))
            context[t, at, :] = jnp.concatenate(parts, axis=1)
            return inner

        lax.fori_loop(0, crops, crop_body, 0)
        attn_sum[...] += nt(context[t], matrix(0, t)[:, mix_cols:])
        gather_tick(n_t + 2 + t)
        return carry

    lax.fori_loop(0, n_t, attend, 0)

    def second_norm(i, carry):
        at = chunk_at(i)
        begin, _ = start_of(at)
        mid = begin + vec[2:3, :] * (attn_sum[at, :] + vec[3:4, :])
        middle[at, :] = mid
        hat, _ = normal(mid)
        norm_two[at, :] = low(hat * vec[4:5, :] + vec[5:6, :])
        return carry

    lax.fori_loop(0, n_chunks, second_norm, 0)
    turned_two[...] = norm_two[...].T
    gather_end(1)

    def hidden_units(t, carry):
        wide_one[...] = nn(norm_two[...], matrix(1, t)) + bias_all[t, 1:2, :]

        def bend(i, inner):
            at = chunk_at(i)
            h = wide_one[at, :]
            cdf = 0.5 + 0.5 * lax.erf(h * 0.7071067811865476)
            active[t, at, :] = low(h * cdf)
            slope[t, at, :] = low(cdf + h * jnp.exp(-0.5 * h * h) * 0.3989422804014327)
            return inner

        lax.fori_loop(0, n_chunks, bend, 0)
        store[3, t] = low(nn(turned_mlp[...], active[t])).reshape(4, 2, unit, width)
        reduce_tick(t)
        gather_tick(2 * n_t + 2 + t)
        return carry

    lax.fori_loop(0, n_t, hidden_units, 0)
    gather_sent(1)
    gather_end(2)

    wide_one[...] = jnp.zeros_like(wide_one)

    def mlp_out(t, carry):
        wide_one[...] += nt(active[t], matrix(2, t))
        return carry

    lax.fori_loop(0, n_t, mlp_out, 0)

    def finish_block(i, total):
        at = chunk_at(i)
        mlp = wide_one[at, :] + vec[7:8, :]
        result[0, at, :] = low(middle[at, :] + vec[6:7, :] * mlp)
        return total + fold(wide(cot_in[at, :]) * mlp)

    mlp_total = lax.fori_loop(0, n_chunks, finish_block, zero8)
    sums[0, 6:7, :] = jnp.sum(mlp_total, axis=0, keepdims=True)
    line_start(1, *line_block)
    own_block = pltpu.make_async_copy(result.at[0], out_block.at[z], own_sem.at[0])
    own_block.start()
    gather_sent(2)

    wide_one[...] = jnp.zeros_like(wide_one)
    ones = jnp.ones((CHUNK, rows), jnp.bfloat16)

    def hidden_back(t, carry):
        wide_two[...] = nn(mlp_grad[...], matrix(2, t))

        def bend(i, inner):
            at = chunk_at(i)
            slope[t, at, :] = low(wide(slope[t, at, :]) * wide_two[at, :])
            return inner

        lax.fori_loop(0, n_chunks, bend, 0)
        sums[0, pl.ds(9 + n_t + t, 1), :] = nn(ones, slope[t])[:1]
        store[2, t] = low(nn(turned_two[...], slope[t])).reshape(4, 2, unit, width)
        wide_one[...] += nt(slope[t], matrix(1, t))
        reduce_tick(n_t + t)
        return carry

    lax.fori_loop(0, n_t, hidden_back, 0)
    line_recv(1, *line_block)
    line_start(2, *line_block)

    def second_back(i, totals):
        gain, shift, scale_one, bias_proj = totals
        at = chunk_at(i)
        upstream = wide_one[at, :]
        hat, rate = normal(middle[at, :])
        e = vec[4:5, :] * upstream
        inner = e - jnp.mean(e, axis=-1, keepdims=True)
        inner = inner - hat * jnp.mean(e * hat, axis=-1, keepdims=True)
        g = wide(cot_in[at, :]) + rate * inner
        grad_mid[at, :] = g
        attn_grad[at, :] = low(vec[2:3, :] * g)
        return (
            gain + fold(upstream * hat),
            shift + fold(upstream),
            scale_one + fold(g * (attn_sum[at, :] + vec[3:4, :])),
            bias_proj + fold(g),
        )

    gain, shift, scale_one, bias_proj = lax.fori_loop(0, n_chunks, second_back, (zero8,) * 4)
    sums[0, 4:5, :] = jnp.sum(gain, axis=0, keepdims=True)
    sums[0, 5:6, :] = jnp.sum(shift, axis=0, keepdims=True)
    sums[0, 2:3, :] = jnp.sum(scale_one, axis=0, keepdims=True)
    sums[0, 3:4, :] = vec[2:3, :] * jnp.sum(bias_proj, axis=0, keepdims=True)
    turned_attn[...] = attn_grad[...].T
    wide_one[...] = jnp.zeros_like(wide_one)

    def attend_back(t, carry):
        gctx = low(nn(attn_grad[...], matrix(0, t)[:, mix_cols:]))
        gmixed[:, :head_cols] = gctx

        def crop_body(b, inner):
            at = pl.ds(pl.multiple_of(b * pad_seq, CHUNK), pad_seq)
            mine = mixed[t, at, :]
            theirs = gmixed[at, :head_cols]
            gq, gk, gv = [], [], []
            for h in range(heads):
                q = mine[:, h * HD : (h + 1) * HD]
                k = mine[:, head_cols + h * HD : head_cols + (h + 1) * HD]
                v = mine[:, 2 * head_cols + h * HD : 2 * head_cols + (h + 1) * HD]
                g = theirs[:, h * HD : (h + 1) * HD]
                p_low = probs[t, b, h]
                p = wide(p_low)
                gp = nt(g, v)
                gs = low(p * (gp - jnp.sum(gp * p, axis=-1, keepdims=True)))
                gq.append(low(nn(gs, k) * scale))
                gk.append(low(tn(gs, q) * scale))
                gv.append(low(tn(p_low, g)))
            gmixed[at, :] = jnp.concatenate(gq + gk + gv, axis=1)
            return inner

        lax.fori_loop(0, crops, crop_body, 0)
        sums[0, pl.ds(9 + t, 1), :mix_cols] = nn(ones, gmixed[...])[:1]
        fresh = jnp.concatenate(
            [
                low(nn(turned_one[...], gmixed[...])),
                low(nn(turned_attn[...], context[t])),
            ],
            axis=1,
        )
        store[1, t] = fresh.reshape(4, 2, unit, width)
        wide_one[...] += nt(gmixed[...], matrix(0, t)[:, :mix_cols])
        reduce_tick(2 * n_t + t)
        return carry

    lax.fori_loop(0, n_t, attend_back, 0)
    line_recv(2, *line_block)
    line_start(3, *line_block)

    def first_back(i, totals):
        gain, shift, token = totals
        at = chunk_at(i)
        upstream = wide_one[at, :]
        begin, chosen = start_of(at)
        hat, rate = normal(begin)
        e = vec[0:1, :] * upstream
        inner = e - jnp.mean(e, axis=-1, keepdims=True)
        inner = inner - hat * jnp.mean(e * hat, axis=-1, keepdims=True)
        g = grad_mid[at, :] + rate * inner
        result[1, at, :] = low(jnp.where(chosen, 0.0, g))
        return (
            gain + fold(upstream * hat),
            shift + fold(upstream),
            token + fold(jnp.where(chosen, g, 0.0)),
        )

    gain, shift, token = lax.fori_loop(0, n_chunks, first_back, (zero8,) * 3)
    sums[0, 0:1, :] = jnp.sum(gain, axis=0, keepdims=True)
    sums[0, 1:2, :] = jnp.sum(shift, axis=0, keepdims=True)
    sums[0, 8:9, :] = jnp.sum(token, axis=0, keepdims=True)
    line_start(1, *line_tokens)
    own_tokens = pltpu.make_async_copy(result.at[1], out_tokens.at[z], own_sem.at[1])
    own_tokens.start()

    sum_start(0, grad_sums)
    for step in range(3):
        reduce_tick(n_jobs + step)
        sum_finish(step, grad_sums)
        sum_start(step + 1, grad_sums)
    for m in (2, 1, 0):
        for k in range(1, n_t):
            rs_line_in(m, k).wait_recv()
        total = shard_out[m]
        for k in range(1, n_t):
            total = total + wide(line_in[m, k - 1])
        shard_out[m] = total
    sums_out[...] = sum_finish(3, grad_sums)
    own_out[0:1, :] = sums_out[pl.ds(9 + z, 1), :]
    own_out[1:2, :] = sums_out[pl.ds(9 + n_t + z, 1), :]
    if stride == 1:
        first = jnp.where(d == 0, 1.0, 0.0)
        both = jnp.where(z == 0, first, 0.0)
        squares = first * square_sum(own_out[...]) + both * square_sum(sums_out[0:9, :])
        for m in range(PIECES):
            squares = squares + square_sum(shard_out[m])
        tiles[0] = jnp.full(tiles.shape[1:], 1.0, jnp.float32) * squares
        for step in range(4):
            sum_start(step, square_sums)
            total = sum_finish(step, square_sums)
        square_out[...] = total
        sum_sent(square_sums)
    else:
        square_out[...] = jnp.zeros_like(square_out)
    line_recv(1, *line_tokens)
    line_start(2, *line_tokens)
    line_recv(2, *line_tokens)
    line_start(3, *line_tokens)
    sum_sent(grad_sums)
    for k in range(1, n_t):
        bias_copy(k).wait_send()

    gather_sent(0)

    def sent(j, carry):
        rs_core(j).wait_send()
        for axis in range(2):
            rs_diag(j, axis).wait_send()
            rs_direct(j, axis).wait_send()

        @pl.when(j % n_t != z)
        def _():
            rs_line_out(j).wait_send()

        return carry

    lax.fori_loop(0, n_jobs, sent, 0)
    line_recv(3, *line_block)
    line_recv(3, *line_tokens)
    for s in (1, 2, 3):
        line_sent(s, *line_block)
        line_sent(s, *line_tokens)
    own_block.wait()
    own_tokens.wait()


def run_block(dims, pack, x_in, cot_in, mask_in, vec, bias_own):
    n_dp, n_t, seq, pad_seq, crops, heads = dims
    unit, width = pack.shape[1:]
    rows = crops * pad_seq
    head_cols = heads * HD
    mix_cols = 3 * head_cols
    n_jobs = PIECES * n_t
    n_sums = -(-(9 + 2 * n_t) // 8) * 8
    bf16, f32 = jnp.bfloat16, jnp.float32
    vmem = pltpu.VMEM
    dma = pltpu.SemaphoreType.DMA
    inside = pl.BlockSpec(memory_space=pltpu.VMEM)
    outside = pl.BlockSpec(memory_space=pl.ANY)
    return pl.pallas_call(
        functools.partial(block_kernel, dims),
        out_shape=(
            jax.ShapeDtypeStruct((n_t, rows, width), bf16),
            jax.ShapeDtypeStruct((n_t, rows, width), bf16),
            jax.ShapeDtypeStruct((PIECES, unit, width), f32),
            jax.ShapeDtypeStruct((n_sums, width), f32),
            jax.ShapeDtypeStruct((2, width), f32),
            jax.ShapeDtypeStruct((8, 128), f32),
        ),
        in_specs=[inside] * 6,
        out_specs=(outside, outside, inside, inside, inside, inside),
        scratch_shapes=[
            vmem((4, n_t, 4, 2, unit, width), bf16),
            vmem((rows, width), bf16),
            vmem((width, rows), bf16),
            vmem((n_t, rows, mix_cols), bf16),
            vmem((n_t, crops, heads, pad_seq, pad_seq), bf16),
            vmem((n_t, rows, head_cols), bf16),
            vmem((rows, width), f32),
            vmem((rows, width), f32),
            vmem((rows, width), bf16),
            vmem((width, rows), bf16),
            vmem((rows, width), bf16),
            vmem((width, rows), bf16),
            vmem((n_t, rows, width), bf16),
            vmem((n_t, rows, width), bf16),
            vmem((rows, width), f32),
            vmem((rows, width), f32),
            vmem((rows, width), f32),
            vmem((rows, width), bf16),
            vmem((width, rows), bf16),
            vmem((rows, mix_cols), bf16),
            vmem((2, rows, width), bf16),
            vmem((2, 4, unit, width), bf16),
            vmem((2, 2, unit // 2, width), bf16),
            vmem((2, 2, unit, width), bf16),
            vmem((PIECES, n_t - 1, unit, width), bf16),
            vmem((n_t, 8, width), f32),
            vmem((4, n_sums, width), f32),
            vmem((3, n_sums, width), f32),
            vmem((n_t, n_sums, width), f32),
            vmem((4, 8, 128), f32),
            vmem((3, 8, 128), f32),
            vmem((n_t, 8, 128), f32),
            dma((PIECES, n_t - 1)),
            dma((PIECES, n_t - 1)),
            dma((n_jobs, 2)),
            dma((n_jobs, 2)),
            dma((n_jobs, 2)),
            dma((n_jobs, 2)),
            dma((n_jobs, 4)),
            dma((n_jobs, 4)),
            dma((n_jobs,)),
            dma((n_jobs,)),
            dma((n_jobs, 2)),
            dma((n_jobs, 2)),
            dma((n_jobs, 2)),
            dma((n_jobs, 2)),
            dma((n_jobs,)),
            dma((PIECES, n_t - 1)),
            dma((2, n_t - 1)),
            dma((2, n_t - 1)),
            dma((2, n_t - 1)),
            dma((2, n_t - 1)),
            dma((2,)),
            dma((n_t - 1,)),
            dma((n_t - 1,)),
            dma((n_t + 2,)),
            dma((n_t + 2,)),
            dma((n_t + 2,)),
            dma((n_t + 2,)),
        ],
        compiler_params=pltpu.CompilerParams(
            collective_id=0, has_side_effects=True, vmem_limit_bytes=62 * 1024 * 1024
        ),
        name="block_step",
    )(pack, x_in, cot_in, mask_in, vec, bias_own)


def adam_kernel(*refs):
    shard, sums, own_sums, square_tile = refs[:4]
    states = [refs[4 + 3 * i : 7 + 3 * i] for i in range(7)]
    norm_out = refs[25]
    results = [refs[26 + 3 * i : 29 + 3 * i] for i in range(7)]
    copies = refs[47:51]
    norm = jnp.sqrt(square_tile[0:1, 0:1])
    norm_out[...] = jnp.broadcast_to(norm, norm_out.shape)
    factor = jnp.minimum(1.0, clip_norm / (norm + 1e-06))
    cols = states[0][0].shape[2]

    def update(i, grad, rate, decay, at=None):
        old = [ref[...] if at is None else ref[at] for ref in states[i]]
        fresh = adam_step(*old, factor * grad, rate, decay)
        for ref, value in zip(results[i], fresh):
            if at is None:
                ref[...] = value
            else:
                ref[at] = value
        if i < 4:
            if at is None:
                copies[i][...] = low(fresh[0])
            else:
                copies[i][at] = low(fresh[0])

    mixed = shard[0]
    for j in range(3):
        update(0, mixed[:, j * cols : (j + 1) * cols], rate_matrix, decay_matrix, j)
    update(1, mixed[:, 3 * cols :].T, rate_matrix, decay_matrix)
    update(2, shard[1], rate_matrix, decay_matrix)
    update(3, shard[2].T, rate_matrix, decay_matrix)
    update(4, sums[0:9, :], rate_vector, 0.0)
    mix = own_sums[0:1, :]
    heads = jnp.concatenate([mix[:, :cols], mix[:, 2 * cols : 3 * cols]], axis=0)
    update(5, heads, rate_vector, 0.0)
    update(6, own_sums[1:2, :], rate_vector, 0.0)


def run_adam(shard, sums, own_sums, square_tile, *states):
    flat = [array for state in states for array in state]
    like = [jax.ShapeDtypeStruct(array.shape, array.dtype) for array in flat]
    copies = [jax.ShapeDtypeStruct(state[0].shape, jnp.bfloat16) for state in states[:4]]
    inside = pl.BlockSpec(memory_space=pltpu.VMEM)
    out_shape = [jax.ShapeDtypeStruct((8, 128), jnp.float32)] + like + copies
    return pl.pallas_call(
        adam_kernel,
        out_shape=out_shape,
        in_specs=[inside] * (4 + len(flat)),
        out_specs=[inside] * len(out_shape),
        compiler_params=pltpu.CompilerParams(vmem_limit_bytes=48 * 1024 * 1024),
        name="adam_step",
    )(shard, sums, own_sums, square_tile, *flat)


def per_device(
    tokens,
    patch_mask,
    cotangent,
    qkv_weight,
    qkv_first,
    qkv_second,
    proj_weight,
    proj_first,
    proj_second,
    fc1_weight,
    fc1_first,
    fc1_second,
    fc2_weight,
    fc2_first,
    fc2_second,
    vectors,
    vectors_first,
    vectors_second,
    head_bias,
    head_bias_first,
    head_bias_second,
    fc1_bias,
    fc1_bias_first,
    fc1_bias_second,
):
    all_crops, seq, width = tokens.shape
    n_dp = lax.axis_size("dp")
    n_t = lax.axis_size("tensor")
    tensor_at = lax.axis_index("tensor")
    crops = all_crops // n_t
    head_cols = qkv_weight.shape[2]
    heads = head_cols // HD
    pad_seq = -(-seq // 16) * 16
    rows = crops * pad_seq
    stride = n_dp // GROUP

    def padded(array):
        here = lax.dynamic_slice_in_dim(array, tensor_at * crops, crops, 0)
        spare = [(0, 0), (0, pad_seq - seq), (0, 0)]
        return jnp.pad(here, spare).reshape(rows, -1)

    x_in = padded(tokens)
    cot_in = padded(cotangent)
    mask_all = jnp.pad(patch_mask, [(0, 0), (1 + REG, 0)]).astype(jnp.float32)
    mask_in = padded(mask_all[:, :, None])
    pack = jnp.stack(
        [
            jnp.concatenate(
                [qkv_weight[0], qkv_weight[1], qkv_weight[2], proj_weight.T], axis=1
            ),
            fc1_weight,
            fc2_weight.T,
        ]
    ).astype(jnp.bfloat16)
    if stride > 1:
        teams = [[b * stride + i for i in range(stride)] for b in range(GROUP)]
        pack = lax.all_gather(pack, "dp", axis_index_groups=teams, axis=1, tiled=True)
    mix_row = jnp.concatenate([head_bias[0], jnp.zeros((head_cols,), jnp.float32), head_bias[1]])
    mix_row = jnp.pad(mix_row, (0, width - 3 * head_cols))
    bias_own = jnp.pad(jnp.stack([mix_row, fc1_bias]), [(0, 6), (0, 0)])
    dims = (n_dp, n_t, seq, pad_seq, crops, heads)
    block_all, grad_all, shard, sums, own_sums, square_tile = run_block(
        dims, pack, x_in, cot_in, mask_in, vectors, bias_own
    )

    def whole(array):
        return array.reshape(all_crops, pad_seq, width)[:, :seq]

    block_out = whole(block_all)
    tokens_grad = whole(grad_all)
    if stride == 1:
        updated = run_adam(
            shard,
            sums,
            own_sums,
            square_tile,
            (qkv_weight, qkv_first, qkv_second),
            (proj_weight, proj_first, proj_second),
            (fc1_weight, fc1_first, fc1_second),
            (fc2_weight, fc2_first, fc2_second),
            (vectors, vectors_first, vectors_second),
            (head_bias, head_bias_first, head_bias_second),
            (fc1_bias[None], fc1_bias_first[None], fc1_bias_second[None]),
        )
        norm_tile = updated[0]
        updated = list(updated[1:])
        for at in (18, 19, 20):
            updated[at] = updated[at][0]
        return (block_out, tokens_grad, norm_tile[0, 0], *updated)
    both = ("dp", "tensor")
    shard = lax.psum_scatter(
        shard, "dp", scatter_dimension=1, axis_index_groups=teams, tiled=True
    )
    qkv_shard = jnp.stack([shard[0, :, i * head_cols : (i + 1) * head_cols] for i in range(3)])
    proj_shard = shard[0, :, 3 * head_cols :].T
    up_shard = shard[1]
    down_shard = shard[2].T
    sums, own_sums = lax.psum((sums, own_sums), "dp", axis_index_groups=teams)
    vector_sum = sums[:9]
    mix_here = own_sums[0]
    head_sum = jnp.stack([mix_here[:head_cols], mix_here[2 * head_cols : 3 * head_cols]])
    fc1b_sum = own_sums[1]
    first_data = (lax.axis_index("dp") == 0).astype(jnp.float32)
    first_tensor = (lax.axis_index("tensor") == 0).astype(jnp.float32)
    local_squares = (
        square_sum(qkv_shard)
        + square_sum(proj_shard)
        + square_sum(up_shard)
        + square_sum(down_shard)
    )
    local_squares = local_squares + first_data * (square_sum(head_sum) + square_sum(fc1b_sum))
    local_squares = local_squares + first_data * first_tensor * square_sum(vector_sum)
    total_squares = lax.psum(local_squares, ("dp", "tensor"))
    grad_norm = jnp.sqrt(total_squares)
    factor = jnp.minimum(1.0, clip_norm / (grad_norm + 1e-06))
    qkv_set = adam_step(
        qkv_weight, qkv_first, qkv_second, factor * qkv_shard, rate_matrix, decay_matrix
    )
    proj_set = adam_step(
        proj_weight, proj_first, proj_second, factor * proj_shard, rate_matrix, decay_matrix
    )
    fc1_set = adam_step(
        fc1_weight, fc1_first, fc1_second, factor * up_shard, rate_matrix, decay_matrix
    )
    fc2_set = adam_step(
        fc2_weight, fc2_first, fc2_second, factor * down_shard, rate_matrix, decay_matrix
    )
    vectors_set = adam_step(
        vectors, vectors_first, vectors_second, factor * vector_sum, rate_vector, 0.0
    )
    head_set = adam_step(
        head_bias, head_bias_first, head_bias_second, factor * head_sum, rate_vector, 0.0
    )
    fc1b_set = adam_step(
        fc1_bias, fc1_bias_first, fc1_bias_second, factor * fc1b_sum, rate_vector, 0.0
    )
    return (
        block_out,
        tokens_grad,
        grad_norm,
        qkv_set[0],
        qkv_set[1],
        qkv_set[2],
        proj_set[0],
        proj_set[1],
        proj_set[2],
        fc1_set[0],
        fc1_set[1],
        fc1_set[2],
        fc2_set[0],
        fc2_set[1],
        fc2_set[2],
        vectors_set[0],
        vectors_set[1],
        vectors_set[2],
        head_set[0],
        head_set[1],
        head_set[2],
        fc1b_set[0],
        fc1b_set[1],
        fc1b_set[2],
        qkv_set[0].astype(jnp.bfloat16),
        proj_set[0].astype(jnp.bfloat16),
        fc1_set[0].astype(jnp.bfloat16),
        fc2_set[0].astype(jnp.bfloat16),
    )


def solution(mesh):
    placed = (
        P("dp", None, None),
        P("dp", None),
        P("dp", None, None),
        P(None, "dp", "tensor"),
        P(None, "dp", "tensor"),
        P(None, "dp", "tensor"),
        P("tensor", "dp"),
        P("tensor", "dp"),
        P("tensor", "dp"),
        P("dp", "tensor"),
        P("dp", "tensor"),
        P("dp", "tensor"),
        P("tensor", "dp"),
        P("tensor", "dp"),
        P("tensor", "dp"),
        P(),
        P(),
        P(),
        P(None, "tensor"),
        P(None, "tensor"),
        P(None, "tensor"),
        P("tensor"),
        P("tensor"),
        P("tensor"),
    )
    return jax.shard_map(
        per_device,
        mesh=mesh,
        in_specs=placed,
        out_specs=(
            P("dp", None, None),
            P("dp", None, None),
            P(),
            P(None, "dp", "tensor"),
            P(None, "dp", "tensor"),
            P(None, "dp", "tensor"),
            P("tensor", "dp"),
            P("tensor", "dp"),
            P("tensor", "dp"),
            P("dp", "tensor"),
            P("dp", "tensor"),
            P("dp", "tensor"),
            P("tensor", "dp"),
            P("tensor", "dp"),
            P("tensor", "dp"),
            P(),
            P(),
            P(),
            P(None, "tensor"),
            P(None, "tensor"),
            P(None, "tensor"),
            P("tensor"),
            P("tensor"),
            P("tensor"),
            P(None, "dp", "tensor"),
            P("tensor", "dp"),
            P("dp", "tensor"),
            P("tensor", "dp"),
        ),
        check_vma=False,
    )
```

```python
import functools

import jax
import jax.numpy as jnp
from jax import lax
from jax.experimental import pallas as pl
from jax.experimental.pallas import tpu as pltpu
from jax.sharding import PartitionSpec as P

HD = 64
REG = 4
STEP = 10
GROUP = 8
LAG = 2
RING = 4

PIECES = 3
CHUNK = 32

norm_eps = 1e-06
clip_norm = 1.0
rate_matrix = 0.04
rate_vector = 0.2
decay_matrix = 0.04
moment_decay = 0.5
adam_eps = 1e-08

def square_sum(values):
    return jnp.sum(values * values)


def adam_step(weight, first, second, grad, rate, decay):
    first_new = moment_decay * first + (1.0 - moment_decay) * grad
    second_new = moment_decay * second + (1.0 - moment_decay) * grad * grad
    correct = 1.0 - moment_decay**STEP
    weight_new = weight - rate * (
        first_new / correct / (jnp.sqrt(second_new / correct) + adam_eps) + decay * weight
    )
    return (weight_new, first_new, second_new)


def nn(a, b):
    return lax.dot_general(a, b, (((1,), (0,)), ((), ())), preferred_element_type=jnp.float32)


def nt(a, b):
    return lax.dot_general(a, b, (((1,), (1,)), ((), ())), preferred_element_type=jnp.float32)


def tn(a, b):
    return lax.dot_general(a, b, (((0,), (0,)), ((), ())), preferred_element_type=jnp.float32)


def low(values):
    return values.astype(jnp.bfloat16)


def wide(values):
    return values.astype(jnp.float32)


def fold(values):
    return jnp.sum(values.reshape(-1, 8, values.shape[-1]), axis=0)


def remote(src, dst, send, recv, device):
    return pltpu.make_async_remote_copy(
        src_ref=src,
        dst_ref=dst,
        send_sem=send,
        recv_sem=recv,
        device_id=device,
        device_id_type=pl.DeviceIdType.MESH,
    )


def block_kernel(
    dims,
    pack,
    x_in,
    x_next,
    cot_in,
    mask_in,
    vec,
    bias_own,
    out_block,
    out_tokens,
    shard_out,
    sums_out,
    own_out,
    square_out,
    store,
    norm_one,
    turned_one,
    mixed,
    probs,
    context,
    attn_sum,
    middle,
    norm_two,
    mlp_grad,
    turned_mlp,
    wide_one,
    wide_two,
    result,
    core_ring,
    diag_ring,
    dir_ring,
    line_in,
    bias_all,
    sums,
    sums_in,
    sums_z,
    tiles,
    tiles_in,
    tiles_z,
    z_send,
    z_recv,
    xy_send,
    xy_recv,
    diag_send,
    diag_recv,
    core_send,
    core_recv,
    rc_send,
    rc_recv,
    rd_send,
    rd_recv,
    rx_send,
    rx_recv,
    rz_send,
    rz_recv,
    ob_send,
    ob_recv,
    og_send,
    og_recv,
    own_sem,
    bs_send,
    bs_recv,
    vs_send,
    vs_recv,
    sq_send,
    sq_recv,
):
    n_dp, n_t, seq, pad_seq, crops, heads = dims
    stride = n_dp // GROUP
    rows = crops * pad_seq
    unit = pack.shape[1]
    half = unit // 2
    width = pack.shape[2]
    head_cols = heads * HD
    mix_cols = 3 * head_cols
    scale = HD ** (-0.5)
    n_chunks = rows // CHUNK

    d = lax.axis_index("dp")
    z = lax.axis_index("tensor")
    place = d // stride
    c = place % 2
    yx = place // 2
    xbit = yx % 2
    ybit = yx // 2
    yx_x = yx + 1 - 2 * xbit
    yx_y = yx + 2 - 4 * ybit
    yx_d = 3 - yx
    to_core = (d + (1 - 2 * c) * stride, z)
    to_x = (d + (1 - 2 * xbit) * 2 * stride, z)
    to_y = (d + (1 - 2 * ybit) * 4 * stride, z)

    def to_line(k):
        return (d, (z + k) % n_t)

    barrier = pltpu.get_barrier_semaphore()
    def to_place(r):
        other = (
            c + (r % 2) * (1 - 2 * c)
            + 2 * (xbit + (r // 2 % 2) * (1 - 2 * xbit))
            + 4 * (ybit + (r // 4) * (1 - 2 * ybit))
        )
        return (d + (other - place) * stride, z)

    peers = [to_place(r) for r in range(1, GROUP)] + [to_line(k) for k in range(1, n_t)]
    for peer in peers:
        pl.semaphore_signal(
            barrier, inc=1, device_id=peer, device_id_type=pl.DeviceIdType.MESH
        )
    pl.semaphore_wait(barrier, len(peers))

    def sum_copy(step, own, arrived, by_z, send, recv):
        if step < 3:
            return remote(
                own.at[step],
                arrived.at[step],
                send.at[step],
                recv.at[step],
                (to_core, to_x, to_y)[step],
            )
        k = step - 2
        return remote(own.at[3], by_z.at[z], send.at[step], recv.at[step], to_line(k))

    def sum_start(step, refs):
        if step < 3:
            sum_copy(step, *refs).start()
        else:
            own, arrived, by_z, send, recv = refs
            by_z[z] = own[3]
            for k in range(1, n_t):
                sum_copy(2 + k, *refs).start()

    def sum_finish(step, refs):
        own, arrived, by_z, send, recv = refs
        if step < 3:
            sum_copy(step, *refs).wait_recv()
            own[step + 1] = own[step] + arrived[step]
            return None
        for k in range(1, n_t):
            sum_copy(2 + k, *refs).wait_recv()
        total = by_z[0]
        for k in range(1, n_t):
            total = total + by_z[k]
        return total

    def sum_sent(refs):
        for step in range(3 + n_t - 1):
            sum_copy(step, *refs).wait_send()

    grad_sums = (sums, sums_in, sums_z, vs_send, vs_recv)

    def tile_copy(i):
        if i < GROUP - 1:
            dst = tiles_in.at[place]
            return remote(tiles.at[0], dst, sq_send.at[i], sq_recv.at[i], to_place(i + 1))
        k = i - GROUP + 2
        return remote(tiles.at[1], tiles_z.at[z], sq_send.at[i], sq_recv.at[i], to_line(k))

    n_tiles = GROUP - 1 + n_t - 1

    n_jobs = PIECES * n_t

    def z_copy(m, k):
        src = store.at[m, z, yx, c]
        return remote(src, src, z_send.at[m, k - 1], z_recv.at[m, k - 1], to_line(k))

    def job_of(i):
        others = jnp.maximum(i - PIECES, 0)
        m = jnp.where(i < PIECES, i, others // (n_t - 1))
        return m, jnp.where(i < PIECES, 0, others % (n_t - 1) + 1)

    def job_at(m, k):
        return jnp.where(k == 0, m, PIECES + m * (n_t - 1) + k - 1)

    def block_at(i, which):
        m, k = job_of(i)
        return store.at[m, (z + n_t - k) % n_t, which, c]

    def direct(i, axis):
        src = block_at(i, yx)
        return remote(
            src, src, xy_send.at[i, axis], xy_recv.at[i, axis], to_x if axis == 0 else to_y
        )

    def diagonal(i, axis):
        which = yx_x if axis == 1 else yx_y
        src = block_at(i, which).at[pl.ds(0 if axis == 1 else half, half)]
        return remote(
            src, src, diag_send.at[i, axis], diag_recv.at[i, axis], to_x if axis == 0 else to_y
        )

    def across(i, slot):
        src = block_at(i, (yx, yx_x, yx_y, yx_d)[slot])
        return remote(src, src, core_send.at[i, slot], core_recv.at[i, slot], to_core)

    def start_line(m):
        for k in range(1, n_t):
            z_copy(m, k).start()

    def first_stage(i):
        m, k = job_of(i)

        @pl.when(k > 0)
        def _():
            z_copy(m, jnp.maximum(k, 1)).wait_recv()

        direct(i, 0).start()
        direct(i, 1).start()
        across(i, 0).start()

    def second_stage(i):
        direct(i, 0).wait_recv()
        diagonal(i, 1).start()
        direct(i, 1).wait_recv()
        diagonal(i, 0).start()
        across(i, 1).start()
        across(i, 2).start()

    def third_stage(i):
        diagonal(i, 0).wait_recv()
        diagonal(i, 1).wait_recv()
        across(i, 3).start()

    def gather_steps(text):
        for stage, i in text:
            {"a": first_stage, "b": second_stage, "c": third_stage, "z": start_line}[stage](i)

    def at_step(value, table):
        for key, text in table.items():

            @pl.when(value == key)
            def _():
                gather_steps(text)

    def gather_end(m):
        def body(k, carry):
            gather_part(m, k)
            return carry

        lax.fori_loop(0, n_t, body, 0)

    def gather_part(m, k):
        for slot in range(4):
            across(job_at(m, k), slot).wait_recv()

    def gather_sent(m):
        for k in range(1, n_t):
            z_copy(m, k).wait_send()

        def body(k, carry):
            i = job_at(m, k)
            for axis in range(2):
                direct(i, axis).wait_send()
                diagonal(i, axis).wait_send()
            for slot in range(4):
                across(i, slot).wait_send()
            return carry

        lax.fori_loop(0, n_t, body, 0)

    late_jobs = 3 * n_t + 2
    n_slots = late_jobs + 2 * n_t

    def late_group(i):
        return jnp.where(i % 2 == 0, i // 2, n_t - 1 - i // 2)

    def job_slot(j):
        early = j < 2 * n_t
        return (
            jnp.where(early, 3 + j % 2, 5),
            jnp.where(early, j // 2, late_group(jnp.maximum(j - late_jobs, 0) // 2)),
        )

    def ring_slot(j):
        return jnp.where(j < 2 * n_t, j % RING, jnp.maximum(j - late_jobs, 0) // 2 % 2)

    def job_valid(j):
        late = jnp.logical_and(j >= late_jobs, (j - late_jobs) % 2 == 0)
        busy = jnp.logical_or(j < 2 * n_t, late)
        return jnp.logical_and(busy, jnp.logical_and(j >= 0, j < n_slots))

    def rs_core(j):
        slot, t = job_slot(j)
        return remote(
            store.at[slot, t, :, 1 - c],
            core_ring.at[ring_slot(j)],
            rc_send.at[j],
            rc_recv.at[j],
            to_core,
        )

    def rs_diag(j, axis):
        slot, t = job_slot(j)
        return remote(
            store.at[slot, t, yx_d, c, pl.ds(axis * half, half)],
            diag_ring.at[ring_slot(j), axis],
            rd_send.at[j, axis],
            rd_recv.at[j, axis],
            to_x if axis == 0 else to_y,
        )

    def rs_direct(j, axis):
        slot, t = job_slot(j)
        return remote(
            store.at[slot, t, yx_x if axis == 0 else yx_y, c],
            dir_ring.at[ring_slot(j), axis],
            rx_send.at[j, axis],
            rx_recv.at[j, axis],
            to_x if axis == 0 else to_y,
        )

    def rs_line(slot, t, up):
        to = z + 1 if up else z - 1
        at = t if up else jnp.where(t == to, n_t, t)
        return remote(
            store.at[slot, t, yx, c],
            line_in.at[5 - slot, at],
            rz_send.at[5 - slot, t],
            rz_recv.at[5 - slot, at],
            to_line(1 if up else n_t - 1),
        )

    def rs_line_in(m, at):
        here = line_in.at[m, at]
        return remote(here, here, rz_send.at[m, 0], rz_recv.at[m, at], to_line(1))

    def reduce_stage(stage, j):
        slot, t = job_slot(j)
        if stage == 0:
            rs_core(j).start()
        if stage == 1:
            rs_core(j).wait_recv()
            per = unit // CHUNK

            def body(s, carry):
                at = pl.ds(pl.multiple_of((s % per) * CHUNK, CHUNK), CHUNK)
                which = s // per
                store[slot, t, which, c, at] = low(
                    wide(store[slot, t, which, c, at]) + wide(core_ring[ring_slot(j), which, at])
                )
                return carry

            lax.fori_loop(0, 4 * per, body, 0)
            rs_diag(j, 0).start()
            rs_diag(j, 1).start()
        if stage == 2:
            for axis in range(2):
                rs_diag(j, axis).wait_recv()
                which = yx_y if axis == 0 else yx_x
                at = pl.ds(axis * half, half)
                store[slot, t, which, c, at] = low(
                    wide(store[slot, t, which, c, at]) + wide(diag_ring[ring_slot(j), axis])
                )
            rs_direct(j, 0).start()
            rs_direct(j, 1).start()
        if stage == 3:
            rs_direct(j, 0).wait_recv()
            rs_direct(j, 1).wait_recv()
            total = (
                wide(store[slot, t, yx, c])
                + wide(dir_ring[ring_slot(j), 0])
                + wide(dir_ring[ring_slot(j), 1])
            )

            @pl.when(t == z)
            def _():
                shard_out[5 - slot] = total

            @pl.when(t != z)
            def _():
                store[slot, t, yx, c] = low(total)

        if stage >= 3:
            hop = stage - 3
            for up in (True, False):
                here = z == (hop if up else n_t - 1 - hop)

                @pl.when(jnp.logical_and(here, t > z if up else t < z))
                def _():
                    if hop > 0:
                        rs_line_in(5 - slot, t).wait_recv()
                        store[slot, t, yx, c] = low(
                            wide(store[slot, t, yx, c]) + wide(line_in[5 - slot, t])
                        )
                    rs_line(slot, t, up).start()

    def reduce_tick(i):
        for stage in range(n_t + 1, -1, -1):

            @pl.when(job_valid(i - stage * LAG))
            def _():
                reduce_stage(stage, jnp.clip(i - stage * LAG, 0, n_slots - 1))

    def line_copy(q, up, out, send, recv, first_src):
        s, b = q // crops + 1, q % crops
        shard = jnp.maximum(z - s + 1, 0) if up else jnp.minimum(z + s - 1, n_t - 1)
        at = pl.ds(b * pad_seq, pad_seq)
        src = first_src.at[at] if s == 1 else out.at[shard, at]
        way = 0 if up else 1
        return remote(
            src,
            out.at[shard, at],
            send.at[way, q],
            recv.at[way, q],
            to_line(1 if up else n_t - 1),
        )

    def line_go(q, action, refs):
        s = q // crops + 1
        skip = refs is line_block and s == 1
        sends = action != "wait_recv"
        for up in (True, False):
            if up:
                ok = jnp.logical_and(z - s + 1 >= 0, z < n_t - 1) if sends else z - s >= 0
                if skip:
                    ok = jnp.logical_and(ok, z != (n_t - 2 if sends else n_t - 1))
            else:
                ok = jnp.logical_and(z + s - 1 <= n_t - 1, z > 0) if sends else z + s <= n_t - 1
                if skip:
                    ok = jnp.logical_and(ok, z != (1 if sends else 0))

            @pl.when(ok)
            def _():
                copy = line_copy(q, up, *refs)
                if action == "start":
                    copy.start()
                elif action == "wait_send":
                    copy.wait_send()
                else:
                    copy.wait_recv()

    n_hops = crops * (n_t - 1)

    def line_begin(refs):
        for q in range(crops):
            line_go(q, "start", refs)

    def line_forward(q, refs):
        line_go(q, "wait_recv", refs)
        if q + crops < n_hops:
            line_go(q + crops, "start", refs)

    def line_end(refs, begin=0):
        for q in range(begin, n_hops):
            line_go(q, "wait_send", refs)

    line_block = (out_block, ob_send, ob_recv, result.at[0])
    line_tokens = (out_tokens, og_send, og_recv, result.at[1])

    for m in range(PIECES):
        store[m, z, yx, c] = pack[m]
    bias_all[z] = bias_own[...]

    def bias_copy(k):
        return remote(
            bias_own, bias_all.at[z], bs_send.at[k - 1], bs_recv.at[k - 1], to_line(k)
        )

    for k in range(1, n_t):
        bias_copy(k).start()
    gather_steps((("z", 0), ("a", 0), ("a", 1), ("a", 2),))
    sums[0] = jnp.zeros(sums.shape[1:], jnp.float32)

    def matrix(slot, t):
        return store[slot, t].reshape(GROUP * unit, width)

    def active_of(t):
        return store[4, t].reshape(GROUP * unit, width)[:rows]

    def slope_of(t):
        return store[5, t].reshape(GROUP * unit, width)[:rows]

    per_unit = unit // CHUNK

    def spot(i):
        block = i // per_unit
        at = pl.ds(pl.multiple_of((i % per_unit) * CHUNK, CHUNK), CHUNK)
        return block // 2, block % 2, at

    def chunk_at(i):
        return pl.ds(pl.multiple_of(i * CHUNK, CHUNK), CHUNK)

    def start_of(at, extra=False):
        chosen = mask_in[at, 1:2] > 0.5 if extra else mask_in[at, 0:1] > 0.5
        source = mlp_grad if extra else x_in
        return jnp.where(chosen, vec[8:9, :], wide(source[at, :])), chosen

    def normal(values):
        mean = jnp.mean(values, axis=-1, keepdims=True)
        centred = values - mean
        spread = jnp.mean(centred * centred, axis=-1, keepdims=True)
        rate = lax.rsqrt(spread + norm_eps)
        return centred * rate, rate

    def first_norm(i, carry, extra=False):
        at = chunk_at(i)
        begin, _ = start_of(at, extra)
        hat, _ = normal(begin)
        norm_one[at, :] = low(hat * vec[0:1, :] + vec[1:2, :])
        return carry

    zero8 = jnp.zeros((8, width), jnp.float32)
    attn_sum[...] = jnp.zeros_like(attn_sum)

    def early(i, carry):
        lax.fori_loop(i * n_chunks // 3, (i + 1) * n_chunks // 3, first_norm, 0)
        at_step(i, {0: (("b", 0),), 1: (("z", 1), ("b", 1),), 2: (("b", 2), ("c", 0), ("c", 1), ("c", 2),)})
        return carry

    lax.fori_loop(0, 3, early, 0)
    gather_steps((("a", 3), ("a", 4), ("a", 5), ("z", 2),))
    for k in range(1, n_t):
        bias_copy(k).wait_recv()

    key_ok = lax.broadcasted_iota(jnp.int32, (1, pad_seq), 1) < seq

    def attend(t, extra=False):
        mixed[t] = low(nn(norm_one[...], matrix(0, t)[:, :mix_cols]) + bias_all[t, 0:1, :mix_cols])

        def crop_body(b, inner):
            at = pl.ds(pl.multiple_of(b * pad_seq, 16), pad_seq)
            mine = mixed[t, at, :]
            parts = []
            for h in range(heads):
                q = mine[:, h * HD : (h + 1) * HD]
                k = mine[:, head_cols + h * HD : head_cols + (h + 1) * HD]
                v = mine[:, 2 * head_cols + h * HD : 2 * head_cols + (h + 1) * HD]
                s = jnp.where(key_ok, nt(q, k) * scale, -1e30)
                e = jnp.exp(s - jnp.max(s, axis=-1, keepdims=True))
                p = low(e / jnp.sum(e, axis=-1, keepdims=True))
                if not extra:
                    probs[t, b, h] = p
                parts.append(low(nn(p, v)))
            context[t, at, :] = jnp.concatenate(parts, axis=1)
            return inner

        lax.fori_loop(0, crops, crop_body, 0)
        attn_sum[...] += nt(context[t], matrix(0, t)[:, mix_cols:])

    def attend_step(k, carry):
        at_step(k, {1: (("b", 3), ("b", 4), ("c", 3), ("b", 5),), 2: (("c", 4), ("a", 6), ("a", 7), ("a", 8),), 3: (("c", 5), ("b", 6), ("b", 7),)})
        gather_part(0, k)
        attend((z + n_t - k) % n_t)
        return carry

    lax.fori_loop(0, n_t, attend_step, 0)

    def second_norm(i, carry, extra=False):
        at = chunk_at(i)
        begin, _ = start_of(at, extra)
        mid = begin + vec[2:3, :] * (attn_sum[at, :] + vec[3:4, :])
        middle[at, :] = mid
        hat, _ = normal(mid)
        norm_two[at, :] = low(hat * vec[4:5, :] + vec[5:6, :])
        return carry

    gather_steps((("b", 8), ("c", 6), ("a", 9), ("a", 10), ("a", 11),))
    lax.fori_loop(0, n_chunks, second_norm, 0)
    gather_steps((("c", 7), ("c", 8), ("b", 9),))
    gather_end(1)

    def hidden_units(t, carry):
        wide_one[...] = nn(norm_two[...], matrix(1, t)) + bias_all[t, 1:2, :]

        def bend(i, inner):
            at = chunk_at(i)
            h = wide_one[at, :]
            cdf = 0.5 + 0.5 * lax.erf(h * 0.7071067811865476)
            a, b, within = spot(i)
            store[4, t, a, b, within] = low(h * cdf)
            store[5, t, a, b, within] = low(cdf + h * jnp.exp(-0.5 * h * h) * 0.3989422804014327)
            return inner

        lax.fori_loop(0, n_chunks, bend, 0)
        at_step(t, {0: (("b", 10), ("b", 11), ("c", 9),), 1: (("c", 10),), 2: (("c", 11),)})
        return carry

    lax.fori_loop(0, n_t, hidden_units, 0)

    wide_one[...] = jnp.zeros_like(wide_one)

    def mlp_out(k, carry):
        gather_part(2, k)
        t = (z + n_t - k) % n_t
        wide_one[...] += nt(active_of(t), matrix(2, t))
        return carry

    lax.fori_loop(0, n_t, mlp_out, 0)

    def finish_block(i, total):
        at = chunk_at(i)
        mlp = wide_one[at, :] + vec[7:8, :]
        result[0, at, :] = low(middle[at, :] + vec[6:7, :] * mlp)
        return total + fold(wide(cot_in[at, :]) * mlp)

    mlp_total = lax.fori_loop(0, n_chunks, finish_block, zero8)
    sums[0, 6:7, :] = jnp.sum(mlp_total, axis=0, keepdims=True)
    line_begin(line_block)
    own_block = pltpu.make_async_copy(result.at[0], out_block.at[z], own_sem.at[0])
    own_block.start()

    turned_one[...] = norm_two[...].T

    def scale_cot(i, total):
        at = chunk_at(i)
        cot = wide(cot_in[at, :])
        mlp_grad[at, :] = low(vec[6:7, :] * cot)
        return total + fold(cot)

    cot_total = lax.fori_loop(0, n_chunks, scale_cot, zero8)
    sums[0, 7:8, :] = vec[6:7, :] * jnp.sum(cot_total, axis=0, keepdims=True)
    turned_mlp[...] = mlp_grad[...].T
    wide_one[...] = jnp.zeros_like(wide_one)
    ones = jnp.ones((CHUNK, rows), jnp.bfloat16)

    def hidden_back(t, carry):
        store[3, t] = low(nn(turned_mlp[...], active_of(t))).reshape(4, 2, unit, width)
        reduce_tick(2 * t)
        wide_two[...] = nn(mlp_grad[...], matrix(2, t))

        def bend(i, inner):
            at = chunk_at(i)
            a, b, within = spot(i)
            store[5, t, a, b, within] = low(wide(store[5, t, a, b, within]) * wide_two[at, :])
            return inner

        lax.fori_loop(0, n_chunks, bend, 0)
        bent = slope_of(t)
        sums[0, pl.ds(9 + n_t + t, 1), :] = nn(ones, bent)[:1]
        store[4, t] = low(nn(turned_one[...], bent)).reshape(4, 2, unit, width)
        wide_one[...] += nt(bent, matrix(1, t))
        reduce_tick(2 * t + 1)

        @pl.when(t == 1)
        def _():
            line_forward(0, line_block)

        return carry

    lax.fori_loop(0, n_t, hidden_back, 0)
    reduce_tick(2 * n_t)
    next_copy = pltpu.make_async_copy(x_next, mlp_grad, own_sem.at[2])
    next_copy.start()
    turned_one[...] = norm_one[...].T

    def second_back(i, totals):
        gain, shift, scale_one, bias_proj = totals
        at = chunk_at(i)
        upstream = wide_one[at, :]
        hat, rate = normal(middle[at, :])
        e = vec[4:5, :] * upstream
        inner = e - jnp.mean(e, axis=-1, keepdims=True)
        inner = inner - hat * jnp.mean(e * hat, axis=-1, keepdims=True)
        g = wide(cot_in[at, :]) + rate * inner
        wide_two[at, :] = g
        norm_two[at, :] = low(vec[2:3, :] * g)
        return (
            gain + fold(upstream * hat),
            shift + fold(upstream),
            scale_one + fold(g * (attn_sum[at, :] + vec[3:4, :])),
            bias_proj + fold(g),
        )

    gain, shift, scale_one, bias_proj = lax.fori_loop(0, n_chunks, second_back, (zero8,) * 4)
    sums[0, 4:5, :] = jnp.sum(gain, axis=0, keepdims=True)
    sums[0, 5:6, :] = jnp.sum(shift, axis=0, keepdims=True)
    sums[0, 2:3, :] = jnp.sum(scale_one, axis=0, keepdims=True)
    sums[0, 3:4, :] = vec[2:3, :] * jnp.sum(bias_proj, axis=0, keepdims=True)
    reduce_tick(2 * n_t + 1)
    turned_mlp[...] = norm_two[...].T
    line_forward(1, line_block)
    wide_one[...] = jnp.zeros_like(wide_one)

    def attend_back(i, carry):
        b, turn = i // n_t, i % n_t
        t = late_group(turn)
        at = pl.ds(pl.multiple_of(b * pad_seq, 16), pad_seq)
        theirs = low(nn(norm_two[at, :], matrix(0, t)[:, mix_cols:]))
        mine = mixed[t, at, :]
        gq, gk, gv = [], [], []
        for h in range(heads):
            q = mine[:, h * HD : (h + 1) * HD]
            k = mine[:, head_cols + h * HD : head_cols + (h + 1) * HD]
            v = mine[:, 2 * head_cols + h * HD : 2 * head_cols + (h + 1) * HD]
            g = theirs[:, h * HD : (h + 1) * HD]
            p_low = probs[t, b, h]
            p = wide(p_low)
            gp = nt(g, v)
            gs = low(p * (gp - jnp.sum(gp * p, axis=-1, keepdims=True)))
            gq.append(low(nn(gs, k) * scale))
            gk.append(low(tn(gs, q) * scale))
            gv.append(low(tn(p_low, g)))
        fresh = jnp.concatenate(gq + gk + gv, axis=1)
        mixed[t, at, :] = fresh
        wide_one[at, :] += nt(fresh, matrix(0, t)[:, :mix_cols])

        @pl.when(b == 0)
        def _():
            reduce_tick(2 * n_t + 2 + turn)

        @pl.when(b == 1)
        def _():
            sums[0, pl.ds(9 + t, 1), :mix_cols] = nn(ones, mixed[t])[:1]
            grads = jnp.concatenate(
                [
                    low(nn(turned_one[...], mixed[t])),
                    low(nn(turned_mlp[...], context[t])),
                ],
                axis=1,
            )
            store[5, t] = grads.reshape(4, 2, unit, width)
            reduce_tick(late_jobs + 2 * turn)
            reduce_tick(late_jobs + 2 * turn + 1)

        for key, (q, refs) in {
            1: (2, line_block),
            3: (3, line_block),
            5: (4, line_block),
            6: (0, line_tokens),
        }.items():

            @pl.when(i == key)
            def _():
                line_forward(q, refs)

        @pl.when(turn == n_t - 1)
        def _():
            start_back(b)

        return carry

    def first_back(at, totals):
        gain, shift, token = totals
        upstream = wide_one[at, :]
        begin, chosen = start_of(at)
        hat, rate = normal(begin)
        e = vec[0:1, :] * upstream
        inner = e - jnp.mean(e, axis=-1, keepdims=True)
        inner = inner - hat * jnp.mean(e * hat, axis=-1, keepdims=True)
        g = wide_two[at, :] + rate * inner
        result[1, at, :] = low(jnp.where(chosen, 0.0, g))
        return (
            gain + fold(upstream * hat),
            shift + fold(upstream),
            token + fold(jnp.where(chosen, g, 0.0)),
        )

    def start_back(b):
        base = b * pad_seq
        full = pad_seq // CHUNK

        def body(i, totals):
            at = pl.ds(pl.multiple_of(base + i * CHUNK, 16), CHUNK)
            return first_back(at, totals)

        totals = lax.fori_loop(0, full, body, (zero8,) * 3)
        if pad_seq % CHUNK:
            at = pl.ds(pl.multiple_of(base + full * CHUNK, 16), pad_seq % CHUNK)
            totals = first_back(at, totals)
        for row, total in zip((0, 1, 8), totals):
            sums[0, row : row + 1, :] += jnp.sum(total, axis=0, keepdims=True)
        for q in range(crops):

            @pl.when(b == q)
            def _():
                line_go(q, "start", line_tokens)

    lax.fori_loop(0, crops * n_t, attend_back, 0)
    own_tokens = pltpu.make_async_copy(result.at[1], out_tokens.at[z], own_sem.at[1])
    own_tokens.start()

    sum_start(0, grad_sums)
    next_copy.wait()
    at_end = jnp.logical_or(z == 0, z == n_t - 1)
    beside = jnp.where(z == 0, 1, n_t - 2)

    @pl.when(at_end)
    def _():
        lax.fori_loop(0, n_chunks, functools.partial(first_norm, extra=True), 0)
        attn_sum[...] = jnp.zeros_like(attn_sum)

    reduce_tick(n_slots)
    sum_finish(0, grad_sums)
    sum_start(1, grad_sums)

    def attend_more(t, carry):
        @pl.when(at_end)
        def _():
            attend((beside + n_t - t) % n_t, extra=True)

        reduce_tick(n_slots + 1 + t)

        @pl.when(t == 0)
        def _():
            line_forward(2, line_tokens)

        @pl.when(t == 1)
        def _():
            sum_finish(1, grad_sums)
            sum_start(2, grad_sums)

        @pl.when(t == 2)
        def _():
            line_forward(1, line_tokens)

        @pl.when(t == 3)
        def _():
            sum_finish(2, grad_sums)
            sum_start(3, grad_sums)

        return carry

    lax.fori_loop(0, n_t, attend_more, 0)
    reduce_tick(n_slots + n_t + 1)

    @pl.when(at_end)
    def _():
        lax.fori_loop(0, n_chunks, functools.partial(second_norm, extra=True), 0)
        wide_two[...] = jnp.zeros_like(wide_two)

    reduce_tick(n_slots + n_t + 2)

    def hidden_more(k, carry):
        t = (beside + n_t - k) % n_t

        @pl.when(at_end)
        def _():
            wide_one[...] = nn(norm_two[...], matrix(1, t)) + bias_all[t, 1:2, :]

            def bend(i, inner):
                at = chunk_at(i)
                h = wide_one[at, :]
                mlp_grad[at, :] = low(h * (0.5 + 0.5 * lax.erf(h * 0.7071067811865476)))
                return inner

            lax.fori_loop(0, n_chunks, bend, 0)
            wide_two[...] += nt(mlp_grad[...], matrix(2, t))

        reduce_tick(n_slots + n_t + 3 + k)

        @pl.when(k == 0)
        def _():
            line_forward(3, line_tokens)

        return carry

    lax.fori_loop(0, n_t, hidden_more, 0)
    for step in range(2 * n_t + 3, LAG * (n_t + 1)):
        reduce_tick(n_slots + step)
    line_forward(n_hops - 1, line_block)
    for q in range(crops):
        line_go(q, "wait_send", line_block)
    own_block.wait()
    more_block = pltpu.make_async_copy(result.at[0], out_block.at[beside], own_sem.at[0])

    @pl.when(at_end)
    def _():
        def finish_more(i, carry):
            at = chunk_at(i)
            mlp = wide_two[at, :] + vec[7:8, :]
            result[0, at, :] = low(middle[at, :] + vec[6:7, :] * mlp)
            return carry

        lax.fori_loop(0, n_chunks, finish_more, 0)
        more_block.start()

    @pl.when(z > 0)
    def _():
        for m in range(PIECES):
            rs_line_in(m, z).wait_recv()
            shard_out[m] = shard_out[m] + wide(line_in[m, z])

    @pl.when(z < n_t - 1)
    def _():
        for m in range(PIECES):
            rs_line_in(m, n_t).wait_recv()
            shard_out[m] = shard_out[m] + wide(line_in[m, n_t])

    sums_out[...] = sum_finish(3, grad_sums)
    own_out[0:1, :] = sums_out[pl.ds(9 + z, 1), :]
    own_out[1:2, :] = sums_out[pl.ds(9 + n_t + z, 1), :]
    if stride == 1:
        first = jnp.where(d == 0, 1.0, 0.0)
        both = jnp.where(z == 0, first, 0.0)
        squares = first * square_sum(own_out[...]) + both * square_sum(sums_out[0:9, :])
        for m in range(PIECES):
            squares = squares + square_sum(shard_out[m])
        tiles[0] = jnp.full(tiles.shape[1:], 1.0, jnp.float32) * squares
        tiles_in[place] = tiles[0]
        for i in range(GROUP - 1):
            tile_copy(i).start()
        for i in range(GROUP - 1):
            tile_copy(i).wait_recv()
        total = tiles_in[0]
        for i in range(1, GROUP):
            total = total + tiles_in[i]
        tiles[1] = total
        tiles_z[z] = total
        for i in range(GROUP - 1, n_tiles):
            tile_copy(i).start()
        for i in range(GROUP - 1, n_tiles):
            tile_copy(i).wait_recv()
        total = tiles_z[0]
        for k in range(1, n_t):
            total = total + tiles_z[k]
        square_out[...] = total
        for i in range(n_tiles):
            tile_copy(i).wait_send()
    else:
        square_out[...] = jnp.zeros_like(square_out)
    for q in range(4, n_hops):
        line_forward(q, line_tokens)
    sum_sent(grad_sums)
    for k in range(1, n_t):
        bias_copy(k).wait_send()

    for m in range(PIECES):
        gather_sent(m)

    def sent(j, carry):
        rs_core(j).wait_send()
        for axis in range(2):
            rs_diag(j, axis).wait_send()
            rs_direct(j, axis).wait_send()

        slot, t = job_slot(j)

        @pl.when(t > z)
        def _():
            rs_line(slot, t, True).wait_send()

        @pl.when(t < z)
        def _():
            rs_line(slot, t, False).wait_send()

        return carry

    lax.fori_loop(0, 2 * n_t, sent, 0)
    lax.fori_loop(0, n_t, lambda t, carry: sent(late_jobs + 2 * t, carry), 0)
    line_end(line_block, crops)
    line_end(line_tokens)

    @pl.when(at_end)
    def _():
        more_block.wait()

    own_tokens.wait()


def run_block(dims, pack, x_in, x_next, cot_in, mask_in, vec, bias_own):
    n_dp, n_t, seq, pad_seq, crops, heads = dims
    unit, width = pack.shape[1:]
    rows = crops * pad_seq
    head_cols = heads * HD
    mix_cols = 3 * head_cols
    n_jobs = PIECES * n_t
    n_sums = -(-(9 + 2 * n_t) // 8) * 8
    bf16, f32 = jnp.bfloat16, jnp.float32
    vmem = pltpu.VMEM
    dma = pltpu.SemaphoreType.DMA
    inside = pl.BlockSpec(memory_space=pltpu.VMEM)
    outside = pl.BlockSpec(memory_space=pl.ANY)
    return pl.pallas_call(
        functools.partial(block_kernel, dims),
        out_shape=(
            jax.ShapeDtypeStruct((n_t, rows, width), bf16),
            jax.ShapeDtypeStruct((n_t, rows, width), bf16),
            jax.ShapeDtypeStruct((PIECES, unit, width), f32),
            jax.ShapeDtypeStruct((n_sums, width), f32),
            jax.ShapeDtypeStruct((2, width), f32),
            jax.ShapeDtypeStruct((8, 128), f32),
        ),
        in_specs=[inside, inside, outside, inside, inside, inside, inside],
        out_specs=(outside, outside, inside, inside, inside, inside),
        scratch_shapes=[
            vmem((6, n_t, 4, 2, unit, width), bf16),
            vmem((rows, width), bf16),
            vmem((width, rows), bf16),
            vmem((n_t, rows, mix_cols), bf16),
            vmem((n_t, crops, heads, pad_seq, pad_seq), bf16),
            vmem((n_t, rows, head_cols), bf16),
            vmem((rows, width), f32),
            vmem((rows, width), f32),
            vmem((rows, width), bf16),
            vmem((rows, width), bf16),
            vmem((width, rows), bf16),
            vmem((rows, width), f32),
            vmem((rows, width), f32),
            vmem((2, rows, width), bf16),
            vmem((RING, 4, unit, width), bf16),
            vmem((RING, 2, unit // 2, width), bf16),
            vmem((RING, 2, unit, width), bf16),
            vmem((PIECES, n_t + 1, unit, width), bf16),
            vmem((n_t, 8, width), f32),
            vmem((4, n_sums, width), f32),
            vmem((3, n_sums, width), f32),
            vmem((n_t, n_sums, width), f32),
            vmem((2, 8, 128), f32),
            vmem((GROUP, 8, 128), f32),
            vmem((n_t, 8, 128), f32),
            dma((PIECES, n_t - 1)),
            dma((PIECES, n_t - 1)),
            dma((n_jobs, 2)),
            dma((n_jobs, 2)),
            dma((n_jobs, 2)),
            dma((n_jobs, 2)),
            dma((n_jobs, 4)),
            dma((n_jobs, 4)),
            dma((5 * n_t + 2,)),
            dma((5 * n_t + 2,)),
            dma((5 * n_t + 2, 2)),
            dma((5 * n_t + 2, 2)),
            dma((5 * n_t + 2, 2)),
            dma((5 * n_t + 2, 2)),
            dma((PIECES, n_t)),
            dma((PIECES, n_t + 1)),
            dma((2, crops * (n_t - 1))),
            dma((2, crops * (n_t - 1))),
            dma((2, crops * (n_t - 1))),
            dma((2, crops * (n_t - 1))),
            dma((3,)),
            dma((n_t - 1,)),
            dma((n_t - 1,)),
            dma((n_t + 2,)),
            dma((n_t + 2,)),
            dma((GROUP + n_t - 2,)),
            dma((GROUP + n_t - 2,)),
        ],
        compiler_params=pltpu.CompilerParams(
            collective_id=0, has_side_effects=True, vmem_limit_bytes=63 * 1024 * 1024
        ),
        name="block_step",
    )(pack, x_in, x_next, cot_in, mask_in, vec, bias_own)


def prepare_kernel(
    dims,
    tokens,
    cot,
    mask,
    qkv,
    proj,
    up,
    down,
    head_bias,
    up_bias,
    x_in,
    x_next,
    cot_in,
    mask_in,
    pack,
    bias_own,
    landing,
    sems,
):
    n_dp, n_t, seq, pad_seq, crops, heads = dims
    z = lax.axis_index("tensor")
    mine = z * crops
    other = jnp.where(z == 0, 1, n_t - 2) * crops
    copies = []
    for source, base in ((tokens, mine), (cot, mine), (tokens, other)):
        for b in range(crops):
            i = len(copies)
            copies.append(pltpu.make_async_copy(source.at[base + b], landing.at[i], sems.at[i]))
            copies[-1].start()
    pack[0] = low(jnp.concatenate([qkv[0], qkv[1], qkv[2], proj[...].T], axis=1))
    pack[1] = low(up[...])
    pack[2] = low(down[...])
    cols = head_bias.shape[1]
    spare = jnp.zeros((1, up_bias.shape[1] - 3 * cols), jnp.float32)
    none = jnp.zeros((1, cols), jnp.float32)
    bias_own[...] = jnp.zeros_like(bias_own)
    bias_own[0:1, :] = jnp.concatenate([head_bias[0:1, :], none, head_bias[1:2, :], spare], axis=1)
    bias_own[1:2, :] = up_bias[...]
    for b in range(crops):
        columns = []
        for base in (mine, other):
            line = jnp.broadcast_to(mask[pl.ds(base + b, 1), :], (8, mask.shape[1]))
            columns.append(line.T[:pad_seq, :1])
        mask_in[b * pad_seq : (b + 1) * pad_seq, :] = jnp.concatenate(columns, axis=1)
    for target in (x_in, cot_in, x_next):
        target[...] = jnp.zeros_like(target)
    for i, copy in enumerate(copies):
        copy.wait()
        begin = i % crops * pad_seq
        (x_in, cot_in, x_next)[i // crops][begin : begin + seq, :] = landing[i]


def run_prepare(dims, *arrays):
    n_dp, n_t, seq, pad_seq, crops, heads = dims
    unit, width = arrays[5].shape
    rows = crops * pad_seq
    inside = pl.BlockSpec(memory_space=pltpu.VMEM)
    outside = pl.BlockSpec(memory_space=pl.ANY)
    activation = jax.ShapeDtypeStruct((rows, width), jnp.bfloat16)
    return pl.pallas_call(
        functools.partial(prepare_kernel, dims),
        out_shape=(
            activation,
            activation,
            activation,
            jax.ShapeDtypeStruct((rows, 2), jnp.float32),
            jax.ShapeDtypeStruct((PIECES, unit, width), jnp.bfloat16),
            jax.ShapeDtypeStruct((8, width), jnp.float32),
        ),
        in_specs=[outside, outside] + [inside] * (len(arrays) - 2),
        out_specs=(inside,) * 6,
        scratch_shapes=[
            pltpu.VMEM((3 * crops, seq, width), jnp.bfloat16),
            pltpu.SemaphoreType.DMA((3 * crops,)),
        ],
        compiler_params=pltpu.CompilerParams(vmem_limit_bytes=32 * 1024 * 1024),
        name="prepare",
    )(*arrays)


def adam_kernel(*refs):
    shard, sums, own_sums, square_tile = refs[:4]
    states = [refs[4 + 3 * i : 7 + 3 * i] for i in range(7)]
    norm_out = refs[25]
    results = [refs[26 + 3 * i : 29 + 3 * i] for i in range(7)]
    copies = refs[47:51]
    norm = jnp.sqrt(square_tile[0:1, 0:1])
    norm_out[...] = jnp.broadcast_to(norm, norm_out.shape)
    factor = jnp.minimum(1.0, clip_norm / (norm + 1e-06))
    cols = states[0][0].shape[2]

    def update(i, grad, rate, decay, at=None):
        old = [ref[...] if at is None else ref[at] for ref in states[i]]
        fresh = adam_step(*old, factor * grad, rate, decay)
        for ref, value in zip(results[i], fresh):
            if at is None:
                ref[...] = value
            else:
                ref[at] = value
        if i < 4:
            if at is None:
                copies[i][...] = low(fresh[0])
            else:
                copies[i][at] = low(fresh[0])

    mixed = shard[0]
    for j in range(3):
        update(0, mixed[:, j * cols : (j + 1) * cols], rate_matrix, decay_matrix, j)
    update(1, mixed[:, 3 * cols :].T, rate_matrix, decay_matrix)
    update(2, shard[1], rate_matrix, decay_matrix)
    update(3, shard[2], rate_matrix, decay_matrix)
    update(4, sums[0:9, :], rate_vector, 0.0)
    mix = own_sums[0:1, :]
    heads = jnp.concatenate([mix[:, :cols], mix[:, 2 * cols : 3 * cols]], axis=0)
    update(5, heads, rate_vector, 0.0)
    update(6, own_sums[1:2, :], rate_vector, 0.0)


def run_adam(shard, sums, own_sums, square_tile, *states):
    flat = [array for state in states for array in state]
    like = [jax.ShapeDtypeStruct(array.shape, array.dtype) for array in flat]
    copies = [jax.ShapeDtypeStruct(state[0].shape, jnp.bfloat16) for state in states[:4]]
    inside = pl.BlockSpec(memory_space=pltpu.VMEM)
    out_shape = [jax.ShapeDtypeStruct((8, 128), jnp.float32)] + like + copies
    return pl.pallas_call(
        adam_kernel,
        out_shape=out_shape,
        in_specs=[inside] * (4 + len(flat)),
        out_specs=[inside] * len(out_shape),
        compiler_params=pltpu.CompilerParams(vmem_limit_bytes=48 * 1024 * 1024),
        name="adam_step",
    )(shard, sums, own_sums, square_tile, *flat)


def per_device(
    tokens,
    patch_mask,
    cotangent,
    qkv_weight,
    qkv_first,
    qkv_second,
    proj_weight,
    proj_first,
    proj_second,
    fc1_weight,
    fc1_first,
    fc1_second,
    fc2_weight,
    fc2_first,
    fc2_second,
    vectors,
    vectors_first,
    vectors_second,
    head_bias,
    head_bias_first,
    head_bias_second,
    fc1_bias,
    fc1_bias_first,
    fc1_bias_second,
):
    all_crops, seq, width = tokens.shape
    n_dp = lax.axis_size("dp")
    n_t = lax.axis_size("tensor")
    tensor_at = lax.axis_index("tensor")
    crops = all_crops // n_t
    head_cols = qkv_weight.shape[2]
    heads = head_cols // HD
    pad_seq = -(-seq // 16) * 16
    rows = crops * pad_seq
    stride = n_dp // GROUP

    dims = (n_dp, n_t, seq, pad_seq, crops, heads)
    teams = [[b * stride + i for i in range(stride)] for b in range(GROUP)]
    if stride == 1:
        lanes = -(-pad_seq // 128) * 128
        margins = [(0, 0), (1 + REG, lanes - patch_mask.shape[1] - 1 - REG)]
        x_in, x_next, cot_in, mask_in, pack, bias_own = run_prepare(
            dims,
            tokens,
            cotangent,
            jnp.pad(patch_mask, margins).astype(jnp.float32),
            qkv_weight,
            proj_weight,
            fc1_weight,
            fc2_weight.T,
            head_bias,
            fc1_bias[None],
        )
    else:
        beside = jnp.where(tensor_at == 0, 1, n_t - 2)

        def padded(array, at=tensor_at):
            here = lax.dynamic_slice_in_dim(array, at * crops, crops, 0)
            spare = [(0, 0), (0, pad_seq - seq), (0, 0)]
            return jnp.pad(here, spare).reshape(rows, -1)

        x_in = padded(tokens)
        x_next = padded(tokens, beside)
        cot_in = padded(cotangent)
        mask_all = jnp.pad(patch_mask, [(0, 0), (1 + REG, 0)]).astype(jnp.float32)
        mask_all = mask_all[:, :, None]
        mask_in = jnp.concatenate([padded(mask_all), padded(mask_all, beside)], axis=1)
        pack = jnp.stack(
            [
                jnp.concatenate(
                    [qkv_weight[0], qkv_weight[1], qkv_weight[2], proj_weight.T], axis=1
                ),
                fc1_weight,
                fc2_weight.T,
            ]
        ).astype(jnp.bfloat16)
        pack = lax.all_gather(pack, "dp", axis_index_groups=teams, axis=1, tiled=True)
        mix_row = jnp.concatenate([head_bias[0], jnp.zeros((head_cols,), jnp.float32), head_bias[1]])
        mix_row = jnp.pad(mix_row, (0, width - 3 * head_cols))
        bias_own = jnp.pad(jnp.stack([mix_row, fc1_bias]), [(0, 6), (0, 0)])
    block_all, grad_all, shard, sums, own_sums, square_tile = run_block(
        dims, pack, x_in, x_next, cot_in, mask_in, vectors, bias_own
    )

    def whole(array):
        return array.reshape(all_crops, pad_seq, width)[:, :seq]

    block_out = whole(block_all)
    tokens_grad = whole(grad_all)
    if stride == 1:
        updated = run_adam(
            shard,
            sums,
            own_sums,
            square_tile,
            (qkv_weight, qkv_first, qkv_second),
            (proj_weight, proj_first, proj_second),
            (fc1_weight, fc1_first, fc1_second),
            (fc2_weight.T, fc2_first.T, fc2_second.T),
            (vectors, vectors_first, vectors_second),
            (head_bias, head_bias_first, head_bias_second),
            (fc1_bias[None], fc1_bias_first[None], fc1_bias_second[None]),
        )
        norm_tile = updated[0]
        updated = list(updated[1:])
        for at in (18, 19, 20):
            updated[at] = updated[at][0]
        for at in (9, 10, 11, 24):
            updated[at] = updated[at].T
        return (block_out, tokens_grad, norm_tile[0, 0], *updated)
    both = ("dp", "tensor")
    shard = lax.psum_scatter(
        shard, "dp", scatter_dimension=1, axis_index_groups=teams, tiled=True
    )
    qkv_shard = jnp.stack([shard[0, :, i * head_cols : (i + 1) * head_cols] for i in range(3)])
    proj_shard = shard[0, :, 3 * head_cols :].T
    up_shard = shard[1]
    down_shard = shard[2].T
    sums, own_sums = lax.psum((sums, own_sums), "dp", axis_index_groups=teams)
    vector_sum = sums[:9]
    mix_here = own_sums[0]
    head_sum = jnp.stack([mix_here[:head_cols], mix_here[2 * head_cols : 3 * head_cols]])
    fc1b_sum = own_sums[1]
    first_data = (lax.axis_index("dp") == 0).astype(jnp.float32)
    first_tensor = (lax.axis_index("tensor") == 0).astype(jnp.float32)
    local_squares = (
        square_sum(qkv_shard)
        + square_sum(proj_shard)
        + square_sum(up_shard)
        + square_sum(down_shard)
    )
    local_squares = local_squares + first_data * (square_sum(head_sum) + square_sum(fc1b_sum))
    local_squares = local_squares + first_data * first_tensor * square_sum(vector_sum)
    total_squares = lax.psum(local_squares, ("dp", "tensor"))
    grad_norm = jnp.sqrt(total_squares)
    factor = jnp.minimum(1.0, clip_norm / (grad_norm + 1e-06))
    qkv_set = adam_step(
        qkv_weight, qkv_first, qkv_second, factor * qkv_shard, rate_matrix, decay_matrix
    )
    proj_set = adam_step(
        proj_weight, proj_first, proj_second, factor * proj_shard, rate_matrix, decay_matrix
    )
    fc1_set = adam_step(
        fc1_weight, fc1_first, fc1_second, factor * up_shard, rate_matrix, decay_matrix
    )
    fc2_set = adam_step(
        fc2_weight, fc2_first, fc2_second, factor * down_shard, rate_matrix, decay_matrix
    )
    vectors_set = adam_step(
        vectors, vectors_first, vectors_second, factor * vector_sum, rate_vector, 0.0
    )
    head_set = adam_step(
        head_bias, head_bias_first, head_bias_second, factor * head_sum, rate_vector, 0.0
    )
    fc1b_set = adam_step(
        fc1_bias, fc1_bias_first, fc1_bias_second, factor * fc1b_sum, rate_vector, 0.0
    )
    return (
        block_out,
        tokens_grad,
        grad_norm,
        qkv_set[0],
        qkv_set[1],
        qkv_set[2],
        proj_set[0],
        proj_set[1],
        proj_set[2],
        fc1_set[0],
        fc1_set[1],
        fc1_set[2],
        fc2_set[0],
        fc2_set[1],
        fc2_set[2],
        vectors_set[0],
        vectors_set[1],
        vectors_set[2],
        head_set[0],
        head_set[1],
        head_set[2],
        fc1b_set[0],
        fc1b_set[1],
        fc1b_set[2],
        qkv_set[0].astype(jnp.bfloat16),
        proj_set[0].astype(jnp.bfloat16),
        fc1_set[0].astype(jnp.bfloat16),
        fc2_set[0].astype(jnp.bfloat16),
    )


def solution(mesh):
    placed = (
        P("dp", None, None),
        P("dp", None),
        P("dp", None, None),
        P(None, "dp", "tensor"),
        P(None, "dp", "tensor"),
        P(None, "dp", "tensor"),
        P("tensor", "dp"),
        P("tensor", "dp"),
        P("tensor", "dp"),
        P("dp", "tensor"),
        P("dp", "tensor"),
        P("dp", "tensor"),
        P("tensor", "dp"),
        P("tensor", "dp"),
        P("tensor", "dp"),
        P(),
        P(),
        P(),
        P(None, "tensor"),
        P(None, "tensor"),
        P(None, "tensor"),
        P("tensor"),
        P("tensor"),
        P("tensor"),
    )
    return jax.shard_map(
        per_device,
        mesh=mesh,
        in_specs=placed,
        out_specs=(
            P("dp", None, None),
            P("dp", None, None),
            P(),
            P(None, "dp", "tensor"),
            P(None, "dp", "tensor"),
            P(None, "dp", "tensor"),
            P("tensor", "dp"),
            P("tensor", "dp"),
            P("tensor", "dp"),
            P("dp", "tensor"),
            P("dp", "tensor"),
            P("dp", "tensor"),
            P("tensor", "dp"),
            P("tensor", "dp"),
            P("tensor", "dp"),
            P(),
            P(),
            P(),
            P(None, "tensor"),
            P(None, "tensor"),
            P(None, "tensor"),
            P("tensor"),
            P("tensor"),
            P("tensor"),
            P(None, "dp", "tensor"),
            P("tensor", "dp"),
            P("dp", "tensor"),
            P("tensor", "dp"),
        ),
        check_vma=False,
    )
```

```python
import functools

import jax
import jax.numpy as jnp
from jax import lax
from jax.experimental import pallas as pl
from jax.experimental.pallas import tpu as pltpu
from jax.sharding import PartitionSpec as P

HD = 64
REG = 4
STEP = 10
GROUP = 8
LAG = 2
RING = 4

PIECES = 3
CHUNK = 32

norm_eps = 1e-06
clip_norm = 1.0
rate_matrix = 0.04
rate_vector = 0.2
decay_matrix = 0.04
moment_decay = 0.5
adam_eps = 1e-08

def square_sum(values):
    return jnp.sum(values * values)


def adam_step(weight, first, second, grad, rate, decay):
    first_new = moment_decay * first + (1.0 - moment_decay) * grad
    second_new = moment_decay * second + (1.0 - moment_decay) * grad * grad
    correct = 1.0 - moment_decay**STEP
    weight_new = weight - rate * (
        first_new / correct / (jnp.sqrt(second_new / correct) + adam_eps) + decay * weight
    )
    return (weight_new, first_new, second_new)


def nn(a, b):
    return lax.dot_general(a, b, (((1,), (0,)), ((), ())), preferred_element_type=jnp.float32)


def nt(a, b):
    return lax.dot_general(a, b, (((1,), (1,)), ((), ())), preferred_element_type=jnp.float32)


def tn(a, b):
    return lax.dot_general(a, b, (((0,), (0,)), ((), ())), preferred_element_type=jnp.float32)


def low(values):
    return values.astype(jnp.bfloat16)


def wide(values):
    return values.astype(jnp.float32)


def fold(values):
    return jnp.sum(values.reshape(-1, 8, values.shape[-1]), axis=0)


def remote(src, dst, send, recv, device):
    return pltpu.make_async_remote_copy(
        src_ref=src,
        dst_ref=dst,
        send_sem=send,
        recv_sem=recv,
        device_id=device,
        device_id_type=pl.DeviceIdType.MESH,
    )


def block_kernel(
    dims,
    pack,
    x_in,
    x_next,
    cot_in,
    mask_in,
    vec,
    bias_own,
    out_block,
    out_tokens,
    shard_out,
    sums_out,
    own_out,
    square_out,
    store,
    norm_one,
    turned_one,
    mixed,
    probs,
    context,
    attn_sum,
    middle,
    norm_two,
    mlp_grad,
    turned_mlp,
    wide_one,
    wide_two,
    result,
    core_ring,
    diag_ring,
    dir_ring,
    line_in,
    bias_all,
    sums,
    sums_in,
    sums_z,
    tiles,
    tiles_in,
    tiles_z,
    z_send,
    z_recv,
    xy_send,
    xy_recv,
    diag_send,
    diag_recv,
    core_send,
    core_recv,
    rc_send,
    rc_recv,
    rd_send,
    rd_recv,
    rx_send,
    rx_recv,
    rz_send,
    rz_recv,
    ob_send,
    ob_recv,
    og_send,
    og_recv,
    own_sem,
    bs_send,
    bs_recv,
    vs_send,
    vs_recv,
    sq_send,
    sq_recv,
):
    n_dp, n_t, seq, pad_seq, crops, heads = dims
    stride = n_dp // GROUP
    rows = crops * pad_seq
    unit = pack.shape[1]
    half = unit // 2
    width = pack.shape[2]
    head_cols = heads * HD
    mix_cols = 3 * head_cols
    scale = HD ** (-0.5)
    n_chunks = rows // CHUNK

    d = lax.axis_index("dp")
    z = lax.axis_index("tensor")
    place = d // stride
    c = place % 2
    yx = place // 2
    xbit = yx % 2
    ybit = yx // 2
    yx_x = yx + 1 - 2 * xbit
    yx_y = yx + 2 - 4 * ybit
    yx_d = 3 - yx
    to_core = (d + (1 - 2 * c) * stride, z)
    to_x = (d + (1 - 2 * xbit) * 2 * stride, z)
    to_y = (d + (1 - 2 * ybit) * 4 * stride, z)

    def to_line(k):
        return (d, (z + k) % n_t)

    barrier = pltpu.get_barrier_semaphore()
    def to_place(r):
        other = (
            c + (r % 2) * (1 - 2 * c)
            + 2 * (xbit + (r // 2 % 2) * (1 - 2 * xbit))
            + 4 * (ybit + (r // 4) * (1 - 2 * ybit))
        )
        return (d + (other - place) * stride, z)

    peers = [to_place(r) for r in range(1, GROUP)] + [to_line(k) for k in range(1, n_t)]
    for peer in peers:
        pl.semaphore_signal(
            barrier, inc=1, device_id=peer, device_id_type=pl.DeviceIdType.MESH
        )
    pl.semaphore_wait(barrier, len(peers))

    def sum_copy(step, own, arrived, by_z, send, recv):
        if step < 3:
            return remote(
                own.at[step],
                arrived.at[step],
                send.at[step],
                recv.at[step],
                (to_core, to_x, to_y)[step],
            )
        k = step - 2
        return remote(own.at[3], by_z.at[z], send.at[step], recv.at[step], to_line(k))

    def sum_start(step, refs):
        if step < 3:
            sum_copy(step, *refs).start()
        else:
            own, arrived, by_z, send, recv = refs
            by_z[z] = own[3]
            for k in range(1, n_t):
                sum_copy(2 + k, *refs).start()

    def sum_finish(step, refs):
        own, arrived, by_z, send, recv = refs
        if step < 3:
            sum_copy(step, *refs).wait_recv()
            own[step + 1] = own[step] + arrived[step]
            return None
        for k in range(1, n_t):
            sum_copy(2 + k, *refs).wait_recv()
        total = by_z[0]
        for k in range(1, n_t):
            total = total + by_z[k]
        return total

    def sum_sent(refs):
        for step in range(3 + n_t - 1):
            sum_copy(step, *refs).wait_send()

    grad_sums = (sums, sums_in, sums_z, vs_send, vs_recv)

    def tile_copy(i):
        if i < GROUP - 1:
            dst = tiles_in.at[place]
            return remote(tiles.at[0], dst, sq_send.at[i], sq_recv.at[i], to_place(i + 1))
        k = i - GROUP + 2
        return remote(tiles.at[1], tiles_z.at[z], sq_send.at[i], sq_recv.at[i], to_line(k))

    n_tiles = GROUP - 1 + n_t - 1

    n_jobs = PIECES * n_t

    def z_copy(m, k):
        src = store.at[m, z, yx, c]
        return remote(src, src, z_send.at[m, k - 1], z_recv.at[m, k - 1], to_line(k))

    def job_of(i):
        others = jnp.maximum(i - PIECES, 0)
        m = jnp.where(i < PIECES, i, others // (n_t - 1))
        return m, jnp.where(i < PIECES, 0, others % (n_t - 1) + 1)

    def job_at(m, k):
        return jnp.where(k == 0, m, PIECES + m * (n_t - 1) + k - 1)

    def block_at(i, which):
        m, k = job_of(i)
        return store.at[m, (z + n_t - k) % n_t, which, c]

    def direct(i, axis):
        src = block_at(i, yx)
        return remote(
            src, src, xy_send.at[i, axis], xy_recv.at[i, axis], to_x if axis == 0 else to_y
        )

    def diagonal(i, axis):
        which = yx_x if axis == 1 else yx_y
        src = block_at(i, which).at[pl.ds(0 if axis == 1 else half, half)]
        return remote(
            src, src, diag_send.at[i, axis], diag_recv.at[i, axis], to_x if axis == 0 else to_y
        )

    def across(i, slot):
        src = block_at(i, (yx, yx_x, yx_y, yx_d)[slot])
        return remote(src, src, core_send.at[i, slot], core_recv.at[i, slot], to_core)

    def start_line(m):
        for k in range(1, n_t):
            z_copy(m, k).start()

    def first_stage(i):
        m, k = job_of(i)

        @pl.when(k > 0)
        def _():
            z_copy(m, jnp.maximum(k, 1)).wait_recv()

        direct(i, 0).start()
        direct(i, 1).start()
        across(i, 0).start()

    def second_stage(i):
        direct(i, 0).wait_recv()
        diagonal(i, 1).start()
        direct(i, 1).wait_recv()
        diagonal(i, 0).start()
        across(i, 1).start()
        across(i, 2).start()

    def third_stage(i):
        diagonal(i, 0).wait_recv()
        diagonal(i, 1).wait_recv()
        across(i, 3).start()

    def gather_steps(text):
        for stage, i in text:
            {"a": first_stage, "b": second_stage, "c": third_stage, "z": start_line}[stage](i)

    def at_step(value, table):
        for key, text in table.items():

            @pl.when(value == key)
            def _():
                gather_steps(text)

    def gather_end(m):
        def body(k, carry):
            gather_part(m, k)
            return carry

        lax.fori_loop(0, n_t, body, 0)

    def gather_part(m, k):
        for slot in range(4):
            across(job_at(m, k), slot).wait_recv()

    def gather_sent(m):
        for k in range(1, n_t):
            z_copy(m, k).wait_send()

        def body(k, carry):
            i = job_at(m, k)
            for axis in range(2):
                direct(i, axis).wait_send()
                diagonal(i, axis).wait_send()
            for slot in range(4):
                across(i, slot).wait_send()
            return carry

        lax.fori_loop(0, n_t, body, 0)

    late_jobs = 3 * n_t + 2
    n_slots = late_jobs + 2 * n_t

    def late_group(i):
        return jnp.where(i % 2 == 0, i // 2, n_t - 1 - i // 2)

    def job_slot(j):
        early = j < 2 * n_t
        return (
            jnp.where(early, 3 + j % 2, 5),
            jnp.where(early, j // 2, late_group(jnp.maximum(j - late_jobs, 0) // 2)),
        )

    def ring_slot(j):
        return jnp.where(j < 2 * n_t, j % RING, jnp.maximum(j - late_jobs, 0) // 2 % 2)

    def job_valid(j):
        late = jnp.logical_and(j >= late_jobs, (j - late_jobs) % 2 == 0)
        busy = jnp.logical_or(j < 2 * n_t, late)
        return jnp.logical_and(busy, jnp.logical_and(j >= 0, j < n_slots))

    def rs_core(j):
        slot, t = job_slot(j)
        return remote(
            store.at[slot, t, :, 1 - c],
            core_ring.at[ring_slot(j)],
            rc_send.at[j],
            rc_recv.at[j],
            to_core,
        )

    def rs_diag(j, axis):
        slot, t = job_slot(j)
        return remote(
            store.at[slot, t, yx_d, c, pl.ds(axis * half, half)],
            diag_ring.at[ring_slot(j), axis],
            rd_send.at[j, axis],
            rd_recv.at[j, axis],
            to_x if axis == 0 else to_y,
        )

    def rs_direct(j, axis):
        slot, t = job_slot(j)
        return remote(
            store.at[slot, t, yx_x if axis == 0 else yx_y, c],
            dir_ring.at[ring_slot(j), axis],
            rx_send.at[j, axis],
            rx_recv.at[j, axis],
            to_x if axis == 0 else to_y,
        )

    def rs_line(slot, t, up):
        to = z + 1 if up else z - 1
        at = t if up else jnp.where(t == to, n_t, t)
        return remote(
            store.at[slot, t, yx, c],
            line_in.at[5 - slot, at],
            rz_send.at[5 - slot, t],
            rz_recv.at[5 - slot, at],
            to_line(1 if up else n_t - 1),
        )

    def rs_line_in(m, at):
        here = line_in.at[m, at]
        return remote(here, here, rz_send.at[m, 0], rz_recv.at[m, at], to_line(1))

    def reduce_stage(stage, j):
        slot, t = job_slot(j)
        if stage == 0:
            rs_core(j).start()
        if stage == 1:
            rs_core(j).wait_recv()
            per = unit // CHUNK

            def body(s, carry):
                at = pl.ds(pl.multiple_of((s % per) * CHUNK, CHUNK), CHUNK)
                which = s // per
                store[slot, t, which, c, at] = low(
                    wide(store[slot, t, which, c, at]) + wide(core_ring[ring_slot(j), which, at])
                )
                return carry

            lax.fori_loop(0, 4 * per, body, 0)
            rs_diag(j, 0).start()
            rs_diag(j, 1).start()
        if stage == 2:
            for axis in range(2):
                rs_diag(j, axis).wait_recv()
                which = yx_y if axis == 0 else yx_x
                at = pl.ds(axis * half, half)
                store[slot, t, which, c, at] = low(
                    wide(store[slot, t, which, c, at]) + wide(diag_ring[ring_slot(j), axis])
                )
            rs_direct(j, 0).start()
            rs_direct(j, 1).start()
        if stage == 3:
            rs_direct(j, 0).wait_recv()
            rs_direct(j, 1).wait_recv()
            total = (
                wide(store[slot, t, yx, c])
                + wide(dir_ring[ring_slot(j), 0])
                + wide(dir_ring[ring_slot(j), 1])
            )

            @pl.when(t == z)
            def _():
                shard_out[5 - slot] = total

            @pl.when(t != z)
            def _():
                store[slot, t, yx, c] = low(total)

        if stage >= 3:
            hop = stage - 3
            for up in (True, False):
                here = z == (hop if up else n_t - 1 - hop)

                @pl.when(jnp.logical_and(here, t > z if up else t < z))
                def _():
                    if hop > 0:
                        rs_line_in(5 - slot, t).wait_recv()
                        store[slot, t, yx, c] = low(
                            wide(store[slot, t, yx, c]) + wide(line_in[5 - slot, t])
                        )
                    rs_line(slot, t, up).start()

    def reduce_tick(i):
        for stage in range(n_t + 1, -1, -1):

            @pl.when(job_valid(i - stage * LAG))
            def _():
                reduce_stage(stage, jnp.clip(i - stage * LAG, 0, n_slots - 1))

    def line_copy(q, up, out, send, recv, first_src):
        s, b = q // crops + 1, q % crops
        shard = jnp.maximum(z - s + 1, 0) if up else jnp.minimum(z + s - 1, n_t - 1)
        at = pl.ds(b * pad_seq, pad_seq)
        src = first_src.at[at] if s == 1 else out.at[shard, at]
        way = 0 if up else 1
        return remote(
            src,
            out.at[shard, at],
            send.at[way, q],
            recv.at[way, q],
            to_line(1 if up else n_t - 1),
        )

    def line_go(q, action, refs):
        s = q // crops + 1
        skip = refs is line_block and s == 1
        sends = action != "wait_recv"
        for up in (True, False):
            if up:
                ok = jnp.logical_and(z - s + 1 >= 0, z < n_t - 1) if sends else z - s >= 0
                if skip:
                    ok = jnp.logical_and(ok, z != (n_t - 2 if sends else n_t - 1))
            else:
                ok = jnp.logical_and(z + s - 1 <= n_t - 1, z > 0) if sends else z + s <= n_t - 1
                if skip:
                    ok = jnp.logical_and(ok, z != (1 if sends else 0))

            @pl.when(ok)
            def _():
                copy = line_copy(q, up, *refs)
                if action == "start":
                    copy.start()
                elif action == "wait_send":
                    copy.wait_send()
                else:
                    copy.wait_recv()

    n_hops = crops * (n_t - 1)

    def line_begin(refs):
        for q in range(crops):
            line_go(q, "start", refs)

    def line_forward(q, refs):
        line_go(q, "wait_recv", refs)
        if q + crops < n_hops:
            line_go(q + crops, "start", refs)

    def line_end(refs, begin=0):
        for q in range(begin, n_hops):
            line_go(q, "wait_send", refs)

    line_block = (out_block, ob_send, ob_recv, result.at[0])
    line_tokens = (out_tokens, og_send, og_recv, result.at[1])

    for m in range(PIECES):
        store[m, z, yx, c] = pack[m]
    bias_all[z] = bias_own[...]

    def bias_copy(k):
        return remote(
            bias_own, bias_all.at[z], bs_send.at[k - 1], bs_recv.at[k - 1], to_line(k)
        )

    for k in range(1, n_t):
        bias_copy(k).start()
    gather_steps((("z", 0), ("a", 0), ("a", 1), ("a", 2),))
    sums[0] = jnp.zeros(sums.shape[1:], jnp.float32)

    def matrix(slot, t):
        return store[slot, t].reshape(GROUP * unit, width)

    def active_of(t):
        return store[4, t].reshape(GROUP * unit, width)[:rows]

    def slope_of(t):
        return store[5, t].reshape(GROUP * unit, width)[:rows]

    per_unit = unit // CHUNK

    def spot(i):
        block = i // per_unit
        at = pl.ds(pl.multiple_of((i % per_unit) * CHUNK, CHUNK), CHUNK)
        return block // 2, block % 2, at

    def chunk_at(i):
        return pl.ds(pl.multiple_of(i * CHUNK, CHUNK), CHUNK)

    def start_of(at, extra=False):
        chosen = mask_in[at, 1:2] > 0.5 if extra else mask_in[at, 0:1] > 0.5
        source = mlp_grad if extra else x_in
        return jnp.where(chosen, vec[8:9, :], wide(source[at, :])), chosen

    def normal(values):
        mean = jnp.mean(values, axis=-1, keepdims=True)
        centred = values - mean
        spread = jnp.mean(centred * centred, axis=-1, keepdims=True)
        rate = lax.rsqrt(spread + norm_eps)
        return centred * rate, rate

    def first_norm(i, carry, extra=False):
        at = chunk_at(i)
        begin, _ = start_of(at, extra)
        hat, _ = normal(begin)
        norm_one[at, :] = low(hat * vec[0:1, :] + vec[1:2, :])
        return carry

    zero8 = jnp.zeros((8, width), jnp.float32)
    attn_sum[...] = jnp.zeros_like(attn_sum)

    def early(i, carry):
        lax.fori_loop(i * n_chunks // 3, (i + 1) * n_chunks // 3, first_norm, 0)
        at_step(i, {0: (("b", 0),), 1: (("z", 1), ("b", 1),), 2: (("b", 2), ("c", 0), ("c", 1), ("c", 2),)})
        return carry

    lax.fori_loop(0, 3, early, 0)
    gather_steps((("a", 3), ("a", 4), ("a", 5), ("z", 2),))
    for k in range(1, n_t):
        bias_copy(k).wait_recv()

    key_ok = lax.broadcasted_iota(jnp.int32, (1, pad_seq), 1) < seq

    def attend(t, extra=False):
        mixed[t] = low(nn(norm_one[...], matrix(0, t)[:, :mix_cols]) + bias_all[t, 0:1, :mix_cols])

        def crop_body(b, inner):
            at = pl.ds(pl.multiple_of(b * pad_seq, 16), pad_seq)
            mine = mixed[t, at, :]
            parts = []
            for h in range(heads):
                q = mine[:, h * HD : (h + 1) * HD]
                k = mine[:, head_cols + h * HD : head_cols + (h + 1) * HD]
                v = mine[:, 2 * head_cols + h * HD : 2 * head_cols + (h + 1) * HD]
                s = jnp.where(key_ok, nt(q, k) * scale, -1e30)
                e = jnp.exp(s - jnp.max(s, axis=-1, keepdims=True))
                p = low(e / jnp.sum(e, axis=-1, keepdims=True))
                if not extra:
                    probs[t, b, h] = p
                parts.append(low(nn(p, v)))
            context[t, at, :] = jnp.concatenate(parts, axis=1)
            return inner

        lax.fori_loop(0, crops, crop_body, 0)
        attn_sum[...] += nt(context[t], matrix(0, t)[:, mix_cols:])

    def attend_step(k, carry):
        at_step(k, {1: (("b", 3), ("b", 4), ("c", 3), ("b", 5),), 2: (("c", 4), ("a", 6), ("a", 7), ("a", 8),), 3: (("c", 5), ("b", 6), ("b", 7),)})
        gather_part(0, k)
        attend((z + n_t - k) % n_t)
        return carry

    lax.fori_loop(0, n_t, attend_step, 0)

    def second_norm(i, carry, extra=False):
        at = chunk_at(i)
        begin, _ = start_of(at, extra)
        mid = begin + vec[2:3, :] * (attn_sum[at, :] + vec[3:4, :])
        middle[at, :] = mid
        hat, _ = normal(mid)
        norm_two[at, :] = low(hat * vec[4:5, :] + vec[5:6, :])
        return carry

    gather_steps((("b", 8), ("c", 6), ("a", 9), ("a", 10), ("a", 11),))
    lax.fori_loop(0, n_chunks, second_norm, 0)
    gather_steps((("c", 7), ("c", 8), ("b", 9),))
    gather_end(1)

    def hidden_units(t, carry):
        wide_one[...] = nn(norm_two[...], matrix(1, t)) + bias_all[t, 1:2, :]

        def bend(i, inner):
            at = chunk_at(i)
            h = wide_one[at, :]
            cdf = 0.5 + 0.5 * lax.erf(h * 0.7071067811865476)
            a, b, within = spot(i)
            store[4, t, a, b, within] = low(h * cdf)
            store[5, t, a, b, within] = low(cdf + h * jnp.exp(-0.5 * h * h) * 0.3989422804014327)
            return inner

        lax.fori_loop(0, n_chunks, bend, 0)
        at_step(t, {0: (("b", 10), ("b", 11), ("c", 9),), 1: (("c", 10),), 2: (("c", 11),)})
        return carry

    lax.fori_loop(0, n_t, hidden_units, 0)

    wide_one[...] = jnp.zeros_like(wide_one)

    def mlp_out(k, carry):
        gather_part(2, k)
        t = (z + n_t - k) % n_t
        wide_one[...] += nt(active_of(t), matrix(2, t))
        return carry

    lax.fori_loop(0, n_t, mlp_out, 0)

    def finish_block(i, total):
        at = chunk_at(i)
        mlp = wide_one[at, :] + vec[7:8, :]
        result[0, at, :] = low(middle[at, :] + vec[6:7, :] * mlp)
        return total + fold(wide(cot_in[at, :]) * mlp)

    mlp_total = lax.fori_loop(0, n_chunks, finish_block, zero8)
    sums[0, 6:7, :] = jnp.sum(mlp_total, axis=0, keepdims=True)
    line_begin(line_block)
    own_block = pltpu.make_async_copy(result.at[0], out_block.at[z], own_sem.at[0])
    own_block.start()

    turned_one[...] = norm_two[...].T

    def scale_cot(i, total):
        at = chunk_at(i)
        cot = wide(cot_in[at, :])
        mlp_grad[at, :] = low(vec[6:7, :] * cot)
        return total + fold(cot)

    cot_total = lax.fori_loop(0, n_chunks, scale_cot, zero8)
    sums[0, 7:8, :] = vec[6:7, :] * jnp.sum(cot_total, axis=0, keepdims=True)
    turned_mlp[...] = mlp_grad[...].T
    wide_one[...] = jnp.zeros_like(wide_one)
    ones = jnp.ones((CHUNK, rows), jnp.bfloat16)

    def hidden_back(t, carry):
        store[3, t] = low(nn(turned_mlp[...], active_of(t))).reshape(4, 2, unit, width)
        reduce_tick(2 * t)
        wide_two[...] = nn(mlp_grad[...], matrix(2, t))

        def bend(i, inner):
            at = chunk_at(i)
            a, b, within = spot(i)
            store[5, t, a, b, within] = low(wide(store[5, t, a, b, within]) * wide_two[at, :])
            return inner

        lax.fori_loop(0, n_chunks, bend, 0)
        bent = slope_of(t)
        sums[0, pl.ds(9 + n_t + t, 1), :] = nn(ones, bent)[:1]
        store[4, t] = low(nn(turned_one[...], bent)).reshape(4, 2, unit, width)
        wide_one[...] += nt(bent, matrix(1, t))
        reduce_tick(2 * t + 1)

        for q in range(crops):

            @pl.when(t == 2 * q)
            def _():
                line_forward(q, line_block)

        return carry

    lax.fori_loop(0, n_t, hidden_back, 0)
    reduce_tick(2 * n_t)
    next_copy = pltpu.make_async_copy(x_next, mlp_grad, own_sem.at[2])
    next_copy.start()
    turned_one[...] = norm_one[...].T

    def second_back(i, totals):
        gain, shift, scale_one, bias_proj = totals
        at = chunk_at(i)
        upstream = wide_one[at, :]
        hat, rate = normal(middle[at, :])
        e = vec[4:5, :] * upstream
        inner = e - jnp.mean(e, axis=-1, keepdims=True)
        inner = inner - hat * jnp.mean(e * hat, axis=-1, keepdims=True)
        g = wide(cot_in[at, :]) + rate * inner
        wide_two[at, :] = g
        norm_two[at, :] = low(vec[2:3, :] * g)
        return (
            gain + fold(upstream * hat),
            shift + fold(upstream),
            scale_one + fold(g * (attn_sum[at, :] + vec[3:4, :])),
            bias_proj + fold(g),
        )

    gain, shift, scale_one, bias_proj = lax.fori_loop(0, n_chunks, second_back, (zero8,) * 4)
    sums[0, 4:5, :] = jnp.sum(gain, axis=0, keepdims=True)
    sums[0, 5:6, :] = jnp.sum(shift, axis=0, keepdims=True)
    sums[0, 2:3, :] = jnp.sum(scale_one, axis=0, keepdims=True)
    sums[0, 3:4, :] = vec[2:3, :] * jnp.sum(bias_proj, axis=0, keepdims=True)
    reduce_tick(2 * n_t + 1)
    turned_mlp[...] = norm_two[...].T
    line_forward(2, line_block)
    wide_one[...] = jnp.zeros_like(wide_one)

    def attend_back(i, carry):
        b, turn = i // n_t, i % n_t
        t = late_group(turn)
        at = pl.ds(pl.multiple_of(b * pad_seq, 16), pad_seq)
        theirs = low(nn(norm_two[at, :], matrix(0, t)[:, mix_cols:]))
        mine = mixed[t, at, :]
        gq, gk, gv = [], [], []
        for h in range(heads):
            q = mine[:, h * HD : (h + 1) * HD]
            k = mine[:, head_cols + h * HD : head_cols + (h + 1) * HD]
            v = mine[:, 2 * head_cols + h * HD : 2 * head_cols + (h + 1) * HD]
            g = theirs[:, h * HD : (h + 1) * HD]
            p_low = probs[t, b, h]
            p = wide(p_low)
            gp = nt(g, v)
            gs = low(p * (gp - jnp.sum(gp * p, axis=-1, keepdims=True)))
            gq.append(low(nn(gs, k) * scale))
            gk.append(low(tn(gs, q) * scale))
            gv.append(low(tn(p_low, g)))
        fresh = jnp.concatenate(gq + gk + gv, axis=1)
        mixed[t, at, :] = fresh
        wide_one[at, :] += nt(fresh, matrix(0, t)[:, :mix_cols])

        @pl.when(b == 0)
        def _():
            reduce_tick(2 * n_t + 2 + turn)

        @pl.when(b == 1)
        def _():
            sums[0, pl.ds(9 + t, 1), :mix_cols] = nn(ones, mixed[t])[:1]
            grads = jnp.concatenate(
                [
                    low(nn(turned_one[...], mixed[t])),
                    low(nn(turned_mlp[...], context[t])),
                ],
                axis=1,
            )
            store[5, t] = grads.reshape(4, 2, unit, width)
            reduce_tick(late_jobs + 2 * turn)
            reduce_tick(late_jobs + 2 * turn + 1)

        for key, (q, refs) in {
            0: (3, line_block),
            5: (0, line_tokens),
        }.items():

            @pl.when(i == key)
            def _():
                line_forward(q, refs)

        @pl.when(turn == n_t - 1)
        def _():
            start_back(b)

        return carry

    def first_back(at, totals):
        gain, shift, token = totals
        upstream = wide_one[at, :]
        begin, chosen = start_of(at)
        hat, rate = normal(begin)
        e = vec[0:1, :] * upstream
        inner = e - jnp.mean(e, axis=-1, keepdims=True)
        inner = inner - hat * jnp.mean(e * hat, axis=-1, keepdims=True)
        g = wide_two[at, :] + rate * inner
        result[1, at, :] = low(jnp.where(chosen, 0.0, g))
        return (
            gain + fold(upstream * hat),
            shift + fold(upstream),
            token + fold(jnp.where(chosen, g, 0.0)),
        )

    def start_back(b):
        base = b * pad_seq
        full = pad_seq // CHUNK

        def body(i, totals):
            at = pl.ds(pl.multiple_of(base + i * CHUNK, 16), CHUNK)
            return first_back(at, totals)

        totals = lax.fori_loop(0, full, body, (zero8,) * 3)
        if pad_seq % CHUNK:
            at = pl.ds(pl.multiple_of(base + full * CHUNK, 16), pad_seq % CHUNK)
            totals = first_back(at, totals)
        for row, total in zip((0, 1, 8), totals):
            sums[0, row : row + 1, :] += jnp.sum(total, axis=0, keepdims=True)
        for q in range(crops):

            @pl.when(b == q)
            def _():
                line_go(q, "start", line_tokens)

    lax.fori_loop(0, crops * n_t, attend_back, 0)
    own_tokens = pltpu.make_async_copy(result.at[1], out_tokens.at[z], own_sem.at[1])
    own_tokens.start()

    sum_start(0, grad_sums)
    next_copy.wait()
    at_end = jnp.logical_or(z == 0, z == n_t - 1)
    beside = jnp.where(z == 0, 1, n_t - 2)

    @pl.when(at_end)
    def _():
        lax.fori_loop(0, n_chunks, functools.partial(first_norm, extra=True), 0)
        attn_sum[...] = jnp.zeros_like(attn_sum)

    reduce_tick(n_slots)
    line_forward(2, line_tokens)
    sum_finish(0, grad_sums)
    sum_start(1, grad_sums)

    def attend_more(t, carry):
        @pl.when(at_end)
        def _():
            attend((beside + n_t - t) % n_t, extra=True)

        reduce_tick(n_slots + 1 + t)

        @pl.when(t == 1)
        def _():
            sum_finish(1, grad_sums)
            sum_start(2, grad_sums)

        @pl.when(t == 2)
        def _():
            line_forward(1, line_tokens)

        @pl.when(t == 3)
        def _():
            sum_finish(2, grad_sums)
            sum_start(3, grad_sums)

        return carry

    lax.fori_loop(0, n_t, attend_more, 0)
    reduce_tick(n_slots + n_t + 1)

    @pl.when(at_end)
    def _():
        lax.fori_loop(0, n_chunks, functools.partial(second_norm, extra=True), 0)
        wide_two[...] = jnp.zeros_like(wide_two)

    reduce_tick(n_slots + n_t + 2)

    def hidden_more(k, carry):
        t = (beside + n_t - k) % n_t

        @pl.when(at_end)
        def _():
            wide_one[...] = nn(norm_two[...], matrix(1, t)) + bias_all[t, 1:2, :]

            def bend(i, inner):
                at = chunk_at(i)
                h = wide_one[at, :]
                mlp_grad[at, :] = low(h * (0.5 + 0.5 * lax.erf(h * 0.7071067811865476)))
                return inner

            lax.fori_loop(0, n_chunks, bend, 0)
            wide_two[...] += nt(mlp_grad[...], matrix(2, t))

        reduce_tick(n_slots + n_t + 3 + k)

        @pl.when(k == 0)
        def _():
            line_forward(3, line_tokens)

        return carry

    lax.fori_loop(0, n_t, hidden_more, 0)
    for step in range(2 * n_t + 3, LAG * (n_t + 1)):
        reduce_tick(n_slots + step)
    for q in range(4, n_hops):
        line_forward(q, line_block)
    for q in range(crops):
        line_go(q, "wait_send", line_block)
    own_block.wait()
    more_block = pltpu.make_async_copy(result.at[0], out_block.at[beside], own_sem.at[0])

    @pl.when(at_end)
    def _():
        def finish_more(i, carry):
            at = chunk_at(i)
            mlp = wide_two[at, :] + vec[7:8, :]
            result[0, at, :] = low(middle[at, :] + vec[6:7, :] * mlp)
            return carry

        lax.fori_loop(0, n_chunks, finish_more, 0)
        more_block.start()

    @pl.when(z > 0)
    def _():
        for m in range(PIECES):
            rs_line_in(m, z).wait_recv()
            shard_out[m] = shard_out[m] + wide(line_in[m, z])

    @pl.when(z < n_t - 1)
    def _():
        for m in range(PIECES):
            rs_line_in(m, n_t).wait_recv()
            shard_out[m] = shard_out[m] + wide(line_in[m, n_t])

    sums_out[...] = sum_finish(3, grad_sums)
    own_out[0:1, :] = sums_out[pl.ds(9 + z, 1), :]
    own_out[1:2, :] = sums_out[pl.ds(9 + n_t + z, 1), :]
    if stride == 1:
        first = jnp.where(d == 0, 1.0, 0.0)
        both = jnp.where(z == 0, first, 0.0)
        squares = first * square_sum(own_out[...]) + both * square_sum(sums_out[0:9, :])
        for m in range(PIECES):
            squares = squares + square_sum(shard_out[m])
        tiles[0] = jnp.full(tiles.shape[1:], 1.0, jnp.float32) * squares
        tiles_in[place] = tiles[0]
        for i in range(GROUP - 1):
            tile_copy(i).start()
        for i in range(GROUP - 1):
            tile_copy(i).wait_recv()
        total = tiles_in[0]
        for i in range(1, GROUP):
            total = total + tiles_in[i]
        tiles[1] = total
        tiles_z[z] = total
        for i in range(GROUP - 1, n_tiles):
            tile_copy(i).start()
        for i in range(GROUP - 1, n_tiles):
            tile_copy(i).wait_recv()
        total = tiles_z[0]
        for k in range(1, n_t):
            total = total + tiles_z[k]
        square_out[...] = total
        for i in range(n_tiles):
            tile_copy(i).wait_send()
    else:
        square_out[...] = jnp.zeros_like(square_out)
    for q in range(4, n_hops):
        line_forward(q, line_tokens)
    sum_sent(grad_sums)
    for k in range(1, n_t):
        bias_copy(k).wait_send()

    for m in range(PIECES):
        gather_sent(m)

    def sent(j, carry):
        rs_core(j).wait_send()
        for axis in range(2):
            rs_diag(j, axis).wait_send()
            rs_direct(j, axis).wait_send()

        slot, t = job_slot(j)

        @pl.when(t > z)
        def _():
            rs_line(slot, t, True).wait_send()

        @pl.when(t < z)
        def _():
            rs_line(slot, t, False).wait_send()

        return carry

    lax.fori_loop(0, 2 * n_t, sent, 0)
    lax.fori_loop(0, n_t, lambda t, carry: sent(late_jobs + 2 * t, carry), 0)
    line_end(line_block, crops)
    line_end(line_tokens)

    @pl.when(at_end)
    def _():
        more_block.wait()

    own_tokens.wait()


def run_block(dims, pack, x_in, x_next, cot_in, mask_in, vec, bias_own):
    n_dp, n_t, seq, pad_seq, crops, heads = dims
    unit, width = pack.shape[1:]
    rows = crops * pad_seq
    head_cols = heads * HD
    mix_cols = 3 * head_cols
    n_jobs = PIECES * n_t
    n_sums = -(-(9 + 2 * n_t) // 8) * 8
    bf16, f32 = jnp.bfloat16, jnp.float32
    vmem = pltpu.VMEM
    dma = pltpu.SemaphoreType.DMA
    inside = pl.BlockSpec(memory_space=pltpu.VMEM)
    outside = pl.BlockSpec(memory_space=pl.ANY)
    return pl.pallas_call(
        functools.partial(block_kernel, dims),
        out_shape=(
            jax.ShapeDtypeStruct((n_t, rows, width), bf16),
            jax.ShapeDtypeStruct((n_t, rows, width), bf16),
            jax.ShapeDtypeStruct((PIECES, unit, width), f32),
            jax.ShapeDtypeStruct((n_sums, width), f32),
            jax.ShapeDtypeStruct((2, width), f32),
            jax.ShapeDtypeStruct((8, 128), f32),
        ),
        in_specs=[inside, inside, outside, inside, inside, inside, inside],
        out_specs=(outside, outside, inside, inside, inside, inside),
        scratch_shapes=[
            vmem((6, n_t, 4, 2, unit, width), bf16),
            vmem((rows, width), bf16),
            vmem((width, rows), bf16),
            vmem((n_t, rows, mix_cols), bf16),
            vmem((n_t, crops, heads, pad_seq, pad_seq), bf16),
            vmem((n_t, rows, head_cols), bf16),
            vmem((rows, width), f32),
            vmem((rows, width), f32),
            vmem((rows, width), bf16),
            vmem((rows, width), bf16),
            vmem((width, rows), bf16),
            vmem((rows, width), f32),
            vmem((rows, width), f32),
            vmem((2, rows, width), bf16),
            vmem((RING, 4, unit, width), bf16),
            vmem((RING, 2, unit // 2, width), bf16),
            vmem((RING, 2, unit, width), bf16),
            vmem((PIECES, n_t + 1, unit, width), bf16),
            vmem((n_t, 8, width), f32),
            vmem((4, n_sums, width), f32),
            vmem((3, n_sums, width), f32),
            vmem((n_t, n_sums, width), f32),
            vmem((2, 8, 128), f32),
            vmem((GROUP, 8, 128), f32),
            vmem((n_t, 8, 128), f32),
            dma((PIECES, n_t - 1)),
            dma((PIECES, n_t - 1)),
            dma((n_jobs, 2)),
            dma((n_jobs, 2)),
            dma((n_jobs, 2)),
            dma((n_jobs, 2)),
            dma((n_jobs, 4)),
            dma((n_jobs, 4)),
            dma((5 * n_t + 2,)),
            dma((5 * n_t + 2,)),
            dma((5 * n_t + 2, 2)),
            dma((5 * n_t + 2, 2)),
            dma((5 * n_t + 2, 2)),
            dma((5 * n_t + 2, 2)),
            dma((PIECES, n_t)),
            dma((PIECES, n_t + 1)),
            dma((2, crops * (n_t - 1))),
            dma((2, crops * (n_t - 1))),
            dma((2, crops * (n_t - 1))),
            dma((2, crops * (n_t - 1))),
            dma((3,)),
            dma((n_t - 1,)),
            dma((n_t - 1,)),
            dma((n_t + 2,)),
            dma((n_t + 2,)),
            dma((GROUP + n_t - 2,)),
            dma((GROUP + n_t - 2,)),
        ],
        compiler_params=pltpu.CompilerParams(
            collective_id=0, has_side_effects=True, vmem_limit_bytes=63 * 1024 * 1024
        ),
        name="block_step",
    )(pack, x_in, x_next, cot_in, mask_in, vec, bias_own)


def prepare_kernel(
    dims,
    tokens,
    cot,
    mask,
    qkv,
    proj,
    up,
    down,
    head_bias,
    up_bias,
    x_in,
    x_next,
    cot_in,
    mask_in,
    pack,
    bias_own,
    landing,
    sems,
):
    n_dp, n_t, seq, pad_seq, crops, heads = dims
    z = lax.axis_index("tensor")
    mine = z * crops
    other = jnp.where(z == 0, 1, n_t - 2) * crops
    copies = []
    for source, base in ((tokens, mine), (cot, mine), (tokens, other)):
        for b in range(crops):
            i = len(copies)
            copies.append(pltpu.make_async_copy(source.at[base + b], landing.at[i], sems.at[i]))
            copies[-1].start()
    pack[0] = low(jnp.concatenate([qkv[0], qkv[1], qkv[2], proj[...].T], axis=1))
    pack[1] = low(up[...])
    pack[2] = low(down[...])
    cols = head_bias.shape[1]
    spare = jnp.zeros((1, up_bias.shape[1] - 3 * cols), jnp.float32)
    none = jnp.zeros((1, cols), jnp.float32)
    bias_own[...] = jnp.zeros_like(bias_own)
    bias_own[0:1, :] = jnp.concatenate([head_bias[0:1, :], none, head_bias[1:2, :], spare], axis=1)
    bias_own[1:2, :] = up_bias[...]
    for b in range(crops):
        columns = []
        for base in (mine, other):
            line = jnp.broadcast_to(mask[pl.ds(base + b, 1), :], (8, mask.shape[1]))
            columns.append(line.T[:pad_seq, :1])
        mask_in[b * pad_seq : (b + 1) * pad_seq, :] = jnp.concatenate(columns, axis=1)
    for target in (x_in, cot_in, x_next):
        target[...] = jnp.zeros_like(target)
    for i, copy in enumerate(copies):
        copy.wait()
        begin = i % crops * pad_seq
        (x_in, cot_in, x_next)[i // crops][begin : begin + seq, :] = landing[i]


def run_prepare(dims, *arrays):
    n_dp, n_t, seq, pad_seq, crops, heads = dims
    unit, width = arrays[5].shape
    rows = crops * pad_seq
    inside = pl.BlockSpec(memory_space=pltpu.VMEM)
    outside = pl.BlockSpec(memory_space=pl.ANY)
    activation = jax.ShapeDtypeStruct((rows, width), jnp.bfloat16)
    return pl.pallas_call(
        functools.partial(prepare_kernel, dims),
        out_shape=(
            activation,
            activation,
            activation,
            jax.ShapeDtypeStruct((rows, 2), jnp.float32),
            jax.ShapeDtypeStruct((PIECES, unit, width), jnp.bfloat16),
            jax.ShapeDtypeStruct((8, width), jnp.float32),
        ),
        in_specs=[outside, outside] + [inside] * (len(arrays) - 2),
        out_specs=(inside,) * 6,
        scratch_shapes=[
            pltpu.VMEM((3 * crops, seq, width), jnp.bfloat16),
            pltpu.SemaphoreType.DMA((3 * crops,)),
        ],
        compiler_params=pltpu.CompilerParams(vmem_limit_bytes=32 * 1024 * 1024),
        name="prepare",
    )(*arrays)


def adam_kernel(*refs):
    shard, sums, own_sums, square_tile = refs[:4]
    states = [refs[4 + 3 * i : 7 + 3 * i] for i in range(7)]
    norm_out = refs[25]
    results = [refs[26 + 3 * i : 29 + 3 * i] for i in range(7)]
    copies = refs[47:51]
    norm = jnp.sqrt(square_tile[0:1, 0:1])
    norm_out[...] = jnp.broadcast_to(norm, norm_out.shape)
    factor = jnp.minimum(1.0, clip_norm / (norm + 1e-06))
    cols = states[0][0].shape[2]

    def update(i, grad, rate, decay, at=None):
        old = [ref[...] if at is None else ref[at] for ref in states[i]]
        fresh = adam_step(*old, factor * grad, rate, decay)
        for ref, value in zip(results[i], fresh):
            if at is None:
                ref[...] = value
            else:
                ref[at] = value
        if i < 4:
            if at is None:
                copies[i][...] = low(fresh[0])
            else:
                copies[i][at] = low(fresh[0])

    mixed = shard[0]
    for j in range(3):
        update(0, mixed[:, j * cols : (j + 1) * cols], rate_matrix, decay_matrix, j)
    update(1, mixed[:, 3 * cols :].T, rate_matrix, decay_matrix)
    update(2, shard[1], rate_matrix, decay_matrix)
    update(3, shard[2], rate_matrix, decay_matrix)
    update(4, sums[0:9, :], rate_vector, 0.0)
    mix = own_sums[0:1, :]
    heads = jnp.concatenate([mix[:, :cols], mix[:, 2 * cols : 3 * cols]], axis=0)
    update(5, heads, rate_vector, 0.0)
    update(6, own_sums[1:2, :], rate_vector, 0.0)


def run_adam(shard, sums, own_sums, square_tile, *states):
    flat = [array for state in states for array in state]
    like = [jax.ShapeDtypeStruct(array.shape, array.dtype) for array in flat]
    copies = [jax.ShapeDtypeStruct(state[0].shape, jnp.bfloat16) for state in states[:4]]
    inside = pl.BlockSpec(memory_space=pltpu.VMEM)
    out_shape = [jax.ShapeDtypeStruct((8, 128), jnp.float32)] + like + copies
    return pl.pallas_call(
        adam_kernel,
        out_shape=out_shape,
        in_specs=[inside] * (4 + len(flat)),
        out_specs=[inside] * len(out_shape),
        compiler_params=pltpu.CompilerParams(vmem_limit_bytes=48 * 1024 * 1024),
        name="adam_step",
    )(shard, sums, own_sums, square_tile, *flat)


def per_device(
    tokens,
    patch_mask,
    cotangent,
    qkv_weight,
    qkv_first,
    qkv_second,
    proj_weight,
    proj_first,
    proj_second,
    fc1_weight,
    fc1_first,
    fc1_second,
    fc2_weight,
    fc2_first,
    fc2_second,
    vectors,
    vectors_first,
    vectors_second,
    head_bias,
    head_bias_first,
    head_bias_second,
    fc1_bias,
    fc1_bias_first,
    fc1_bias_second,
):
    all_crops, seq, width = tokens.shape
    n_dp = lax.axis_size("dp")
    n_t = lax.axis_size("tensor")
    tensor_at = lax.axis_index("tensor")
    crops = all_crops // n_t
    head_cols = qkv_weight.shape[2]
    heads = head_cols // HD
    pad_seq = -(-seq // 16) * 16
    rows = crops * pad_seq
    stride = n_dp // GROUP

    dims = (n_dp, n_t, seq, pad_seq, crops, heads)
    teams = [[b * stride + i for i in range(stride)] for b in range(GROUP)]
    if stride == 1:
        lanes = -(-pad_seq // 128) * 128
        margins = [(0, 0), (1 + REG, lanes - patch_mask.shape[1] - 1 - REG)]
        x_in, x_next, cot_in, mask_in, pack, bias_own = run_prepare(
            dims,
            tokens,
            cotangent,
            jnp.pad(patch_mask, margins).astype(jnp.float32),
            qkv_weight,
            proj_weight,
            fc1_weight,
            fc2_weight.T,
            head_bias,
            fc1_bias[None],
        )
    else:
        beside = jnp.where(tensor_at == 0, 1, n_t - 2)

        def padded(array, at=tensor_at):
            here = lax.dynamic_slice_in_dim(array, at * crops, crops, 0)
            spare = [(0, 0), (0, pad_seq - seq), (0, 0)]
            return jnp.pad(here, spare).reshape(rows, -1)

        x_in = padded(tokens)
        x_next = padded(tokens, beside)
        cot_in = padded(cotangent)
        mask_all = jnp.pad(patch_mask, [(0, 0), (1 + REG, 0)]).astype(jnp.float32)
        mask_all = mask_all[:, :, None]
        mask_in = jnp.concatenate([padded(mask_all), padded(mask_all, beside)], axis=1)
        pack = jnp.stack(
            [
                jnp.concatenate(
                    [qkv_weight[0], qkv_weight[1], qkv_weight[2], proj_weight.T], axis=1
                ),
                fc1_weight,
                fc2_weight.T,
            ]
        ).astype(jnp.bfloat16)
        pack = lax.all_gather(pack, "dp", axis_index_groups=teams, axis=1, tiled=True)
        mix_row = jnp.concatenate([head_bias[0], jnp.zeros((head_cols,), jnp.float32), head_bias[1]])
        mix_row = jnp.pad(mix_row, (0, width - 3 * head_cols))
        bias_own = jnp.pad(jnp.stack([mix_row, fc1_bias]), [(0, 6), (0, 0)])
    block_all, grad_all, shard, sums, own_sums, square_tile = run_block(
        dims, pack, x_in, x_next, cot_in, mask_in, vectors, bias_own
    )

    def whole(array):
        return array.reshape(all_crops, pad_seq, width)[:, :seq]

    block_out = whole(block_all)
    tokens_grad = whole(grad_all)
    if stride == 1:
        updated = run_adam(
            shard,
            sums,
            own_sums,
            square_tile,
            (qkv_weight, qkv_first, qkv_second),
            (proj_weight, proj_first, proj_second),
            (fc1_weight, fc1_first, fc1_second),
            (fc2_weight.T, fc2_first.T, fc2_second.T),
            (vectors, vectors_first, vectors_second),
            (head_bias, head_bias_first, head_bias_second),
            (fc1_bias[None], fc1_bias_first[None], fc1_bias_second[None]),
        )
        norm_tile = updated[0]
        updated = list(updated[1:])
        for at in (18, 19, 20):
            updated[at] = updated[at][0]
        for at in (9, 10, 11, 24):
            updated[at] = updated[at].T
        return (block_out, tokens_grad, norm_tile[0, 0], *updated)
    both = ("dp", "tensor")
    shard = lax.psum_scatter(
        shard, "dp", scatter_dimension=1, axis_index_groups=teams, tiled=True
    )
    qkv_shard = jnp.stack([shard[0, :, i * head_cols : (i + 1) * head_cols] for i in range(3)])
    proj_shard = shard[0, :, 3 * head_cols :].T
    up_shard = shard[1]
    down_shard = shard[2].T
    sums, own_sums = lax.psum((sums, own_sums), "dp", axis_index_groups=teams)
    vector_sum = sums[:9]
    mix_here = own_sums[0]
    head_sum = jnp.stack([mix_here[:head_cols], mix_here[2 * head_cols : 3 * head_cols]])
    fc1b_sum = own_sums[1]
    first_data = (lax.axis_index("dp") == 0).astype(jnp.float32)
    first_tensor = (lax.axis_index("tensor") == 0).astype(jnp.float32)
    local_squares = (
        square_sum(qkv_shard)
        + square_sum(proj_shard)
        + square_sum(up_shard)
        + square_sum(down_shard)
    )
    local_squares = local_squares + first_data * (square_sum(head_sum) + square_sum(fc1b_sum))
    local_squares = local_squares + first_data * first_tensor * square_sum(vector_sum)
    total_squares = lax.psum(local_squares, ("dp", "tensor"))
    grad_norm = jnp.sqrt(total_squares)
    factor = jnp.minimum(1.0, clip_norm / (grad_norm + 1e-06))
    qkv_set = adam_step(
        qkv_weight, qkv_first, qkv_second, factor * qkv_shard, rate_matrix, decay_matrix
    )
    proj_set = adam_step(
        proj_weight, proj_first, proj_second, factor * proj_shard, rate_matrix, decay_matrix
    )
    fc1_set = adam_step(
        fc1_weight, fc1_first, fc1_second, factor * up_shard, rate_matrix, decay_matrix
    )
    fc2_set = adam_step(
        fc2_weight, fc2_first, fc2_second, factor * down_shard, rate_matrix, decay_matrix
    )
    vectors_set = adam_step(
        vectors, vectors_first, vectors_second, factor * vector_sum, rate_vector, 0.0
    )
    head_set = adam_step(
        head_bias, head_bias_first, head_bias_second, factor * head_sum, rate_vector, 0.0
    )
    fc1b_set = adam_step(
        fc1_bias, fc1_bias_first, fc1_bias_second, factor * fc1b_sum, rate_vector, 0.0
    )
    return (
        block_out,
        tokens_grad,
        grad_norm,
        qkv_set[0],
        qkv_set[1],
        qkv_set[2],
        proj_set[0],
        proj_set[1],
        proj_set[2],
        fc1_set[0],
        fc1_set[1],
        fc1_set[2],
        fc2_set[0],
        fc2_set[1],
        fc2_set[2],
        vectors_set[0],
        vectors_set[1],
        vectors_set[2],
        head_set[0],
        head_set[1],
        head_set[2],
        fc1b_set[0],
        fc1b_set[1],
        fc1b_set[2],
        qkv_set[0].astype(jnp.bfloat16),
        proj_set[0].astype(jnp.bfloat16),
        fc1_set[0].astype(jnp.bfloat16),
        fc2_set[0].astype(jnp.bfloat16),
    )


def solution(mesh):
    placed = (
        P("dp", None, None),
        P("dp", None),
        P("dp", None, None),
        P(None, "dp", "tensor"),
        P(None, "dp", "tensor"),
        P(None, "dp", "tensor"),
        P("tensor", "dp"),
        P("tensor", "dp"),
        P("tensor", "dp"),
        P("dp", "tensor"),
        P("dp", "tensor"),
        P("dp", "tensor"),
        P("tensor", "dp"),
        P("tensor", "dp"),
        P("tensor", "dp"),
        P(),
        P(),
        P(),
        P(None, "tensor"),
        P(None, "tensor"),
        P(None, "tensor"),
        P("tensor"),
        P("tensor"),
        P("tensor"),
    )
    return jax.shard_map(
        per_device,
        mesh=mesh,
        in_specs=placed,
        out_specs=(
            P("dp", None, None),
            P("dp", None, None),
            P(),
            P(None, "dp", "tensor"),
            P(None, "dp", "tensor"),
            P(None, "dp", "tensor"),
            P("tensor", "dp"),
            P("tensor", "dp"),
            P("tensor", "dp"),
            P("dp", "tensor"),
            P("dp", "tensor"),
            P("dp", "tensor"),
            P("tensor", "dp"),
            P("tensor", "dp"),
            P("tensor", "dp"),
            P(),
            P(),
            P(),
            P(None, "tensor"),
            P(None, "tensor"),
            P(None, "tensor"),
            P("tensor"),
            P("tensor"),
            P("tensor"),
            P(None, "dp", "tensor"),
            P("tensor", "dp"),
            P("dp", "tensor"),
            P("tensor", "dp"),
        ),
        check_vma=False,
    )
```
